32 devices in a mesh: dp: 16 (over z, y, core), mp: 2 (over x).
Axes of the slice: x: 2, y: 2, z: 4, core: 2. Of those that a mesh axis runs over, the one named last changes fastest.
Arguments:
- image_tokens: bfloat16 [256, 64, 1536], P('dp'), may hold values from -6 to 6
- text_tokens: bfloat16 [256, 32, 1536], P('dp'), may hold values from -6 to 6
- image_weight: bfloat16 [1536, 1536], P(None, 'mp'), may hold values from -0.15625 to 0.15625
- text_weight: bfloat16 [1536, 1536], P(None, 'mp'), may hold values from -0.15625 to 0.15625
- logit_scale: float32 [1], replicated, may hold values from 6 to 14
- logit_bias: float32 [1], replicated, may hold values from -8 to -5
- loss_scale: float32 [1], replicated, may hold values from 256 to 4096
- valid_count: int32 [16], P('dp'), may hold values from 3 to 16, as said below
Outputs:
- loss: float32 [], replicated
- image_weight_grad: float32 [1536, 1536], P('dp', 'mp')
- text_weight_grad: float32 [1536, 1536], P('dp', 'mp')
The draws below stay inside these ranges and needn't reach their ends.
Inputs may be any that keep to these rules, and one draw needn't show every extreme that they name: `valid_count`: at least one index of dp has all 16 pairs valid.
All inputs are finite; a program needn't handle non-finite values.
Results may differ from the reference program's by a relative error of at most 0.0014.
Values may be sent and summed in bfloat16 or wider, within the bound.
No kernel may reach another device: no remote copies, remote signals or barrier semaphores. Data moves between devices by JAX's collectives and lax.ppermute only.
A program may use at most 128 MiB of HBM per device.

```python
import math
import jax
import jax.numpy as jnp
from jax import lax

D = 1536
SAMP_DEV = 16
IMG_TOK = 64
TXT_TOK = 32
SAMPLES = 256
N_DP = 16


def draw_valid_count(key, part):
    key = jax.random.fold_in(key, 7)
    positions_dp = jnp.arange(N_DP, dtype=jnp.int32)
    baseline = (SAMP_DEV + 2 * SAMP_DEV * positions_dp // max(N_DP - 1, 1)) // 3
    jitter_draw = jax.random.randint(key, (N_DP,), -(SAMP_DEV // 8), SAMP_DEV // 8 + 1, dtype=jnp.int32)
    counted = jnp.clip(baseline + jitter_draw, 1, SAMP_DEV)
    return jnp.where(positions_dp == N_DP - 1, SAMP_DEV, counted).astype(jnp.int32)


def strengthened(array, key, source, target, parts, factor):
    owner, partner = [(jnp.arange(array.shape[dim]) // (array.shape[dim] // parts)).reshape([-1 if axis == dim else 1 for axis in range(array.ndim)]) for dim in (source, target)]
    chosen = jax.random.permutation(key, parts)[partner]
    strong = (owner == chosen) | (owner == (partner + parts // 2) % parts)
    return jnp.where(strong, factor * array, array)


def block_scale(rng, dims, cuts, least, high):
    def one(dim, blocks):
        steps = jax.random.uniform(jax.random.fold_in(jax.random.fold_in(rng, 6), dim), (blocks,), jnp.float32, least / len(cuts), high / len(cuts))
        return jnp.repeat(jnp.exp(steps), dims[dim] // blocks).reshape((-1,) + (1,) * (len(dims) - dim - 1))

    loudness = one(*cuts[0])
    for cut in cuts[1:]:
        loudness = loudness * one(*cut)
    return loudness


def scatter_about(stream_key, extent, scale, bound, shards=(), kind=jnp.bfloat16):
    gain = block_scale(stream_key, extent, shards, -0.22, 0.18) if shards else 1.0
    drawn = jax.random.normal(stream_key, extent, jnp.float32) * scale * gain
    return jnp.minimum(jnp.maximum(drawn, -bound), bound).astype(kind)


def bell_draw_with(stream_key, extent, width, reach, shards, heavy, held_as=jnp.bfloat16):
    array = width * jax.random.normal(stream_key, extent, jnp.float32)
    if shards:
        array = array * block_scale(stream_key, extent, shards, -0.22, 0.18)
    return jnp.clip(strengthened(array, jax.random.fold_in(stream_key, 3), *heavy), -reach, reach).astype(held_as)


def setup_inputs(seed: int = 0) -> dict:
    key_of = jax.random.split(jax.random.key(seed), 9)
    image_tokens = bell_draw_with(key_of[0], (SAMPLES, IMG_TOK, D), 1.0, 6.0, ((0, 16),), (0, 2, 16, 2.0))
    text_tokens = bell_draw_with(key_of[1], (SAMPLES, TXT_TOK, D), 1.0, 6.0, ((0, 16),), (0, 2, 16, 2.0))
    image_weight = scatter_about(key_of[2], (D, D), D ** -0.5, 0.15625, ((1, 2),))
    text_weight = scatter_about(key_of[3], (D, D), D ** -0.5, 0.15625, ((1, 2),))
    logit_scale = jnp.clip(jax.random.uniform(key_of[4], (1,), jnp.float32, 6.0, 14.0), 6.0, 14.0)
    logit_bias = jnp.clip(jax.random.uniform(key_of[5], (1,), jnp.float32, -8.0, -5.0), -8.0, -5.0)
    loss_scale = jnp.clip(jnp.exp(jax.random.uniform(key_of[6], (1,), jnp.float32, math.log(256.0), math.log(4096.0))), 256.0, 4096.0)
    valid_count = draw_valid_count(jax.random.fold_in(key_of[8], 71), 0)
    return dict(image_tokens=image_tokens, text_tokens=text_tokens, image_weight=image_weight, text_weight=text_weight, logit_scale=logit_scale, logit_bias=logit_bias, loss_scale=loss_scale, valid_count=valid_count)


def gelu_slope(values):
    return jax.jvp(lambda inner: jax.nn.gelu(inner, approximate=True), (values,), (jnp.ones_like(values),))[1]

def tower_pooled(tokens, weight):
    blocks = tokens.reshape(N_DP, SAMP_DEV, tokens.shape[1], D)

    def one_block(block):
        flat_tokens = block.reshape(-1, D)
        preact = jnp.dot(flat_tokens, weight, preferred_element_type=jnp.float32)
        hidden = flat_tokens.astype(jnp.float32) + jax.nn.gelu(preact, approximate=True)
        return lax.optimization_barrier(jnp.mean(hidden.reshape(SAMP_DEV, block.shape[1], D), axis=1))
    return lax.map(one_block, blocks).reshape(-1, D)

def tower_weight_grad(tokens, weight, grad_pooled):
    token_count = tokens.shape[1]
    blocks = tokens.reshape(N_DP, SAMP_DEV, token_count, D)
    grads = grad_pooled.reshape(N_DP, SAMP_DEV, D)

    def one_block(total_grad, paired):
        block, grad_block = paired
        flat_tokens = block.reshape(-1, D)
        preact = jnp.dot(flat_tokens, weight, preferred_element_type=jnp.float32)
        slope = gelu_slope(preact.reshape(SAMP_DEV, token_count, D))
        grad_preact = (grad_block[:, None, :] / token_count * slope).astype(jnp.bfloat16).reshape(-1, D)
        term = lax.dot_general(flat_tokens, grad_preact, (((0,), (0,)), ((), ())), preferred_element_type=jnp.float32)
        return (total_grad + term, None)
    result, _ = lax.scan(one_block, jnp.zeros((D, D), jnp.float32), (blocks, grads))
    return result

def unitize(pooled):
    norm = jnp.sqrt(lax.optimization_barrier(jnp.sum(pooled * pooled, axis=1)) + 1e-06)
    return (pooled / norm[:, None], norm)

def reference(image_tokens, text_tokens, image_weight, text_weight, logit_scale, logit_bias, loss_scale, valid_count):
    logit_mult = logit_scale[0]
    offset_term = logit_bias[0]
    image_unit, image_norm = unitize(tower_pooled(image_tokens, image_weight))
    text_unit, text_norm = unitize(tower_pooled(text_tokens, text_weight))
    image_bf = image_unit.astype(jnp.bfloat16)
    text_bf = text_unit.astype(jnp.bfloat16)
    indices = jnp.arange(SAMP_DEV * N_DP, dtype=jnp.int32)
    usable = indices % SAMP_DEV < valid_count[indices // SAMP_DEV]
    total_count = jnp.sum(valid_count).astype(jnp.float32)
    logits = logit_mult * jnp.dot(image_bf, text_bf.T, preferred_element_type=jnp.float32) + offset_term
    pair_sign = jnp.where(indices[:, None] == indices[None, :], 1.0, -1.0).astype(jnp.float32)
    weighting = usable[:, None] & usable[None, :]
    margin = -pair_sign * logits
    loss = jnp.sum(jnp.where(weighting, jax.nn.softplus(margin), 0.0)) / total_count
    grad_coeff = loss_scale[0] / total_count
    dlogit = (jnp.where(weighting, -pair_sign * jax.nn.sigmoid(margin), 0.0) * grad_coeff).astype(jnp.bfloat16)
    image_grad = logit_mult * jnp.dot(dlogit, text_bf, preferred_element_type=jnp.float32)
    text_grad = logit_mult * jnp.dot(dlogit.T, image_bf, preferred_element_type=jnp.float32)
    image_gp = (image_grad - image_unit * lax.optimization_barrier(jnp.sum(image_unit * image_grad, axis=1))[:, None]) / image_norm[:, None]
    text_gp = (text_grad - text_unit * lax.optimization_barrier(jnp.sum(text_unit * text_grad, axis=1))[:, None]) / text_norm[:, None]
    image_weight_grad = tower_weight_grad(image_tokens, image_weight, image_gp)
    text_weight_grad = tower_weight_grad(text_tokens, text_weight, text_gp)
    return (loss, image_weight_grad, text_weight_grad)
```

```python
import functools

import jax
import jax.numpy as jnp
from jax import lax
from jax.experimental import pallas as pl
from jax.experimental.pallas import tpu as pltpu
from jax.sharding import PartitionSpec as P

F32 = jnp.float32
BF16 = jnp.bfloat16
ROWS = 256
VMEM_BYTES = 48 * 2**20
HALF_MAX = 16384.0


def vmem():
    return pl.BlockSpec(memory_space=pltpu.VMEM)


def smem():
    return pl.BlockSpec(memory_space=pltpu.SMEM)


def anyplace():
    return pl.BlockSpec(memory_space=pl.ANY)


def params():
    return pltpu.CompilerParams(vmem_limit_bytes=VMEM_BYTES)


def gelu_and_slope(x):
    c = 0.7978845608028654
    square = x * x
    t = jnp.tanh(c * (x + 0.044715 * (square * x)))
    cdf = 0.5 * (1.0 + t)
    slope = cdf + 0.5 * x * (1.0 - t * t) * (c * (1.0 + 3 * 0.044715 * square))
    return x * cdf, slope


def forward_kernel(
    tokens_of,
    place_ref,
    image_hbm,
    text_hbm,
    image_w_hbm,
    text_w_hbm,
    pooled_ref,
    square_ref,
    image_slope_hbm,
    text_slope_hbm,
    image_v,
    text_v,
    image_w,
    text_w,
    image_slope,
    text_slope,
    in_sem,
    w_sem,
    out_sem,
):
    width = image_w.shape[1]
    samples = pooled_ref.shape[0] // 2
    image_tok, text_tok = tokens_of
    jobs = []
    for hbm, buf, w, slope, slope_hbm, tok, base in (
        (text_hbm, text_v, text_w, text_slope, text_slope_hbm, text_tok, samples),
        (image_hbm, image_v, image_w, image_slope, image_slope_hbm, image_tok, 0),
    ):
        for start in range(0, buf.shape[0], ROWS):
            jobs.append((hbm, buf, w, slope, slope_hbm, tok, base, start))
    w_copies = {}
    in_copies = []
    for n, (hbm, buf, w, slope, slope_hbm, tok, base, start) in enumerate(jobs):
        if start == 0:
            first = hbm is text_hbm
            copy = pltpu.make_async_copy(
                text_w_hbm if first else image_w_hbm, w, w_sem.at[0 if first else 1]
            )
            copy.start()
            w_copies[n] = copy
        copy = pltpu.make_async_copy(
            hbm.at[pl.ds(start, ROWS), :], buf.at[pl.ds(start, ROWS), :], in_sem.at[n]
        )
        copy.start()
        in_copies.append(copy)
    column = pl.multiple_of(place_ref[0] * width, 128)
    out_copies = []
    for n, (hbm, buf, w, slope, slope_hbm, tok, base, start) in enumerate(jobs):
        if n in w_copies:
            w_copies[n].wait()
        in_copies[n].wait()
        preact = jnp.dot(buf[pl.ds(start, ROWS), :], w[...], preferred_element_type=F32)
        value, slant = gelu_and_slope(preact)
        slope[pl.ds(start, ROWS), :] = slant
        copy = pltpu.make_async_copy(
            slope.at[pl.ds(start, ROWS), :], slope_hbm.at[pl.ds(start, ROWS), :], out_sem.at[n]
        )
        copy.start()
        out_copies.append(copy)
        hidden = buf[pl.ds(start, ROWS), pl.ds(column, width)].astype(F32) + value
        group = ROWS // tok
        pooled = jnp.sum(hidden.reshape(group, tok, width), axis=1) / tok
        pooled_ref[pl.ds(base + start // tok, group), :] = pooled
    pooled = pooled_ref[...]
    total = jnp.sum(pooled * pooled, axis=1, keepdims=True)
    square_ref[...] = jnp.broadcast_to(total, square_ref.shape)
    for copy in out_copies:
        copy.wait()


def forward(place, image_flat, text_flat, image_w, text_w, samples):
    width = image_w.shape[1]
    depth = image_w.shape[0]
    rows_i, rows_t = image_flat.shape[0], text_flat.shape[0]
    jobs = (rows_i + rows_t) // ROWS
    return pl.pallas_call(
        functools.partial(forward_kernel, (rows_i // samples, rows_t // samples)),
        out_shape=(
            jax.ShapeDtypeStruct((2 * samples, width), F32),
            jax.ShapeDtypeStruct((2 * samples, 128), F32),
            jax.ShapeDtypeStruct((rows_i, width), F32),
            jax.ShapeDtypeStruct((rows_t, width), F32),
        ),
        in_specs=[smem()] + [anyplace()] * 4,
        out_specs=(vmem(), vmem(), anyplace(), anyplace()),
        scratch_shapes=[
            pltpu.VMEM((rows_i, depth), BF16),
            pltpu.VMEM((rows_t, depth), BF16),
            pltpu.VMEM((depth, width), BF16),
            pltpu.VMEM((depth, width), BF16),
            pltpu.VMEM((rows_i, width), F32),
            pltpu.VMEM((rows_t, width), F32),
            pltpu.SemaphoreType.DMA((jobs,)),
            pltpu.SemaphoreType.DMA((2,)),
            pltpu.SemaphoreType.DMA((jobs,)),
        ],
        compiler_params=params(),
        cost_estimate=pl.CostEstimate(
            flops=2 * (rows_i + rows_t) * depth * width,
            bytes_accessed=2 * (rows_i + rows_t) * (depth + 2 * width) + 4 * depth * width,
            transcendentals=(rows_i + rows_t) * width,
        ),
    )(place, image_flat, text_flat, image_w, text_w)


def turn_kernel(owner_ref, tokens_ref, out_ref, most_ref, turned):
    turned[...] = tokens_ref[...].T
    largest = jnp.max(jnp.abs(tokens_ref[...]).astype(F32), axis=0, keepdims=True)
    largest = jnp.broadcast_to(jnp.max(largest, axis=1, keepdims=True), most_ref.shape)

    @pl.when(pl.program_id(0) == 0)
    def _():
        most_ref[...] = jnp.zeros_like(most_ref)

    most_ref[...] = jnp.maximum(most_ref[...], largest)
    blocks = owner_ref.shape[0]
    height = out_ref.shape[0] // blocks
    for q in range(blocks):
        source = pl.multiple_of(owner_ref[q] * height, height)
        out_ref[q * height : (q + 1) * height, :] = turned[pl.ds(source, height), :]


def turn(owners, flat):
    rows, depth = flat.shape
    blocks = owners.shape[0]
    if (depth // blocks) % 16:
        turned = flat.T.reshape(blocks, depth // blocks, rows)[owners].reshape(depth, rows)
        return turned, jnp.max(jnp.abs(flat)).astype(F32)
    turned, most = pl.pallas_call(
        turn_kernel,
        out_shape=(
            jax.ShapeDtypeStruct((depth, rows), flat.dtype),
            jax.ShapeDtypeStruct((8, 128), F32),
        ),
        grid=(rows // ROWS,),
        in_specs=[smem(), pl.BlockSpec((ROWS, depth), lambda i: (i, 0))],
        out_specs=(
            pl.BlockSpec((depth, ROWS), lambda i: (0, i)),
            pl.BlockSpec((8, 128), lambda i: (0, 0)),
        ),
        scratch_shapes=[pltpu.VMEM((depth, ROWS), flat.dtype)],
        compiler_params=params(),
        cost_estimate=pl.CostEstimate(
            flops=0, bytes_accessed=4 * rows * depth, transcendentals=0
        ),
    )(owners, flat)
    return turned, most[0, 0]


def row_products(left, right):
    return lax.dot_general(left, right, (((1,), (1,)), ((), ())), preferred_element_type=F32)


def towers(blocks_ref, samples):
    blocks, _, width = blocks_ref.shape
    image = blocks_ref[:, :samples, :].reshape(blocks * samples, width)
    text = blocks_ref[:, samples:, :].reshape(blocks * samples, width)
    return image, text


def product_kernel(near_ref, far_ref, out_ref):
    samples = near_ref.shape[1] // 2
    own_image = near_ref[0, :samples, :]
    own_text = near_ref[0, samples:, :]
    start = 0
    for ref in (near_ref, far_ref):
        image, text = towers(ref, samples)
        stop = start + image.shape[0]
        out_ref[:samples, start:stop] = row_products(own_image, text)
        out_ref[samples:, start:stop] = row_products(own_text, image)
        start = stop


def products(near, far):
    blocks, both, _ = near.shape
    return pl.pallas_call(
        product_kernel,
        out_shape=jax.ShapeDtypeStruct((both, blocks * both), F32),
        in_specs=[vmem()] * 2,
        out_specs=vmem(),
        compiler_params=params(),
    )(near, far)


def middle_kernel(
    tokens_of,
    scalar_ref,
    own_ref,
    other_ref,
    column_ref,
    row_ref,
    near_ref,
    far_ref,
    unit_ref,
    norm_ref,
    grad_ref,
    loss_ref,
):
    samples = near_ref.shape[1] // 2
    split = near_ref.shape[0] * samples
    scale, bias, coeff = scalar_ref[0], scalar_ref[1], scalar_ref[2]
    dots = own_ref[...] + other_ref[...]
    logits = scale * dots + bias
    row = lax.broadcasted_iota(jnp.int32, dots.shape, 0) % samples
    column = lax.broadcasted_iota(jnp.int32, dots.shape, 1)
    sign = jnp.where(row == column, 1.0, -1.0).astype(F32)
    used = row_ref[...] * column_ref[...] > 0.5
    margin = -sign * logits
    small = jnp.exp(-jnp.abs(margin))
    soft = jnp.maximum(margin, 0.0) + jnp.log1p(small)
    sigmoid = jnp.where(margin >= 0, 1.0, small) / (1.0 + small)
    part = jnp.where(used, soft, 0.0)[:samples, :]
    loss_ref[...] = jnp.broadcast_to(
        jnp.sum(jnp.sum(part, axis=1, keepdims=True), axis=0, keepdims=True), loss_ref.shape
    )
    dlogit = (jnp.where(used, -sign * sigmoid, 0.0) * coeff).astype(BF16)
    radial = scale * jnp.sum(dlogit.astype(F32) * dots, axis=1, keepdims=True)
    near_image, near_text = towers(near_ref, samples)
    far_image, far_text = towers(far_ref, samples)
    for start, near, far, tokens in (
        (0, near_text, far_text, tokens_of[0]),
        (samples, near_image, far_image, tokens_of[1]),
    ):
        stop = start + samples
        weights = dlogit[start:stop, :]
        raw = jnp.dot(weights[:, :split], near, preferred_element_type=F32)
        raw += jnp.dot(weights[:, split:], far, preferred_element_type=F32)
        inward = unit_ref[start:stop, :] * radial[start:stop, :]
        grad_ref[start:stop, :] = (scale * raw - inward) / norm_ref[start:stop, :] / tokens


def middle(tokens_of, scalars, own, other, columns, rows, near, far, unit, norm):
    return pl.pallas_call(
        functools.partial(middle_kernel, tokens_of),
        out_shape=(
            jax.ShapeDtypeStruct(unit.shape, F32),
            jax.ShapeDtypeStruct((8, 128), F32),
        ),
        in_specs=[smem()] + [vmem()] * 8,
        out_specs=(vmem(), vmem()),
        compiler_params=params(),
    )(scalars, own, other, columns, rows, near, far, unit, norm)


def weight_kernel(grad_ref, slope_ref, turned_ref, send_ref, keep_ref, preact_grad):
    step = pl.program_id(0)
    half = pl.num_programs(0) // 2

    @pl.when(step == 0)
    def _():
        samples, width = grad_ref.shape
        rows = slope_ref.shape[0]
        slope = slope_ref[...].reshape(samples, rows // samples, width)
        grad = grad_ref[...].reshape(samples, 1, width)
        preact_grad[...] = (grad * slope).reshape(rows, width).astype(BF16)

    term = jnp.dot(turned_ref[...], preact_grad[...], preferred_element_type=F32)

    @pl.when(step < half)
    def _():
        send_ref[...] = term

    @pl.when(step >= half)
    def _():
        keep_ref[...] = term


def weight_terms(grad, slope, turned, start, width, base):
    depth, rows = turned.shape
    samples = grad.shape[0] // 2
    half = depth // 2 // ROWS
    chunk = start // width
    return pl.pallas_call(
        weight_kernel,
        grid=(2 * half,),
        out_shape=(jax.ShapeDtypeStruct((depth // 2, width), F32),) * 2,
        in_specs=[
            pl.BlockSpec((samples, width), lambda i: (base, chunk)),
            pl.BlockSpec((rows, width), lambda i: (0, chunk)),
            pl.BlockSpec((ROWS, rows), lambda i: ((i + half) % (2 * half), 0)),
        ],
        out_specs=(
            pl.BlockSpec((ROWS, width), lambda i: (jnp.minimum(i, half - 1), 0)),
            pl.BlockSpec((ROWS, width), lambda i: (jnp.maximum(i - half, 0), 0)),
        ),
        scratch_shapes=[pltpu.VMEM((rows, width), BF16)],
        compiler_params=params(),
        cost_estimate=pl.CostEstimate(
            flops=2 * depth * rows * width,
            bytes_accessed=2 * depth * rows + 4 * rows * width + 4 * depth * width,
            transcendentals=0,
        ),
    )(grad, slope, turned)


def body(
    image_tokens,
    text_tokens,
    image_weight,
    text_weight,
    logit_scale,
    logit_bias,
    loss_scale,
    valid_count,
):
    samples, image_tok, depth = image_tokens.shape
    text_tok = text_tokens.shape[1]
    width = image_weight.shape[1]
    cycle = lax.axis_size("dp")
    bits = cycle.bit_length() - 1
    place = lax.axis_index("dp")

    def swap(array, mask):
        return lax.ppermute(array, "dp", [(i, i ^ mask) for i in range(cycle)])

    def swap_halves(array):
        return lax.ppermute(array, "mp", [(0, 1), (1, 0)])

    def reverse(value):
        return sum(((value >> b) & 1) << (bits - 1 - b) for b in range(bits))

    image_flat = image_tokens.reshape(-1, depth)
    text_flat = text_tokens.reshape(-1, depth)
    owners = jnp.asarray([reverse(q) for q in range(cycle)], jnp.int32) ^ place

    counts = valid_count
    for b in reversed(range(bits)):
        counts = jnp.concatenate([counts, swap(counts, 1 << b)])
    positions = jnp.arange(samples, dtype=jnp.int32)
    columns = (positions[None, :] < counts[:, None]).astype(F32).reshape(1, -1)
    rows = (positions < valid_count[0]).astype(F32)
    rows = jnp.concatenate([rows, rows])[:, None]
    total = jnp.sum(counts).astype(F32)
    scalars = jnp.stack([logit_scale[0], logit_bias[0], loss_scale[0] / total])

    model_place = lax.axis_index("mp").astype(jnp.int32).reshape(1)
    pooled, square, image_slope, text_slope = forward(
        model_place, image_flat, text_flat, image_weight, text_weight, samples
    )
    norm = jnp.sqrt(square[:, :1] + swap_halves(square)[:, :1] + 1e-06)
    unit = pooled / norm
    unit_bf = unit.astype(BF16)

    gathered = unit_bf[None]
    low = 0
    if bits >= 2:
        low = bits - 2
        one, two = 1 << (bits - 1), 1 << (bits - 2)
        parts = [unit_bf] + [swap(unit_bf, mask) for mask in (one, two, one | two)]
        gathered = jnp.stack(parts)
    for b in reversed(range(1, low)):
        gathered = jnp.concatenate([gathered, swap(gathered, 1 << b)])
    near, far = gathered, swap(gathered, 1)

    image_turned, image_most = turn(owners, image_flat)
    text_turned, text_most = turn(owners, text_flat)

    own_dots = products(near, far)
    other_dots = swap_halves(own_dots)
    grad, loss_part = middle(
        (image_tok, text_tok), scalars, own_dots, other_dots, columns, rows, near, far, unit, norm
    )
    steepest = jnp.max(jnp.abs(grad).reshape(2, -1), axis=1)
    sizes = jnp.stack([image_most * image_tok, text_most * text_tok])
    loss_sum, limits = loss_part[0, :1], 1.2 * cycle * samples * sizes * steepest
    for b in range(bits):
        there = swap(jnp.concatenate([loss_sum, limits]), 1 << b)
        loss_sum, limits = loss_sum + there[:1], jnp.maximum(limits, there[1:])
    loss = loss_sum[0] / total

    def reduce(keep, send, factor):
        left = (keep + swap(send, 1)) * factor
        for b in range(1, low):
            half = left.shape[0] // 2
            there = swap(left[half:].astype(jnp.float16), 1 << b)
            left = left[:half] + there.astype(F32)
        if low:
            quarter = left.shape[0] // 4
            pieces = [
                swap(left[k * quarter : (k + 1) * quarter].astype(jnp.float16), mask)
                for k, mask in ((1, one), (2, two), (3, one | two))
            ]
            left = left[:quarter] + sum(piece.astype(F32) for piece in pieces)
        return left / factor

    outputs = []
    chunk = width // 2
    for slope, turned, base, limit in (
        (text_slope, text_turned, 1, limits[1]),
        (image_slope, image_turned, 0, limits[0]),
    ):
        factor = HALF_MAX / jnp.maximum(limit, 1e-30)
        done = []
        for start in range(0, width, chunk):
            send, keep = weight_terms(grad, slope, turned, start, chunk, base)
            done.append(reduce(keep, send, factor))
        outputs.append(jnp.concatenate(done, axis=1))
    return (loss, outputs[1], outputs[0])


def solution(mesh):
    placed = (
        P("dp", None, None),
        P("dp", None, None),
        P(None, "mp"),
        P(None, "mp"),
        P(),
        P(),
        P(),
        P("dp"),
    )
    return jax.shard_map(
        body,
        mesh=mesh,
        in_specs=placed,
        out_specs=(P(), P("dp", "mp"), P("dp", "mp")),
        check_vma=False,
    )
```

```python
import functools

import jax
import jax.numpy as jnp
from jax import lax
from jax.experimental import pallas as pl
from jax.experimental.pallas import tpu as pltpu
from jax.sharding import PartitionSpec as P

F32 = jnp.float32
BF16 = jnp.bfloat16
ROWS = 256
JOB_ROWS = 512
ROOT = 0.7978845608028654
HALF_MAX = 16384.0
UNUSABLE = 2.0
CHUNKS = 2


def vmem():
    return pl.BlockSpec(memory_space=pltpu.VMEM)


def smem():
    return pl.BlockSpec(memory_space=pltpu.SMEM)


def anyplace():
    return pl.BlockSpec(memory_space=pl.ANY)


def hbm():
    return pl.BlockSpec(memory_space=pltpu.HBM)


def params(mib):
    return pltpu.CompilerParams(vmem_limit_bytes=mib * 2**20)


def gelu(x):
    return x * (0.5 * (1.0 + jnp.tanh(ROOT * (x + 0.044715 * (x * x * x)))))


def gelu_slope(x):
    square = x * x
    t = jnp.tanh(ROOT * (x + 0.044715 * (square * x)))
    rise = (0.5 * x) * (1.0 - t * t) * (ROOT + (3 * 0.044715 * ROOT) * square)
    return 0.5 * (1.0 + t) + rise


def in_strips(rows, width, height, work):
    def step(i, carry):
        here = pl.ds(pl.multiple_of(i * height, height), height)
        for column in range(0, width, 128):
            work(i, here, slice(column, column + 128))
        return carry

    lax.fori_loop(0, rows // height, step, 0)


def forward_kernel(
    tokens_of,
    place_ref,
    image_hbm,
    text_hbm,
    image_w_hbm,
    text_w_hbm,
    pooled_ref,
    square_ref,
    image_pre_hbm,
    text_pre_hbm,
    image_v,
    text_v,
    image_w,
    text_w,
    image_pre,
    text_pre,
    in_sem,
    w_sem,
    out_sem,
):
    width = image_w.shape[1]
    samples = pooled_ref.shape[0] // 2
    jobs = []
    for source, buf, w_source, w, pre, pre_out, tok, base in (
        (text_hbm, text_v, text_w_hbm, text_w, text_pre, text_pre_hbm, tokens_of[1], samples),
        (image_hbm, image_v, image_w_hbm, image_w, image_pre, image_pre_hbm, tokens_of[0], 0),
    ):
        for start in range(0, buf.shape[0], JOB_ROWS):
            jobs.append((source, buf, w_source, w, pre, pre_out, tok, base, start))
    waits = []
    weights = 0
    for n, (source, buf, w_source, w, _, _, _, _, start) in enumerate(jobs):
        here = []
        if start == 0:
            here.append(pltpu.make_async_copy(w_source, w, w_sem.at[weights]))
            weights += 1
        part = pl.ds(start, JOB_ROWS)
        here.append(pltpu.make_async_copy(source.at[part, :], buf.at[part, :], in_sem.at[n]))
        for copy in here:
            copy.start()
        waits.append(here)
    first = place_ref[0] * width

    def project(n):
        _, buf, _, w, pre, _, _, _, start = jobs[n]
        for copy in waits[n]:
            copy.wait()
        part = pl.ds(start, JOB_ROWS)
        pre[part, :] = jnp.dot(buf[part, :], w[...], preferred_element_type=F32)

    out_copies = []
    project(0)
    for n, (_, buf, _, _, pre, pre_out, tok, base, start) in enumerate(jobs):
        part = pl.ds(start, JOB_ROWS)
        copy = pltpu.make_async_copy(pre.at[part, :], pre_out.at[part, :], out_sem.at[n])
        copy.start()
        out_copies.append(copy)
        if n + 1 < len(jobs):
            project(n + 1)
        for row in range(start, start + JOB_ROWS, tok):
            sample = base + row // tok
            for column in range(0, width, 128):
                token_columns = pl.ds(pl.multiple_of(first + column, 128), 128)
                value = gelu(pre[row : row + tok, column : column + 128])
                hidden = buf[row : row + tok, token_columns].astype(F32) + value
                pooled_ref[sample : sample + 1, column : column + 128] = (
                    jnp.sum(hidden, axis=0, keepdims=True) / tok
                )
    pooled = pooled_ref[...]
    total = jnp.sum(pooled * pooled, axis=1, keepdims=True)
    square_ref[...] = jnp.broadcast_to(total, square_ref.shape)
    for copy in out_copies:
        copy.wait()


def forward(place, image_flat, text_flat, image_w, text_w, samples):
    width = image_w.shape[1]
    depth = image_w.shape[0]
    rows_i, rows_t = image_flat.shape[0], text_flat.shape[0]
    jobs = (rows_i + rows_t) // JOB_ROWS
    return pl.pallas_call(
        functools.partial(forward_kernel, (rows_i // samples, rows_t // samples)),
        out_shape=(
            jax.ShapeDtypeStruct((2 * samples, width), F32),
            jax.ShapeDtypeStruct((2 * samples, 128), F32),
            jax.ShapeDtypeStruct((rows_i, width), F32),
            jax.ShapeDtypeStruct((rows_t, width), F32),
        ),
        in_specs=[smem()] + [hbm()] * 4,
        out_specs=(vmem(), vmem(), hbm(), hbm()),
        scratch_shapes=[
            pltpu.VMEM((rows_i, depth), BF16),
            pltpu.VMEM((rows_t, depth), BF16),
            pltpu.VMEM((depth, width), BF16),
            pltpu.VMEM((depth, width), BF16),
            pltpu.VMEM((rows_i, width), F32),
            pltpu.VMEM((rows_t, width), F32),
            pltpu.SemaphoreType.DMA((jobs,)),
            pltpu.SemaphoreType.DMA((2,)),
            pltpu.SemaphoreType.DMA((jobs,)),
        ],
        compiler_params=params(63),
        cost_estimate=pl.CostEstimate(
            flops=2 * (rows_i + rows_t) * depth * width,
            bytes_accessed=2 * (rows_i + rows_t) * (depth + 2 * width) + 4 * depth * width,
            transcendentals=(rows_i + rows_t) * width,
        ),
    )(place, image_flat, text_flat, image_w, text_w)


def unit_kernel(count_ref, pooled_ref, own_ref, other_ref, unit_ref, sent_ref, norm_ref):
    both = pooled_ref.shape[0]
    norm = jnp.sqrt(own_ref[...] + other_ref[...] + 1e-06)
    norm_ref[...] = norm
    unit = pooled_ref[...] / norm[:, :1]
    unit_ref[...] = unit
    row = lax.broadcasted_iota(jnp.int32, unit.shape, 0) % (both // 2)
    sent_ref[...] = jnp.where(row < count_ref[0], unit, UNUSABLE).astype(BF16)


def units(count, pooled, own, other):
    return pl.pallas_call(
        unit_kernel,
        out_shape=(
            jax.ShapeDtypeStruct(pooled.shape, F32),
            jax.ShapeDtypeStruct(pooled.shape, BF16),
            jax.ShapeDtypeStruct(own.shape, F32),
        ),
        in_specs=[smem()] + [vmem()] * 3,
        out_specs=(vmem(),) * 3,
        compiler_params=params(4),
    )(count, pooled, own, other)


def stack_kernel(_, *refs):
    *parts, out_ref = refs
    for n, part in enumerate(parts):
        out_ref[n] = part[...]


def stack(parts, after):
    return pl.pallas_call(
        stack_kernel,
        out_shape=jax.ShapeDtypeStruct((len(parts), *parts[0].shape), parts[0].dtype),
        in_specs=[anyplace()] + [vmem()] * len(parts),
        out_specs=vmem(),
        compiler_params=params(4),
    )(after, *parts)


def prepare_kernel(source_ref, tokens_ref, pre_ref, _, turned_ref, most_ref, slope_ref, turned):
    def one(i, here, columns):
        slope_ref[here, columns] = gelu_slope(pre_ref[here, columns])

    in_strips(*pre_ref.shape, 32, one)
    turned[...] = tokens_ref[...].T
    largest = jnp.max(jnp.abs(tokens_ref[...]).astype(F32), axis=0, keepdims=True)
    largest = jnp.broadcast_to(jnp.max(largest, axis=1, keepdims=True), most_ref.shape)

    @pl.when(pl.program_id(0) == 0)
    def _():
        most_ref[...] = jnp.zeros_like(most_ref)

    most_ref[...] = jnp.maximum(most_ref[...], largest)
    blocks = source_ref.shape[0]
    height = turned_ref.shape[0] // blocks
    for q in range(blocks):
        source = pl.multiple_of(source_ref[q] * height, height)
        turned_ref[q * height : (q + 1) * height, :] = turned[pl.ds(source, height), :]


def prepare(sources, flat, pre, after):
    rows, depth = flat.shape
    width = pre.shape[1]
    blocks = sources.shape[0]
    odd = (depth // blocks) % 16
    picked = jnp.arange(16, dtype=jnp.int32) if odd else sources
    turned, most, slope = pl.pallas_call(
        prepare_kernel,
        out_shape=(
            jax.ShapeDtypeStruct((depth, rows), flat.dtype),
            jax.ShapeDtypeStruct((8, 128), F32),
            jax.ShapeDtypeStruct((rows, width), F32),
        ),
        grid=(rows // ROWS,),
        in_specs=[
            smem(),
            pl.BlockSpec((ROWS, depth), lambda i: (i, 0)),
            pl.BlockSpec((ROWS, width), lambda i: (i, 0)),
            anyplace(),
        ],
        out_specs=(
            pl.BlockSpec((depth, ROWS), lambda i: (0, i)),
            pl.BlockSpec((8, 128), lambda i: (0, 0)),
            pl.BlockSpec((ROWS, width), lambda i: (i, 0)),
        ),
        scratch_shapes=[pltpu.VMEM((depth, ROWS), flat.dtype)],
        compiler_params=params(16),
        cost_estimate=pl.CostEstimate(
            flops=0, bytes_accessed=4 * rows * depth + 8 * rows * width, transcendentals=0
        ),
    )(picked, flat, pre, after)
    if odd:
        turned = turned.reshape(blocks, depth // blocks, rows)[sources].reshape(depth, rows)
    return turned, most, slope


def row_products(left, right):
    return lax.dot_general(left, right, (((1,), (1,)), ((), ())), preferred_element_type=F32)


def towers(blocks_ref, samples):
    blocks, _, width = blocks_ref.shape
    image = blocks_ref[:, :samples, :].reshape(blocks * samples, width)
    text = blocks_ref[:, samples:, :].reshape(blocks * samples, width)
    return image, text


def product_kernel(image_most_ref, text_most_ref, *refs):
    *block_refs, out_ref, mark_ref = refs
    near_ref = block_refs[0]
    samples = near_ref.shape[1] // 2
    own_image = near_ref[0, :samples, :]
    own_text = near_ref[0, samples:, :]
    lane = lax.broadcasted_iota(jnp.int32, own_image.shape, 1)
    first = jnp.where(lane == 0, 1.0, 0.0).astype(BF16)
    start = 0
    for ref in block_refs:
        image, text = towers(ref, samples)
        stop = start + image.shape[0]
        found = row_products(jnp.concatenate([own_image, first], axis=0), text)
        out_ref[:samples, start:stop] = found[:samples]
        mark_ref[:, start:stop] = found[samples : samples + 8]
        out_ref[samples:, start:stop] = row_products(own_text, image)
        start = stop


def products(blocks, mosts):
    both = blocks[0].shape[1]
    columns = sum(b.shape[0] for b in blocks) * (both // 2)
    return pl.pallas_call(
        product_kernel,
        out_shape=(
            jax.ShapeDtypeStruct((both, columns), F32),
            jax.ShapeDtypeStruct((8, columns), F32),
        ),
        in_specs=[anyplace()] * 2 + [vmem()] * len(blocks),
        out_specs=(vmem(),) * 2,
        compiler_params=params(8),
    )(*mosts, *blocks)


def middle_kernel(
    tokens_of,
    scale_ref,
    bias_ref,
    gain_ref,
    count_ref,
    own_ref,
    other_ref,
    mark_ref,
    unit_ref,
    norm_ref,
    image_most_ref,
    text_most_ref,
    *refs,
):
    *block_refs, grad_ref, stat_ref = refs
    samples = unit_ref.shape[0] // 2
    scale, bias = scale_ref[0], bias_ref[0]
    dots = own_ref[...] + other_ref[...]
    logits = scale * dots + bias
    row = lax.broadcasted_iota(jnp.int32, dots.shape, 0) % samples
    column = lax.broadcasted_iota(jnp.int32, dots.shape, 1)
    sign = jnp.where(row == column, 1.0, -1.0).astype(F32)
    usable = jnp.where(mark_ref[:1, :] < 1.5, 1.0, 0.0)
    total = jnp.sum(usable, axis=1, keepdims=True)
    used = (usable > 0.5) & (row < count_ref[0])
    margin = -sign * logits
    small = jnp.exp(-jnp.abs(margin))
    soft = jnp.maximum(margin, 0.0) + jnp.log1p(small)
    sigmoid = jnp.where(margin >= 0, 1.0, small) / (1.0 + small)
    part = jnp.where(used, soft, 0.0)[:samples, :]
    loss = jnp.sum(jnp.sum(part, axis=1, keepdims=True), axis=0, keepdims=True) / total
    coeff = gain_ref[0] / total
    dlogit = (jnp.where(used, -sign * sigmoid, 0.0) * coeff).astype(BF16)
    radial = scale * jnp.sum(dlogit.astype(F32) * dots, axis=1, keepdims=True)
    raws = [jnp.zeros((samples, unit_ref.shape[1]), F32) for _ in range(2)]
    start = 0
    for ref in block_refs:
        image, text = towers(ref, samples)
        stop = start + image.shape[0]
        raws[0] += jnp.dot(dlogit[:samples, start:stop], text, preferred_element_type=F32)
        raws[1] += jnp.dot(dlogit[samples:, start:stop], image, preferred_element_type=F32)
        start = stop
    limits = []
    for n, most_ref in enumerate((image_most_ref, text_most_ref)):
        here = slice(n * samples, (n + 1) * samples)
        inward = unit_ref[here, :] * radial[here, :]
        grad = (scale * raws[n] - inward) / norm_ref[here, :1] / tokens_of[n]
        grad_ref[here, :] = grad
        steep = jnp.max(jnp.max(jnp.abs(grad), axis=1, keepdims=True), axis=0, keepdims=True)
        limits.append(1.2 * samples * tokens_of[n] * most_ref[:1, :1] * steep)
    line = lax.broadcasted_iota(jnp.int32, stat_ref.shape, 0)
    stat_ref[...] = jnp.where(line == 0, loss, jnp.where(line == 1, limits[0], limits[1]))


def middle(tokens_of, scale, bias, gain, count, own, other, mark, unit, norm, mosts, blocks):
    return pl.pallas_call(
        functools.partial(middle_kernel, tokens_of),
        out_shape=(
            jax.ShapeDtypeStruct(unit.shape, F32),
            jax.ShapeDtypeStruct((8, unit.shape[1]), F32),
        ),
        in_specs=[smem()] * 4 + [vmem()] * (7 + len(blocks)),
        out_specs=(vmem(), vmem()),
        compiler_params=params(12),
    )(scale, bias, gain, count, own, other, mark, unit, norm, *mosts, *blocks)


def weight_kernel(base, chunk, carries, first, grad_ref, slope_hbm, turned_hbm, stat_ref, *refs):
    _, send_out, keep_out, grad_out, slope_v, turned_v, terms, slope_sem, in_sem, out_sem = refs
    _, height, width = terms.shape
    slope_copy = pltpu.make_async_copy(slope_hbm, slope_v if first else grad_out, slope_sem)
    slope_copy.start()
    copies = []
    for n in range(2):
        block = 2 * chunk + 1 - n
        copy = pltpu.make_async_copy(
            turned_hbm.at[pl.ds(block * height, height), :], turned_v.at[n], in_sem.at[n]
        )
        copy.start()
        copies.append(copy)
    out_copies = []
    if carries:
        copy = pltpu.make_async_copy(
            stat_ref, send_out.at[pl.ds(height, stat_ref.shape[0]), :], out_sem.at[2]
        )
        copy.start()
        out_copies.append(copy)
    slope_copy.wait()
    if first:
        samples = grad_ref.shape[0] // 2
        tok = slope_v.shape[0] // samples
        for sample in range(samples):
            here = slice(sample * tok, (sample + 1) * tok)
            row = base * samples + sample
            for column in range(0, width, 128):
                columns = slice(column, column + 128)
                slope = slope_v[here, columns]
                grad_out[here, columns] = (grad_ref[row : row + 1, columns] * slope).astype(BF16)
    for n, out in enumerate((send_out, keep_out)):
        copies[n].wait()
        terms[n] = jnp.dot(turned_v[n], grad_out[...], preferred_element_type=F32)
        copy = pltpu.make_async_copy(terms.at[n], out.at[pl.ds(0, height), :], out_sem.at[n])
        copy.start()
        out_copies.append(copy)
    for copy in out_copies:
        copy.wait()


def weight_terms(grad, slope, turned, stat, base, chunk, carries, first, after):
    depth, rows = turned.shape
    width = slope.shape[1]
    height = depth // (2 * CHUNKS)
    sent = height + (stat.shape[0] if carries else 0)
    return pl.pallas_call(
        functools.partial(weight_kernel, base, chunk, carries, first),
        out_shape=(
            jax.ShapeDtypeStruct((sent, width), F32),
            jax.ShapeDtypeStruct((height, width), F32),
            jax.ShapeDtypeStruct((rows, width), BF16),
        ),
        in_specs=[vmem(), anyplace(), anyplace(), vmem(), anyplace()],
        out_specs=(anyplace(), anyplace(), vmem()),
        scratch_shapes=[
            pltpu.VMEM((rows if first else 8, width), F32),
            pltpu.VMEM((2, height, rows), BF16),
            pltpu.VMEM((2, height, width), F32),
            pltpu.SemaphoreType.DMA,
            pltpu.SemaphoreType.DMA((2,)),
            pltpu.SemaphoreType.DMA((3,)),
        ],
        compiler_params=params(14),
        cost_estimate=pl.CostEstimate(
            flops=depth * rows * width,
            bytes_accessed=depth * rows + 4 * rows * width + 2 * depth * width,
            transcendentals=0,
        ),
    )(grad, slope, turned, stat, after)


def sum_of(terms):
    total = None
    for term, unit in terms:
        value = term if unit is None else term.astype(F32) * unit
        total = value if total is None else total + value
    return total


def body(
    image_tokens,
    text_tokens,
    image_weight,
    text_weight,
    logit_scale,
    logit_bias,
    loss_scale,
    valid_count,
):
    samples, image_tok, depth = image_tokens.shape
    text_tok = text_tokens.shape[1]
    width = image_weight.shape[1]
    cycle = lax.axis_size("dp")
    bits = cycle.bit_length() - 1
    place = lax.axis_index("dp")

    def swap(array, mask):
        return lax.ppermute(array, "dp", [(i, i ^ mask) for i in range(cycle)])

    def swap_halves(array):
        return lax.ppermute(array, "mp", [(0, 1), (1, 0)])

    def picked(order):
        owners = [
            sum(((q >> (bits - 1 - i)) & 1) << b for i, b in enumerate(order)) for q in range(cycle)
        ]
        return jnp.asarray(owners, jnp.int32) ^ place

    image_flat = image_tokens.reshape(-1, depth)
    text_flat = text_tokens.reshape(-1, depth)
    near_first = list(range(bits))
    far_first = [0] + list(range(2, bits)) + [1]
    text_orders, image_orders = (near_first, far_first), (near_first, near_first)

    def sources(orders):
        return jnp.concatenate([picked(order) * CHUNKS + c for c, order in enumerate(orders)])

    model_place = lax.axis_index("mp").astype(jnp.int32).reshape(1)
    pooled, square, image_pre, text_pre = forward(
        model_place, image_flat, text_flat, image_weight, text_weight, samples
    )
    unit, sent, norm = units(valid_count, pooled, square, swap_halves(square))

    low = max(bits - 2, 1)
    tops = [1 << b for b in reversed(range(low, bits))]
    masks = tops + [tops[0] | tops[1]] if len(tops) == 2 else tops
    arrived = [swap(sent, mask) for mask in masks]
    image_turned, image_most, image_slope = prepare(
        sources(image_orders), image_flat, image_pre, sent
    )
    gathered = stack([sent] + arrived, image_most)
    text_turned, text_most, text_slope = prepare(
        sources(text_orders), text_flat, text_pre, gathered
    )
    blocks = [gathered]
    for b in reversed(range(1, low)):
        blocks = blocks + [swap(block, 1 << b) for block in blocks]
    far = [swap(block, 1) for block in blocks[:1]]
    for block in blocks[1:]:
        far.append(swap(stack([block], text_most)[0], 1))
    blocks = blocks + far

    own_dots, mark = products(blocks, (image_most, text_most))
    grad, stat = middle(
        (image_tok, text_tok),
        logit_scale,
        logit_bias,
        loss_scale,
        valid_count,
        own_dots,
        swap_halves(own_dots),
        mark,
        unit,
        norm,
        (image_most, text_most),
        blocks,
    )

    def terms_of(slope, turned, base, chunk, carries, after):
        first = chunk == 0
        return weight_terms(grad, slope, turned, stat, base, chunk, carries, first, after)

    def split(sent, kept):
        height = kept.shape[0]
        there = swap(sent, 1)
        return [(kept, None), (there[:height], None)], there[height:]

    def level(terms, line, bit, here, there, after):
        half = terms[0][0].shape[0] // 2
        leaving = sum_of([(term[half:], unit) for term, unit in terms])
        factor = HALF_MAX / jnp.maximum(here[line : line + 1], 1e-30)
        for array in after:
            factor = factor + 0.0 * array[:1].astype(F32)
        coded = (leaving * factor).astype(jnp.float16)
        coming = swap(coded, 1 << bit)
        unit = jnp.maximum(there[line : line + 1], 1e-30) / HALF_MAX
        return [(term[:half], u) for term, u in terms] + [(coming, unit)], coded, coming

    send, keep, text_grad = terms_of(text_slope, text_turned, 1, 0, True, grad)
    text0, stat_there = split(send, keep)
    near_stats = [stat + stat_there]
    near_theres = [swap(near_stats[0], 1 << near_first[1])]
    far_stats = [near_stats[0]]
    far_theres = [swap(far_stats[0], 1 << far_first[1])]
    text0, coded, text0_in = level(text0, 2, near_first[1], near_stats[0], near_theres[0], ())

    send, keep, _ = terms_of(text_grad, text_turned, 1, 1, False, text_grad)
    text1, _ = split(send, keep)
    after = coded[:8].astype(F32)
    text1, coded, text1_in = level(text1, 2, far_first[1], far_stats[0], far_theres[0], (coded,))

    send, keep, image_grad = terms_of(image_slope, image_turned, 0, 0, False, after)
    image0, _ = split(send, keep)
    after = coded[:8].astype(F32)
    image0, coded, _ = level(
        image0, 1, near_first[1], near_stats[0], near_theres[0], (coded,)
    )
    send, keep, _ = terms_of(image_grad, image_turned, 0, 1, False, after)
    image1, _ = split(send, keep)

    for step in range(2, bits):
        last = step == bits - 1
        near_stats.append(near_stats[-1] + near_theres[-1] + 0.0 * text0_in[:8].astype(F32))
        near_theres.append(swap(near_stats[-1], 1 << near_first[step]))
        if not last:
            far_stats.append(far_stats[-1] + far_theres[-1] + 0.0 * text1_in[:8].astype(F32))
            far_theres.append(swap(far_stats[-1], 1 << far_first[step]))
            text1, coded, text1_in = level(
                text1, 2, far_first[step], far_stats[-1], far_theres[-1], (coded,)
            )
        text0, coded, text0_in = level(
            text0, 2, near_first[step], near_stats[-1], near_theres[-1], (coded,)
        )
        if step == 2:
            image1, coded, _ = level(
                image1, 1, near_first[1], near_stats[0], near_theres[0], (coded, text0_in)
            )
    full = near_stats[-1] + near_theres[-1]
    loss = full[0, 0]
    text1, coded, _ = level(text1, 2, far_first[-1], full, full, (coded,))
    for step in range(2, bits):
        image0, coded, _ = level(
            image0, 1, near_first[step], near_stats[step - 1], near_theres[step - 1], (coded,)
        )
    for step in range(2, bits):
        image1, coded, _ = level(
            image1, 1, near_first[step], near_stats[step - 1], near_theres[step - 1], (coded,)
        )
    text = jnp.concatenate([sum_of(text0), sum_of(text1)])
    image = jnp.concatenate([sum_of(image0), sum_of(image1)])
    return (loss, image, text)


def solution(mesh):
    placed = (
        P("dp", None, None),
        P("dp", None, None),
        P(None, "mp"),
        P(None, "mp"),
        P(),
        P(),
        P(),
        P("dp"),
    )
    return jax.shard_map(
        body,
        mesh=mesh,
        in_specs=placed,
        out_specs=(P(), P("dp", "mp"), P("dp", "mp")),
        check_vma=False,
    )
```

```python
import functools

import jax
import jax.numpy as jnp
from jax import lax
from jax.experimental import pallas as pl
from jax.experimental.pallas import tpu as pltpu
from jax.sharding import PartitionSpec as P

F32 = jnp.float32
BF16 = jnp.bfloat16
ROWS = 256
JOB_ROWS = 512
JOB_COLUMNS = 256
STRIP = 64
ROOT = 0.7978845608028654
HALF_MAX = 16384.0
UNUSABLE = 2.0


def vmem():
    return pl.BlockSpec(memory_space=pltpu.VMEM)


def smem():
    return pl.BlockSpec(memory_space=pltpu.SMEM)


def anyplace():
    return pl.BlockSpec(memory_space=pl.ANY)


def hbm():
    return pl.BlockSpec(memory_space=pltpu.HBM)


def params(mib):
    return pltpu.CompilerParams(vmem_limit_bytes=mib * 2**20)


def gelu_and_slope(x):
    square = x * x
    cdf = 0.5 + 0.5 * jnp.tanh(x * (ROOT + (0.044715 * ROOT) * square))
    value = x * cdf
    rise = (value - value * cdf) * (2 * ROOT + (6 * 0.044715 * ROOT) * square)
    return value, cdf + rise


def forward_kernel(
    tokens_of,
    place_ref,
    image_hbm,
    text_hbm,
    image_w_hbm,
    text_w_hbm,
    pooled_ref,
    square_ref,
    image_slope_hbm,
    text_slope_hbm,
    image_v,
    text_v,
    image_w,
    text_w,
    image_slope,
    text_slope,
    in_sem,
    w_sem,
    out_sem,
):
    width = image_w.shape[1]
    samples = pooled_ref.shape[0] // 2
    towers_here = (
        (text_hbm, text_v, text_w_hbm, text_w, text_slope, text_slope_hbm, tokens_of[1], samples),
        (image_hbm, image_v, image_w_hbm, image_w, image_slope, image_slope_hbm, tokens_of[0], 0),
    )
    waits, tiles = [], []
    for t, (source, buf, w_source, w, _, _, _, _) in enumerate(towers_here):
        here = [
            pltpu.make_async_copy(w_source, w, w_sem.at[t]),
            pltpu.make_async_copy(source, buf, in_sem.at[t]),
        ]
        for copy in here:
            copy.start()
        waits.append(here)
        for start in range(0, buf.shape[0], JOB_ROWS):
            for column in range(0, width, JOB_COLUMNS):
                tiles.append((t, start, column))
    first = place_ref[0] * width

    def project(n):
        t, start, column = tiles[n]
        _, buf, _, w, slope, _, _, _ = towers_here[t]
        if start == 0 and column == 0:
            for copy in waits[t]:
                copy.wait()
        rows, columns = slice(start, start + JOB_ROWS), slice(column, column + JOB_COLUMNS)
        slope[rows, columns] = jnp.dot(buf[rows, :], w[:, columns], preferred_element_type=F32)

    out_copies = []
    project(0)
    for n, (t, start, tile_column) in enumerate(tiles):
        _, buf, _, _, slope, slope_out, tok, base = towers_here[t]
        if n + 1 < len(tiles):
            project(n + 1)
        for row in range(start, start + JOB_ROWS, STRIP):
            rows = slice(row, row + STRIP)
            here = (rows, slice(tile_column, tile_column + JOB_COLUMNS))
            token_columns = pl.ds(pl.multiple_of(first + tile_column, 128), JOB_COLUMNS)
            value, slant = gelu_and_slope(slope[here])
            slope[here] = slant
            hidden = buf[rows, token_columns].astype(F32) + value
            for part in range(0, STRIP, tok):
                sample = base + (row + part) // tok
                pooled_ref[sample : sample + 1, here[1]] = (
                    jnp.sum(hidden[part : part + tok], axis=0, keepdims=True) / tok
                )
        if tile_column + JOB_COLUMNS == width:
            part = pl.ds(start, JOB_ROWS)
            copy = pltpu.make_async_copy(
                slope.at[part, :], slope_out.at[part, :], out_sem.at[len(out_copies)]
            )
            copy.start()
            out_copies.append(copy)
    pooled = pooled_ref[...]
    total = jnp.sum(pooled * pooled, axis=1, keepdims=True)
    square_ref[...] = jnp.broadcast_to(total, square_ref.shape)
    for copy in out_copies:
        copy.wait()


def forward(place, image_flat, text_flat, image_w, text_w, samples):
    width = image_w.shape[1]
    depth = image_w.shape[0]
    rows_i, rows_t = image_flat.shape[0], text_flat.shape[0]
    jobs = (rows_i + rows_t) // JOB_ROWS
    return pl.pallas_call(
        functools.partial(forward_kernel, (rows_i // samples, rows_t // samples)),
        out_shape=(
            jax.ShapeDtypeStruct((2 * samples, width), F32),
            jax.ShapeDtypeStruct((2 * samples, 128), F32),
            jax.ShapeDtypeStruct((rows_i, width), F32),
            jax.ShapeDtypeStruct((rows_t, width), F32),
        ),
        in_specs=[smem()] + [hbm()] * 4,
        out_specs=(vmem(), vmem(), hbm(), hbm()),
        scratch_shapes=[
            pltpu.VMEM((rows_i, depth), BF16),
            pltpu.VMEM((rows_t, depth), BF16),
            pltpu.VMEM((depth, width), BF16),
            pltpu.VMEM((depth, width), BF16),
            pltpu.VMEM((rows_i, width), F32),
            pltpu.VMEM((rows_t, width), F32),
            pltpu.SemaphoreType.DMA((2,)),
            pltpu.SemaphoreType.DMA((2,)),
            pltpu.SemaphoreType.DMA((jobs,)),
        ],
        compiler_params=params(53),
        cost_estimate=pl.CostEstimate(
            flops=2 * (rows_i + rows_t) * depth * width,
            bytes_accessed=2 * (rows_i + rows_t) * (depth + 2 * width) + 4 * depth * width,
            transcendentals=(rows_i + rows_t) * width,
        ),
    )(place, image_flat, text_flat, image_w, text_w)


def unit_kernel(count_ref, pooled_ref, own_ref, other_ref, unit_ref, sent_ref, norm_ref):
    both = pooled_ref.shape[0]
    norm = jnp.sqrt(own_ref[...] + other_ref[...] + 1e-06)
    norm_ref[...] = norm
    unit = pooled_ref[...] / norm[:, :1]
    unit_ref[...] = unit
    row = lax.broadcasted_iota(jnp.int32, unit.shape, 0) % (both // 2)
    sent_ref[...] = jnp.where(row < count_ref[0], unit, UNUSABLE).astype(BF16)


def units(count, pooled, own, other):
    return pl.pallas_call(
        unit_kernel,
        out_shape=(
            jax.ShapeDtypeStruct(pooled.shape, F32),
            jax.ShapeDtypeStruct(pooled.shape, BF16),
            jax.ShapeDtypeStruct(own.shape, F32),
        ),
        in_specs=[smem()] + [pl.BlockSpec()] * 3,
        out_specs=(vmem(),) * 3,
        compiler_params=params(4),
    )(count, pooled, own, other)


def stack_kernel(afters, *refs):
    parts, out_ref = refs[afters:-1], refs[-1]
    for n, part in enumerate(parts):
        out_ref[n] = part[...]


def stack(parts, *afters):
    return pl.pallas_call(
        functools.partial(stack_kernel, len(afters)),
        out_shape=jax.ShapeDtypeStruct((len(parts), *parts[0].shape), parts[0].dtype),
        in_specs=[anyplace()] * len(afters) + [vmem()] * len(parts),
        out_specs=vmem(),
        compiler_params=params(4),
    )(*afters, *parts)


def turn_kernel(source_ref, tokens_ref, _, turned_ref, most_ref, turned):
    rows, _ = tokens_ref.shape
    blocks = source_ref.shape[0]
    height = turned_ref.shape[0] // blocks
    largest = None
    for start in range(0, rows, ROWS):
        tokens = tokens_ref[start : start + ROWS, :]
        turned[...] = tokens.T
        most = jnp.max(jnp.abs(tokens).astype(F32), axis=0, keepdims=True)
        largest = most if largest is None else jnp.maximum(largest, most)
        for q in range(blocks):
            source = pl.multiple_of(source_ref[q] * height, height)
            turned_ref[q * height : (q + 1) * height, start : start + ROWS] = turned[
                pl.ds(source, height), :
            ]
    most_ref[...] = jnp.broadcast_to(jnp.max(largest, axis=1, keepdims=True), most_ref.shape)


def turn(sources, flat, after):
    rows, depth = flat.shape
    blocks = sources.shape[0]
    odd = (depth // blocks) % 16
    picked = jnp.arange(16, dtype=jnp.int32) if odd else sources
    turned, most = pl.pallas_call(
        turn_kernel,
        out_shape=(
            jax.ShapeDtypeStruct((depth, rows), flat.dtype),
            jax.ShapeDtypeStruct((8, 128), F32),
        ),
        in_specs=[smem(), vmem(), anyplace()],
        out_specs=(vmem(), vmem()),
        scratch_shapes=[pltpu.VMEM((depth, ROWS), flat.dtype)],
        compiler_params=params(8),
        cost_estimate=pl.CostEstimate(
            flops=0, bytes_accessed=4 * rows * depth, transcendentals=0
        ),
    )(picked, flat, after)
    if odd:
        turned = turned.reshape(blocks, depth // blocks, rows)[sources].reshape(depth, rows)
    return turned, most


def row_products(left, right):
    return lax.dot_general(left, right, (((1,), (1,)), ((), ())), preferred_element_type=F32)


def towers(blocks_ref, samples):
    blocks, _, width = blocks_ref.shape
    image = blocks_ref[:, :samples, :].reshape(blocks * samples, width)
    text = blocks_ref[:, samples:, :].reshape(blocks * samples, width)
    return image, text


def product_kernel(image_most_ref, text_most_ref, *refs):
    *block_refs, out_ref, mark_ref = refs
    near_ref = block_refs[0]
    samples = near_ref.shape[1] // 2
    own_image = near_ref[0, :samples, :]
    own_text = near_ref[0, samples:, :]
    lane = lax.broadcasted_iota(jnp.int32, own_image.shape, 1)
    first = jnp.where(lane == 0, 1.0, 0.0).astype(BF16)
    start = 0
    for ref in block_refs:
        image, text = towers(ref, samples)
        stop = start + image.shape[0]
        found = row_products(jnp.concatenate([own_image, first], axis=0), text)
        out_ref[:samples, start:stop] = found[:samples]
        mark_ref[:, start:stop] = found[samples : samples + 8]
        out_ref[samples:, start:stop] = row_products(own_text, image)
        start = stop


def products(blocks, mosts):
    both = blocks[0].shape[1]
    columns = sum(b.shape[0] for b in blocks) * (both // 2)
    return pl.pallas_call(
        product_kernel,
        out_shape=(
            jax.ShapeDtypeStruct((both, columns), F32),
            jax.ShapeDtypeStruct((8, columns), F32),
        ),
        in_specs=[anyplace()] * 2 + [vmem()] * len(blocks),
        out_specs=(vmem(),) * 2,
        compiler_params=params(8),
    )(*mosts, *blocks)


def middle_kernel(
    tokens_of,
    scale_ref,
    bias_ref,
    gain_ref,
    count_ref,
    own_ref,
    other_ref,
    mark_ref,
    unit_ref,
    norm_ref,
    image_most_ref,
    text_most_ref,
    *refs,
):
    *block_refs, grad_ref, stat_ref = refs
    samples = unit_ref.shape[0] // 2
    scale, bias = scale_ref[0], bias_ref[0]
    dots = own_ref[...] + other_ref[...]
    logits = scale * dots + bias
    row = lax.broadcasted_iota(jnp.int32, dots.shape, 0) % samples
    column = lax.broadcasted_iota(jnp.int32, dots.shape, 1)
    sign = jnp.where(row == column, 1.0, -1.0).astype(F32)
    usable = jnp.where(mark_ref[:1, :] < 1.5, 1.0, 0.0)
    total = jnp.sum(usable, axis=1, keepdims=True)
    used = (usable > 0.5) & (row < count_ref[0])
    margin = -sign * logits
    small = jnp.exp(-jnp.abs(margin))
    soft = jnp.maximum(margin, 0.0) + jnp.log1p(small)
    sigmoid = jnp.where(margin >= 0, 1.0, small) / (1.0 + small)
    part = jnp.where(used, soft, 0.0)[:samples, :]
    loss = jnp.sum(jnp.sum(part, axis=1, keepdims=True), axis=0, keepdims=True) / total
    coeff = gain_ref[0] / total
    dlogit = (jnp.where(used, -sign * sigmoid, 0.0) * coeff).astype(BF16)
    radial = scale * jnp.sum(dlogit.astype(F32) * dots, axis=1, keepdims=True)
    raws = [jnp.zeros((samples, unit_ref.shape[1]), F32) for _ in range(2)]
    start = 0
    for ref in block_refs:
        image, text = towers(ref, samples)
        stop = start + image.shape[0]
        raws[0] += jnp.dot(dlogit[:samples, start:stop], text, preferred_element_type=F32)
        raws[1] += jnp.dot(dlogit[samples:, start:stop], image, preferred_element_type=F32)
        start = stop
    limits = []
    for n, most_ref in enumerate((image_most_ref, text_most_ref)):
        here = slice(n * samples, (n + 1) * samples)
        inward = unit_ref[here, :] * radial[here, :]
        grad = (scale * raws[n] - inward) / norm_ref[here, :1] / tokens_of[n]
        grad_ref[here, :] = grad
        steep = jnp.max(jnp.max(jnp.abs(grad), axis=1, keepdims=True), axis=0, keepdims=True)
        limits.append(1.2 * samples * tokens_of[n] * most_ref[:1, :1] * steep)
    line = lax.broadcasted_iota(jnp.int32, stat_ref.shape, 0)
    stat_ref[...] = jnp.where(line == 0, loss, jnp.where(line == 1, limits[0], limits[1]))


def middle(tokens_of, scale, bias, gain, count, own, other, mark, unit, norm, mosts, blocks):
    return pl.pallas_call(
        functools.partial(middle_kernel, tokens_of),
        out_shape=(
            jax.ShapeDtypeStruct(unit.shape, F32),
            jax.ShapeDtypeStruct((8, unit.shape[1]), F32),
        ),
        in_specs=[smem()] * 4 + [vmem()] * (7 + len(blocks)),
        out_specs=(vmem(), vmem()),
        compiler_params=params(12),
    )(scale, bias, gain, count, own, other, mark, unit, norm, *mosts, *blocks)


def weight_kernel(
    base, carries, grad_ref, slope_ref, turned_ref, stat_ref, _, soon_ref, late_ref, keep_ref, preact_grad
):
    rows, width = slope_ref.shape
    samples = grad_ref.shape[0] // 2
    tok = rows // samples
    for sample in range(samples):
        here = slice(sample * tok, (sample + 1) * tok)
        row = base * samples + sample
        for column in range(0, width, 128):
            columns = slice(column, column + 128)
            slope = slope_ref[here, columns]
            preact_grad[here, columns] = (grad_ref[row : row + 1, columns] * slope).astype(BF16)
    height = late_ref.shape[0]
    if carries:
        soon_ref[height:, :] = stat_ref[...]
    for n, (out, start) in enumerate(
        ((soon_ref, 0), (late_ref, 0), (keep_ref, 0), (keep_ref, height))
    ):
        out[start : start + height, :] = jnp.dot(
            turned_ref[n * height : (n + 1) * height, :],
            preact_grad[...],
            preferred_element_type=F32,
        )


def weight_terms(grad, slope, turned, stat, base, carries, after):
    depth, rows = turned.shape
    width = slope.shape[1]
    quarter = depth // 4
    soon = quarter + (stat.shape[0] if carries else 0)
    return pl.pallas_call(
        functools.partial(weight_kernel, base, carries),
        out_shape=tuple(jax.ShapeDtypeStruct((n, width), F32) for n in (soon, quarter, 2 * quarter)),
        in_specs=[vmem()] * 4 + [anyplace()],
        out_specs=(vmem(),) * 3,
        scratch_shapes=[pltpu.VMEM((rows, width), BF16)],
        compiler_params=params(8),
        cost_estimate=pl.CostEstimate(
            flops=2 * depth * rows * width,
            bytes_accessed=2 * depth * rows + 4 * rows * width + 4 * depth * width,
            transcendentals=0,
        ),
    )(grad, slope, turned, stat, after)


def sum_of(terms):
    total = None
    for term, unit in terms:
        value = term if unit is None else term.astype(F32) * unit
        total = value if total is None else total + value
    return total


def body(
    image_tokens,
    text_tokens,
    image_weight,
    text_weight,
    logit_scale,
    logit_bias,
    loss_scale,
    valid_count,
):
    samples, image_tok, depth = image_tokens.shape
    text_tok = text_tokens.shape[1]
    width = image_weight.shape[1]
    cycle = lax.axis_size("dp")
    bits = cycle.bit_length() - 1
    place = lax.axis_index("dp")

    def swap(array, mask):
        return lax.ppermute(array, "dp", [(i, i ^ mask) for i in range(cycle)])

    def swap_halves(array):
        return lax.ppermute(array, "mp", [(0, 1), (1, 0)])

    def bits_of(value, order):
        return sum(((value >> (len(order) - 1 - i)) & 1) << b for i, b in enumerate(order))

    image_flat = image_tokens.reshape(-1, depth)
    text_flat = text_tokens.reshape(-1, depth)
    text_orders = [list(range(2, bits)), list(range(3, bits)) + [2]]
    image_order = [2, 1] + list(range(3, bits))
    later = [(c, q) for c in range(2) for q in range(cycle // 4)]
    text_blocks = [
        2 * (high + bits_of(q, text_orders[c])) + c for high in (3, 1, 0, 2) for c, q in later
    ]
    image_blocks = [
        high + bits_of(q, image_order[1:])
        for high in (5, 1, 0, 4)
        for q in range(cycle // 4)
    ]
    text_blocks = jnp.asarray(text_blocks, jnp.int32) ^ (2 * place)
    image_blocks = jnp.asarray(image_blocks, jnp.int32) ^ place

    model_place = lax.axis_index("mp").astype(jnp.int32).reshape(1)
    pooled, square, image_slope, text_slope = forward(
        model_place, image_flat, text_flat, image_weight, text_weight, samples
    )
    unit, sent, norm = units(valid_count, pooled, square, swap_halves(square))

    low = max(bits - 2, 1)
    tops = [1 << b for b in reversed(range(low, bits))]
    masks = tops + [tops[0] | tops[1]] if len(tops) == 2 else tops
    arrived = [swap(sent, mask) for mask in masks]
    image_turned, image_most = turn(image_blocks, image_flat, sent)
    gathered = stack([sent] + arrived, image_most)
    text_turned, text_most = turn(text_blocks, text_flat, gathered)
    blocks = [gathered]
    for b in reversed(range(1, low)):
        blocks = blocks + [swap(block, 1 << b) for block in blocks]
    far = [swap(block, 1) for block in blocks[:1]]
    for block in blocks[1:]:
        far.append(swap(stack([block], text_most)[0], 1))
    blocks = blocks + far

    own_dots, mark = products(blocks, (image_most, text_most))
    grad, stat = middle(
        (image_tok, text_tok),
        logit_scale,
        logit_bias,
        loss_scale,
        valid_count,
        own_dots,
        swap_halves(own_dots),
        mark,
        unit,
        norm,
        (image_most, text_most),
        blocks,
    )

    lines = lax.broadcasted_iota(jnp.int32, (16, width), 0)

    def footer(exponents, stat):
        rows = list(exponents)
        rest = stat[:1]
        for _ in range(3):
            part = lax.reduce_precision(rest, 5, 10)
            rows.append(part)
            rest = (rest - part) * 2048.0
        found = jnp.zeros((16, width), F32)
        for n, row in enumerate(rows):
            found = jnp.where(lines == n, row, found)
        return found

    def exponents_of(stat):
        return [jnp.ceil(jnp.log2(jnp.maximum(stat[n : n + 1], 1e-30))) for n in (1, 2)]

    def merged(stat, message):
        foot = message[-16:].astype(F32)
        loss = (foot[4:5] / 2048.0 + foot[3:4]) / 2048.0 + foot[2:3]
        there = [foot[:1], foot[1:2]]
        add = [loss, jnp.exp2(there[0]), jnp.exp2(there[1])]
        total = [stat[n : n + 1] + row for n, row in enumerate(add)]
        return jnp.concatenate(total), there

    def halves(terms):
        half = terms[0][0].shape[0] // 2
        return [[(term[rows], unit) for term, unit in terms] for rows in (slice(half), slice(half, None))]

    def leave(terms, stat, tower, bit, after):
        rows = terms[0][0].shape[0]
        exponents = exponents_of(stat)
        factor = HALF_MAX * jnp.exp2(-exponents[tower]) + 0.0 * after[:1].astype(F32)
        coded = sum_of(terms) * factor
        foot = footer(exponents, stat) + 0.0 * coded[:1]
        coded = jnp.pad(coded, ((0, 16), (0, 0))) + jnp.pad(foot, ((rows, 0), (0, 0)))
        coded = coded.astype(jnp.float16)
        return coded, swap(coded, 1 << bit)

    def take(terms, stat, tower, coming):
        stat, there = merged(stat, coming)
        return terms + [(coming[:-16], jnp.exp2(there[tower]) / HALF_MAX)], stat

    def core_step(soon, late, keep):
        height = late.shape[0]
        there = swap(soon, 1)
        stays = [(keep[:height], None), (swap(late, 1), None)]
        return stays, [(keep[height:], None), (there[:height], None)], there[height:]

    text_terms = weight_terms(grad, text_slope, text_turned, stat, 1, True, stat)
    text, text_leaves, stat_there = core_step(*text_terms)
    start_stat = stat[:3] + stat_there[:3]
    image_terms = weight_terms(grad, image_slope, image_turned, stat, 0, False, text_terms[0])
    image, image_leaves, _ = core_step(*image_terms)

    coded, text_in = leave(text_leaves, start_stat, 1, 1, start_stat)
    coded, image_in = leave(image_leaves, start_stat, 0, image_order[0], coded)
    text, text_stat = take(text, start_stat, 1, text_in)
    parts = [(terms, text_stat) for terms in halves(text)]
    image, image_stat = take(image, start_stat, 0, image_in)
    for step in range(bits - 2):
        last = step == bits - 3
        image, image_leaves = halves(image)
        if last:
            coded, image_in = leave(image_leaves, image_stat, 0, image_order[step + 1], coded)
        arrivals = []
        for order, (terms, terms_stat) in zip(text_orders, parts):
            terms, leaves = halves(terms)
            coded, arrival = leave(leaves, terms_stat, 1, order[step], coded)
            arrivals.append((terms, terms_stat, arrival))
        if not last:
            coded, image_in = leave(image_leaves, image_stat, 0, image_order[step + 1], coded)
        parts = [take(terms, old, 1, arrival) for terms, old, arrival in arrivals]
        image, image_stat = take(image, image_stat, 0, image_in)
    text = jnp.concatenate([sum_of(terms) for terms, _ in parts])
    loss = jnp.max(parts[0][1][0] + 0.0 * coded[0].astype(F32))
    return (loss, sum_of(image), text)


def solution(mesh):
    placed = (
        P("dp", None, None),
        P("dp", None, None),
        P(None, "mp"),
        P(None, "mp"),
        P(),
        P(),
        P(),
        P("dp"),
    )
    return jax.shard_map(
        body,
        mesh=mesh,
        in_specs=placed,
        out_specs=(P(), P("dp", "mp"), P("dp", "mp")),
        check_vma=False,
    )
```

```python
import functools

import jax
import jax.numpy as jnp
from jax import lax
from jax.experimental import pallas as pl
from jax.experimental.pallas import tpu as pltpu
from jax.sharding import PartitionSpec as P

F32 = jnp.float32
BF16 = jnp.bfloat16
ROWS = 256
JOB_ROWS = 256
JOB_COLUMNS = 256
STRIP = 64
ROOT = 0.7978845608028654
HALF_MAX = 16384.0
FOOT = 8
UNUSABLE = 2.0


def vmem():
    return pl.BlockSpec(memory_space=pltpu.VMEM)


def smem():
    return pl.BlockSpec(memory_space=pltpu.SMEM)


def anyplace():
    return pl.BlockSpec(memory_space=pl.ANY)


def hbm():
    return pl.BlockSpec(memory_space=pltpu.HBM)


def params(mib):
    return pltpu.CompilerParams(vmem_limit_bytes=mib * 2**20)


def gelu_and_slope(x):
    square = x * x
    cdf = 0.5 + 0.5 * jnp.tanh(x * (ROOT + (0.044715 * ROOT) * square))
    value = x * cdf
    rise = (value - value * cdf) * (2 * ROOT + (6 * 0.044715 * ROOT) * square)
    return value, cdf + rise


def forward_kernel(
    tokens_of,
    place_ref,
    image_hbm,
    text_hbm,
    image_w_hbm,
    text_w_hbm,
    pooled_ref,
    square_ref,
    image_slope_hbm,
    text_slope_hbm,
    image_v,
    text_v,
    image_w,
    text_w,
    image_slope,
    text_slope,
    in_sem,
    w_sem,
    out_sem,
):
    width = image_w.shape[1]
    samples = pooled_ref.shape[0] // 2
    towers_here = (
        (text_hbm, text_v, text_w_hbm, text_w, text_slope, text_slope_hbm, tokens_of[1], samples),
        (image_hbm, image_v, image_w_hbm, image_w, image_slope, image_slope_hbm, tokens_of[0], 0),
    )
    waits, tiles = [], []
    for t, (source, buf, w_source, w, _, _, _, _) in enumerate(towers_here):
        here = [
            pltpu.make_async_copy(w_source, w, w_sem.at[t]),
            pltpu.make_async_copy(source, buf, in_sem.at[t]),
        ]
        for copy in here:
            copy.start()
        waits.append(here)
        for start in range(0, buf.shape[0], JOB_ROWS):
            for column in range(0, width, JOB_COLUMNS):
                tiles.append((t, start, column))
    first = place_ref[0] * width

    def project(n):
        t, start, column = tiles[n]
        _, buf, _, w, slope, _, _, _ = towers_here[t]
        if start == 0 and column == 0:
            for copy in waits[t]:
                copy.wait()
        rows, columns = slice(start, start + JOB_ROWS), slice(column, column + JOB_COLUMNS)
        slope[rows, columns] = jnp.dot(buf[rows, :], w[:, columns], preferred_element_type=F32)

    out_copies = []
    project(0)
    for n, (t, start, tile_column) in enumerate(tiles):
        _, buf, _, _, slope, slope_out, tok, base = towers_here[t]
        if n + 1 < len(tiles):
            project(n + 1)
        for row in range(start, start + JOB_ROWS, STRIP):
            rows = slice(row, row + STRIP)
            here = (rows, slice(tile_column, tile_column + JOB_COLUMNS))
            token_columns = pl.ds(pl.multiple_of(first + tile_column, 128), JOB_COLUMNS)
            value, slant = gelu_and_slope(slope[here])
            slope[here] = slant
            hidden = buf[rows, token_columns].astype(F32) + value
            for part in range(0, STRIP, tok):
                sample = base + (row + part) // tok
                pooled_ref[sample : sample + 1, here[1]] = (
                    jnp.sum(hidden[part : part + tok], axis=0, keepdims=True) / tok
                )
        if tile_column + JOB_COLUMNS == width:
            part = pl.ds(start, JOB_ROWS)
            copy = pltpu.make_async_copy(
                slope.at[part, :], slope_out.at[part, :], out_sem.at[len(out_copies)]
            )
            copy.start()
            out_copies.append(copy)
    pooled = pooled_ref[...]
    total = jnp.sum(pooled * pooled, axis=1, keepdims=True)
    square_ref[...] = jnp.broadcast_to(total, square_ref.shape)
    for copy in out_copies:
        copy.wait()


def forward(place, image_flat, text_flat, image_w, text_w, samples):
    width = image_w.shape[1]
    depth = image_w.shape[0]
    rows_i, rows_t = image_flat.shape[0], text_flat.shape[0]
    jobs = (rows_i + rows_t) // JOB_ROWS
    return pl.pallas_call(
        functools.partial(forward_kernel, (rows_i // samples, rows_t // samples)),
        out_shape=(
            jax.ShapeDtypeStruct((2 * samples, width), F32),
            jax.ShapeDtypeStruct((2 * samples, 128), F32),
            jax.ShapeDtypeStruct((rows_i, width), F32),
            jax.ShapeDtypeStruct((rows_t, width), F32),
        ),
        in_specs=[smem()] + [hbm()] * 4,
        out_specs=(vmem(), vmem(), hbm(), hbm()),
        scratch_shapes=[
            pltpu.VMEM((rows_i, depth), BF16),
            pltpu.VMEM((rows_t, depth), BF16),
            pltpu.VMEM((depth, width), BF16),
            pltpu.VMEM((depth, width), BF16),
            pltpu.VMEM((rows_i, width), F32),
            pltpu.VMEM((rows_t, width), F32),
            pltpu.SemaphoreType.DMA((2,)),
            pltpu.SemaphoreType.DMA((2,)),
            pltpu.SemaphoreType.DMA((jobs,)),
        ],
        compiler_params=params(53),
        cost_estimate=pl.CostEstimate(
            flops=2 * (rows_i + rows_t) * depth * width,
            bytes_accessed=2 * (rows_i + rows_t) * (depth + 2 * width) + 4 * depth * width,
            transcendentals=(rows_i + rows_t) * width,
        ),
    )(place, image_flat, text_flat, image_w, text_w)


def unit_kernel(count_ref, pooled_ref, own_ref, other_ref, unit_ref, sent_ref, norm_ref):
    both = pooled_ref.shape[0]
    norm = jnp.sqrt(own_ref[...] + other_ref[...] + 1e-06)
    norm_ref[...] = norm
    unit = pooled_ref[...] / norm[:, :1]
    unit_ref[...] = unit
    row = lax.broadcasted_iota(jnp.int32, unit.shape, 0) % (both // 2)
    sent_ref[...] = jnp.where(row < count_ref[0], unit, UNUSABLE).astype(BF16)


def units(count, pooled, own, other):
    return pl.pallas_call(
        unit_kernel,
        out_shape=(
            jax.ShapeDtypeStruct(pooled.shape, F32),
            jax.ShapeDtypeStruct(pooled.shape, BF16),
            jax.ShapeDtypeStruct(own.shape, F32),
        ),
        in_specs=[smem()] + [pl.BlockSpec()] * 3,
        out_specs=(vmem(),) * 3,
        compiler_params=params(4),
    )(count, pooled, own, other)


def stack_kernel(afters, *refs):
    parts, out_ref = refs[afters:-1], refs[-1]
    for n, part in enumerate(parts):
        out_ref[n] = part[...]


def stack(parts, *afters):
    return pl.pallas_call(
        functools.partial(stack_kernel, len(afters)),
        out_shape=jax.ShapeDtypeStruct((len(parts), *parts[0].shape), parts[0].dtype),
        in_specs=[anyplace()] * len(afters) + [vmem()] * len(parts),
        out_specs=vmem(),
        compiler_params=params(4),
    )(*afters, *parts)


def turn_kernel(source_ref, tokens_ref, _, turned_ref, most_ref, turned):
    rows, _ = tokens_ref.shape
    blocks = source_ref.shape[0]
    height = turned_ref.shape[0] // blocks
    largest = None
    for start in range(0, rows, ROWS):
        tokens = tokens_ref[start : start + ROWS, :]
        turned[...] = tokens.T
        most = jnp.max(jnp.abs(tokens).astype(F32), axis=0, keepdims=True)
        largest = most if largest is None else jnp.maximum(largest, most)
        for q in range(blocks):
            source = pl.multiple_of(source_ref[q] * height, height)
            turned_ref[q * height : (q + 1) * height, start : start + ROWS] = turned[
                pl.ds(source, height), :
            ]
    most_ref[...] = jnp.broadcast_to(jnp.max(largest, axis=1, keepdims=True), most_ref.shape)


def turn(sources, flat, after):
    rows, depth = flat.shape
    blocks = sources.shape[0]
    odd = (depth // blocks) % 16
    picked = jnp.arange(16, dtype=jnp.int32) if odd else sources
    turned, most = pl.pallas_call(
        turn_kernel,
        out_shape=(
            jax.ShapeDtypeStruct((depth, rows), flat.dtype),
            jax.ShapeDtypeStruct((8, 128), F32),
        ),
        in_specs=[smem(), vmem(), anyplace()],
        out_specs=(vmem(), vmem()),
        scratch_shapes=[pltpu.VMEM((depth, ROWS), flat.dtype)],
        compiler_params=params(8),
        cost_estimate=pl.CostEstimate(
            flops=0, bytes_accessed=4 * rows * depth, transcendentals=0
        ),
    )(picked, flat, after)
    if odd:
        turned = turned.reshape(blocks, depth // blocks, rows)[sources].reshape(depth, rows)
    return turned, most


def row_products(left, right):
    return lax.dot_general(left, right, (((1,), (1,)), ((), ())), preferred_element_type=F32)


def towers(blocks_ref, samples):
    blocks, _, width = blocks_ref.shape
    image = blocks_ref[:, :samples, :].reshape(blocks * samples, width)
    text = blocks_ref[:, samples:, :].reshape(blocks * samples, width)
    return image, text


def product_kernel(image_most_ref, text_most_ref, *refs):
    *block_refs, out_ref, mark_ref = refs
    near_ref = block_refs[0]
    samples = near_ref.shape[1] // 2
    own_image = near_ref[0, :samples, :]
    own_text = near_ref[0, samples:, :]
    lane = lax.broadcasted_iota(jnp.int32, own_image.shape, 1)
    first = jnp.where(lane == 0, 1.0, 0.0).astype(BF16)
    start = 0
    for ref in block_refs:
        image, text = towers(ref, samples)
        stop = start + image.shape[0]
        found = row_products(jnp.concatenate([own_image, first], axis=0), text)
        out_ref[:samples, start:stop] = found[:samples]
        mark_ref[:, start:stop] = found[samples : samples + 8]
        out_ref[samples:, start:stop] = row_products(own_text, image)
        start = stop


def products(blocks, mosts):
    both = blocks[0].shape[1]
    columns = sum(b.shape[0] for b in blocks) * (both // 2)
    return pl.pallas_call(
        product_kernel,
        out_shape=(
            jax.ShapeDtypeStruct((both, columns), F32),
            jax.ShapeDtypeStruct((8, columns), F32),
        ),
        in_specs=[anyplace()] * 2 + [vmem()] * len(blocks),
        out_specs=(vmem(),) * 2,
        compiler_params=params(8),
    )(*mosts, *blocks)


def middle_kernel(
    tokens_of,
    scale_ref,
    bias_ref,
    gain_ref,
    count_ref,
    own_ref,
    other_ref,
    mark_ref,
    unit_ref,
    norm_ref,
    image_most_ref,
    text_most_ref,
    *refs,
):
    *block_refs, grad_ref, stat_ref = refs
    samples = unit_ref.shape[0] // 2
    scale, bias = scale_ref[0], bias_ref[0]
    dots = own_ref[...] + other_ref[...]
    logits = scale * dots + bias
    row = lax.broadcasted_iota(jnp.int32, dots.shape, 0) % samples
    column = lax.broadcasted_iota(jnp.int32, dots.shape, 1)
    sign = jnp.where(row == column, 1.0, -1.0).astype(F32)
    usable = jnp.where(mark_ref[:1, :] < 1.5, 1.0, 0.0)
    total = jnp.sum(usable, axis=1, keepdims=True)
    used = (usable > 0.5) & (row < count_ref[0])
    margin = -sign * logits
    small = jnp.exp(-jnp.abs(margin))
    soft = jnp.maximum(margin, 0.0) + jnp.log1p(small)
    sigmoid = jnp.where(margin >= 0, 1.0, small) / (1.0 + small)
    part = jnp.where(used, soft, 0.0)[:samples, :]
    loss = jnp.sum(jnp.sum(part, axis=1, keepdims=True), axis=0, keepdims=True) / total
    coeff = gain_ref[0] / total
    dlogit = (jnp.where(used, -sign * sigmoid, 0.0) * coeff).astype(BF16)
    radial = scale * jnp.sum(dlogit.astype(F32) * dots, axis=1, keepdims=True)
    raws = [jnp.zeros((samples, unit_ref.shape[1]), F32) for _ in range(2)]
    start = 0
    for ref in block_refs:
        image, text = towers(ref, samples)
        stop = start + image.shape[0]
        raws[0] += jnp.dot(dlogit[:samples, start:stop], text, preferred_element_type=F32)
        raws[1] += jnp.dot(dlogit[samples:, start:stop], image, preferred_element_type=F32)
        start = stop
    limits = []
    for n, most_ref in enumerate((image_most_ref, text_most_ref)):
        here = slice(n * samples, (n + 1) * samples)
        inward = unit_ref[here, :] * radial[here, :]
        grad = (scale * raws[n] - inward) / norm_ref[here, :1] / tokens_of[n]
        grad_ref[here, :] = grad
        steep = jnp.max(jnp.max(jnp.abs(grad), axis=1, keepdims=True), axis=0, keepdims=True)
        limits.append(1.2 * samples * tokens_of[n] * most_ref[:1, :1] * steep)
    line = lax.broadcasted_iota(jnp.int32, stat_ref.shape, 0)
    stat_ref[...] = jnp.where(line == 0, loss, jnp.where(line == 1, limits[0], limits[1]))


def middle(tokens_of, scale, bias, gain, count, own, other, mark, unit, norm, mosts, blocks):
    return pl.pallas_call(
        functools.partial(middle_kernel, tokens_of),
        out_shape=(
            jax.ShapeDtypeStruct(unit.shape, F32),
            jax.ShapeDtypeStruct((8, unit.shape[1]), F32),
        ),
        in_specs=[smem()] * 4 + [vmem()] * (7 + len(blocks)),
        out_specs=(vmem(), vmem()),
        compiler_params=params(12),
    )(scale, bias, gain, count, own, other, mark, unit, norm, *mosts, *blocks)


def weight_kernel(
    base, carries, grad_ref, slope_ref, turned_ref, stat_ref, _, soon_ref, late_ref, keep_ref, preact_grad
):
    rows, width = slope_ref.shape
    samples = grad_ref.shape[0] // 2
    tok = rows // samples
    for sample in range(samples):
        here = slice(sample * tok, (sample + 1) * tok)
        row = base * samples + sample
        for column in range(0, width, 128):
            columns = slice(column, column + 128)
            slope = slope_ref[here, columns]
            preact_grad[here, columns] = (grad_ref[row : row + 1, columns] * slope).astype(BF16)
    height = late_ref.shape[0]
    if carries:
        soon_ref[height:, :] = stat_ref[...]
    for n, (out, start) in enumerate(
        ((soon_ref, 0), (late_ref, 0), (keep_ref, 0), (keep_ref, height))
    ):
        out[start : start + height, :] = jnp.dot(
            turned_ref[n * height : (n + 1) * height, :],
            preact_grad[...],
            preferred_element_type=F32,
        )


def weight_terms(grad, slope, turned, stat, base, carries, after):
    depth, rows = turned.shape
    width = slope.shape[1]
    quarter = depth // 4
    soon = quarter + (stat.shape[0] if carries else 0)
    return pl.pallas_call(
        functools.partial(weight_kernel, base, carries),
        out_shape=tuple(jax.ShapeDtypeStruct((n, width), F32) for n in (soon, quarter, 2 * quarter)),
        in_specs=[vmem()] * 4 + [anyplace()],
        out_specs=(vmem(),) * 3,
        scratch_shapes=[pltpu.VMEM((rows, width), BF16)],
        compiler_params=params(8),
        cost_estimate=pl.CostEstimate(
            flops=2 * depth * rows * width,
            bytes_accessed=2 * depth * rows + 4 * rows * width + 4 * depth * width,
            transcendentals=0,
        ),
    )(grad, slope, turned, stat, after)


def sum_of(terms):
    total = None
    for term, unit in terms:
        value = term if unit is None else term.astype(F32) * unit
        total = value if total is None else total + value
    return total


def body(
    image_tokens,
    text_tokens,
    image_weight,
    text_weight,
    logit_scale,
    logit_bias,
    loss_scale,
    valid_count,
):
    samples, image_tok, depth = image_tokens.shape
    text_tok = text_tokens.shape[1]
    width = image_weight.shape[1]
    cycle = lax.axis_size("dp")
    bits = cycle.bit_length() - 1
    place = lax.axis_index("dp")

    def swap(array, mask):
        return lax.ppermute(array, "dp", [(i, i ^ mask) for i in range(cycle)])

    def swap_halves(array):
        return lax.ppermute(array, "mp", [(0, 1), (1, 0)])

    def bits_of(value, order):
        return sum(((value >> (len(order) - 1 - i)) & 1) << b for i, b in enumerate(order))

    image_flat = image_tokens.reshape(-1, depth)
    text_flat = text_tokens.reshape(-1, depth)
    text_orders = [list(range(2, bits)), list(range(3, bits)) + [2]]
    image_order = [2, 1] + list(range(3, bits))
    later = [(c, q) for c in range(2) for q in range(cycle // 4)]
    text_blocks = [
        2 * (high + bits_of(q, text_orders[c])) + c for high in (3, 1, 0, 2) for c, q in later
    ]
    image_blocks = [
        high + bits_of(q, image_order[1:])
        for high in (5, 1, 0, 4)
        for q in range(cycle // 4)
    ]
    text_blocks = jnp.asarray(text_blocks, jnp.int32) ^ (2 * place)
    image_blocks = jnp.asarray(image_blocks, jnp.int32) ^ place

    model_place = lax.axis_index("mp").astype(jnp.int32).reshape(1)
    pooled, square, image_slope, text_slope = forward(
        model_place, image_flat, text_flat, image_weight, text_weight, samples
    )
    unit, sent, norm = units(valid_count, pooled, square, swap_halves(square))

    low = max(bits - 2, 1)
    tops = [1 << b for b in reversed(range(low, bits))]
    masks = tops + [tops[0] | tops[1]] if len(tops) == 2 else tops
    arrived = [swap(sent, mask) for mask in masks]
    image_turned, image_most = turn(image_blocks, image_flat, sent)
    gathered = stack([sent] + arrived, image_most)
    text_turned, text_most = turn(text_blocks, text_flat, gathered)
    blocks = [gathered]
    for b in reversed(range(1, low)):
        blocks = blocks + [swap(block, 1 << b) for block in blocks]
    far = [swap(block, 1) for block in blocks[:1]]
    for block in blocks[1:]:
        far.append(swap(stack([block], text_most)[0], 1))
    blocks = blocks + far

    own_dots, mark = products(blocks, (image_most, text_most))
    grad, stat = middle(
        (image_tok, text_tok),
        logit_scale,
        logit_bias,
        loss_scale,
        valid_count,
        own_dots,
        swap_halves(own_dots),
        mark,
        unit,
        norm,
        (image_most, text_most),
        blocks,
    )

    lines = lax.broadcasted_iota(jnp.int32, (FOOT, width), 0)

    def footer(exponents, stat):
        rows = list(exponents)
        rest = stat[:1]
        for _ in range(3):
            part = lax.reduce_precision(rest, 5, 10)
            rows.append(part)
            rest = (rest - part) * 2048.0
        found = jnp.zeros((FOOT, width), F32)
        for n, row in enumerate(rows):
            found = jnp.where(lines == n, row, found)
        return found

    def exponents_of(stat):
        return [jnp.ceil(jnp.log2(jnp.maximum(stat[n : n + 1], 1e-30))) for n in (1, 2)]

    def merged(stat, message):
        foot = message[-FOOT:].astype(F32)
        loss = (foot[4:5] / 2048.0 + foot[3:4]) / 2048.0 + foot[2:3]
        there = [foot[:1], foot[1:2]]
        add = [loss, jnp.exp2(there[0]), jnp.exp2(there[1])]
        total = [stat[n : n + 1] + row for n, row in enumerate(add)]
        return jnp.concatenate(total), there

    def halves(terms):
        half = terms[0][0].shape[0] // 2
        return [[(term[rows], unit) for term, unit in terms] for rows in (slice(half), slice(half, None))]

    def leave(terms, stat, tower, bit, after):
        rows = terms[0][0].shape[0]
        exponents = exponents_of(stat)
        factor = HALF_MAX * jnp.exp2(-exponents[tower]) + 0.0 * after[:1].astype(F32)
        coded = sum_of(terms) * factor
        foot = footer(exponents, stat) + 0.0 * coded[:1]
        coded = jnp.pad(coded, ((0, FOOT), (0, 0))) + jnp.pad(foot, ((rows, 0), (0, 0)))
        coded = coded.astype(jnp.float16)
        return coded, swap(coded, 1 << bit)

    def take(terms, stat, tower, coming):
        stat, there = merged(stat, coming)
        return terms + [(coming[:-FOOT], jnp.exp2(there[tower]) / HALF_MAX)], stat

    def core_step(soon, late, keep):
        height = late.shape[0]
        there = swap(soon, 1)
        stays = [(keep[:height], None), (swap(late, 1), None)]
        return stays, [(keep[height:], None), (there[:height], None)], there[height:]

    text_terms = weight_terms(grad, text_slope, text_turned, stat, 1, True, stat)
    text, text_leaves, stat_there = core_step(*text_terms)
    start_stat = stat[:3] + stat_there[:3]
    image_terms = weight_terms(grad, image_slope, image_turned, stat, 0, False, text_terms[0])
    image, image_leaves, _ = core_step(*image_terms)

    coded, text_in = leave(text_leaves, start_stat, 1, 1, start_stat)
    coded, image_in = leave(image_leaves, start_stat, 0, image_order[0], coded)
    text, text_stat = take(text, start_stat, 1, text_in)
    parts = [(terms, text_stat) for terms in halves(text)]
    image, image_stat = take(image, start_stat, 0, image_in)
    for step in range(bits - 2):
        image, image_leaves = halves(image)
        arrivals, before = [], coded
        for order, (terms, terms_stat) in zip(text_orders, parts):
            terms, leaves = halves(terms)
            last, arrival = leave(leaves, terms_stat, 1, order[step], before)
            before = last if step == 0 else before
            arrivals.append((terms, terms_stat, arrival))
        coded, image_in = leave(image_leaves, image_stat, 0, image_order[step + 1], before)
        parts = [take(terms, old, 1, arrival) for terms, old, arrival in arrivals]
        image, image_stat = take(image, image_stat, 0, image_in)
    row = 0.0 * coded[:1].astype(F32)
    text = jnp.concatenate([sum_of(terms) + row for terms, _ in parts])
    loss = jnp.max(parts[0][1][:1] + row)
    return (loss, sum_of(image), text)


def solution(mesh):
    placed = (
        P("dp", None, None),
        P("dp", None, None),
        P(None, "mp"),
        P(None, "mp"),
        P(),
        P(),
        P(),
        P("dp"),
    )
    return jax.shard_map(
        body,
        mesh=mesh,
        in_specs=placed,
        out_specs=(P(), P("dp", "mp"), P("dp", "mp")),
        check_vma=False,
    )
```

```python
import functools

import jax
import jax.numpy as jnp
from jax import lax
from jax.experimental import pallas as pl
from jax.experimental.pallas import tpu as pltpu
from jax.sharding import PartitionSpec as P

F32 = jnp.float32
BF16 = jnp.bfloat16
ROWS = 256
JOB_ROWS = 256
JOB_COLUMNS = 256
STRIP = 64
ROOT = 0.7978845608028654
HALF_MAX = 16384.0
FOOT = 8
UNUSABLE = 2.0


def vmem():
    return pl.BlockSpec(memory_space=pltpu.VMEM)


def smem():
    return pl.BlockSpec(memory_space=pltpu.SMEM)


def anyplace():
    return pl.BlockSpec(memory_space=pl.ANY)


def hbm():
    return pl.BlockSpec(memory_space=pltpu.HBM)


def params(mib):
    return pltpu.CompilerParams(vmem_limit_bytes=mib * 2**20)


def gelu_and_slope(x):
    square = x * x
    cdf = 0.5 + 0.5 * jnp.tanh(x * (ROOT + (0.044715 * ROOT) * square))
    value = x * cdf
    rise = (value - value * cdf) * (2 * ROOT + (6 * 0.044715 * ROOT) * square)
    return value, cdf + rise


def forward_kernel(
    tokens_of,
    place_ref,
    image_hbm,
    text_hbm,
    image_w_hbm,
    text_w_hbm,
    pooled_ref,
    square_ref,
    image_slope_hbm,
    text_slope_hbm,
    image_v,
    text_v,
    image_w,
    text_w,
    image_slope,
    text_slope,
    in_sem,
    w_sem,
    out_sem,
):
    width = image_w.shape[1]
    samples = pooled_ref.shape[0] // 2
    towers_here = (
        (text_hbm, text_v, text_w_hbm, text_w, text_slope, text_slope_hbm, tokens_of[1], samples),
        (image_hbm, image_v, image_w_hbm, image_w, image_slope, image_slope_hbm, tokens_of[0], 0),
    )
    waits, tiles = [], []
    for t, (source, buf, w_source, w, _, _, _, _) in enumerate(towers_here):
        here = [
            pltpu.make_async_copy(w_source, w, w_sem.at[t]),
            pltpu.make_async_copy(source, buf, in_sem.at[t]),
        ]
        for copy in here:
            copy.start()
        waits.append(here)
        for start in range(0, buf.shape[0], JOB_ROWS):
            for column in range(0, width, JOB_COLUMNS):
                tiles.append((t, start, column))
    first = place_ref[0] * width

    def project(n):
        t, start, column = tiles[n]
        _, buf, _, w, slope, _, _, _ = towers_here[t]
        if start == 0 and column == 0:
            for copy in waits[t]:
                copy.wait()
        rows, columns = slice(start, start + JOB_ROWS), slice(column, column + JOB_COLUMNS)
        slope[rows, columns] = jnp.dot(buf[rows, :], w[:, columns], preferred_element_type=F32)

    out_copies = []
    project(0)
    for n, (t, start, tile_column) in enumerate(tiles):
        _, buf, _, _, slope, slope_out, tok, base = towers_here[t]
        if n + 1 < len(tiles):
            project(n + 1)
        for row in range(start, start + JOB_ROWS, STRIP):
            rows = slice(row, row + STRIP)
            here = (rows, slice(tile_column, tile_column + JOB_COLUMNS))
            token_columns = pl.ds(pl.multiple_of(first + tile_column, 128), JOB_COLUMNS)
            value, slant = gelu_and_slope(slope[here])
            slope[here] = slant
            hidden = buf[rows, token_columns].astype(F32) + value
            for part in range(0, STRIP, tok):
                sample = base + (row + part) // tok
                pooled_ref[sample : sample + 1, here[1]] = (
                    jnp.sum(hidden[part : part + tok], axis=0, keepdims=True) / tok
                )
        if tile_column + JOB_COLUMNS == width:
            part = pl.ds(start, JOB_ROWS)
            copy = pltpu.make_async_copy(
                slope.at[part, :], slope_out.at[part, :], out_sem.at[len(out_copies)]
            )
            copy.start()
            out_copies.append(copy)
    pooled = pooled_ref[...]
    total = jnp.sum(pooled * pooled, axis=1, keepdims=True)
    square_ref[...] = jnp.broadcast_to(total, square_ref.shape)
    for copy in out_copies:
        copy.wait()


def forward(place, image_flat, text_flat, image_w, text_w, samples):
    width = image_w.shape[1]
    depth = image_w.shape[0]
    rows_i, rows_t = image_flat.shape[0], text_flat.shape[0]
    jobs = (rows_i + rows_t) // JOB_ROWS
    return pl.pallas_call(
        functools.partial(forward_kernel, (rows_i // samples, rows_t // samples)),
        out_shape=(
            jax.ShapeDtypeStruct((2 * samples, width), F32),
            jax.ShapeDtypeStruct((2 * samples, 128), F32),
            jax.ShapeDtypeStruct((rows_i, width), F32),
            jax.ShapeDtypeStruct((rows_t, width), F32),
        ),
        in_specs=[smem()] + [hbm()] * 4,
        out_specs=(vmem(), vmem(), hbm(), hbm()),
        scratch_shapes=[
            pltpu.VMEM((rows_i, depth), BF16),
            pltpu.VMEM((rows_t, depth), BF16),
            pltpu.VMEM((depth, width), BF16),
            pltpu.VMEM((depth, width), BF16),
            pltpu.VMEM((rows_i, width), F32),
            pltpu.VMEM((rows_t, width), F32),
            pltpu.SemaphoreType.DMA((2,)),
            pltpu.SemaphoreType.DMA((2,)),
            pltpu.SemaphoreType.DMA((jobs,)),
        ],
        compiler_params=params(53),
        cost_estimate=pl.CostEstimate(
            flops=2 * (rows_i + rows_t) * depth * width,
            bytes_accessed=2 * (rows_i + rows_t) * (depth + 2 * width) + 4 * depth * width,
            transcendentals=(rows_i + rows_t) * width,
        ),
    )(place, image_flat, text_flat, image_w, text_w)


def unit_kernel(count_ref, pooled_ref, own_ref, other_ref, unit_ref, sent_ref, norm_ref):
    both = pooled_ref.shape[0]
    norm = jnp.sqrt(own_ref[...] + other_ref[...] + 1e-06)
    norm_ref[...] = norm
    unit = pooled_ref[...] / norm[:, :1]
    unit_ref[...] = unit
    row = lax.broadcasted_iota(jnp.int32, unit.shape, 0) % (both // 2)
    sent_ref[...] = jnp.where(row < count_ref[0], unit, UNUSABLE).astype(BF16)


def units(count, pooled, own, other):
    return pl.pallas_call(
        unit_kernel,
        out_shape=(
            jax.ShapeDtypeStruct(pooled.shape, F32),
            jax.ShapeDtypeStruct(pooled.shape, BF16),
            jax.ShapeDtypeStruct(own.shape, F32),
        ),
        in_specs=[smem()] + [pl.BlockSpec()] * 3,
        out_specs=(vmem(),) * 3,
        compiler_params=params(4),
    )(count, pooled, own, other)


def stack_kernel(afters, *refs):
    parts, out_ref = refs[afters:-1], refs[-1]
    for n, part in enumerate(parts):
        out_ref[n] = part[...]


def stack(parts, *afters):
    return pl.pallas_call(
        functools.partial(stack_kernel, len(afters)),
        out_shape=jax.ShapeDtypeStruct((len(parts), *parts[0].shape), parts[0].dtype),
        in_specs=[anyplace()] * len(afters) + [vmem()] * len(parts),
        out_specs=vmem(),
        compiler_params=params(4),
    )(*afters, *parts)


def turn_kernel(source_ref, tokens_ref, _, turned_ref, most_ref, turned):
    rows, _ = tokens_ref.shape
    blocks = source_ref.shape[0]
    height = turned_ref.shape[0] // blocks
    largest = None
    for start in range(0, rows, ROWS):
        tokens = tokens_ref[start : start + ROWS, :]
        turned[...] = tokens.T
        most = jnp.max(jnp.abs(tokens).astype(F32), axis=0, keepdims=True)
        largest = most if largest is None else jnp.maximum(largest, most)
        for q in range(blocks):
            source = pl.multiple_of(source_ref[q] * height, height)
            turned_ref[q * height : (q + 1) * height, start : start + ROWS] = turned[
                pl.ds(source, height), :
            ]
    most_ref[...] = jnp.broadcast_to(jnp.max(largest, axis=1, keepdims=True), most_ref.shape)


def turn(sources, flat, after):
    rows, depth = flat.shape
    blocks = sources.shape[0]
    odd = (depth // blocks) % 16
    picked = jnp.arange(16, dtype=jnp.int32) if odd else sources
    turned, most = pl.pallas_call(
        turn_kernel,
        out_shape=(
            jax.ShapeDtypeStruct((depth, rows), flat.dtype),
            jax.ShapeDtypeStruct((8, 128), F32),
        ),
        in_specs=[smem(), vmem(), anyplace()],
        out_specs=(vmem(), vmem()),
        scratch_shapes=[pltpu.VMEM((depth, ROWS), flat.dtype)],
        compiler_params=params(8),
        cost_estimate=pl.CostEstimate(
            flops=0, bytes_accessed=4 * rows * depth, transcendentals=0
        ),
    )(picked, flat, after)
    if odd:
        turned = turned.reshape(blocks, depth // blocks, rows)[sources].reshape(depth, rows)
    return turned, most


def row_products(left, right):
    return lax.dot_general(left, right, (((1,), (1,)), ((), ())), preferred_element_type=F32)


def towers(blocks_ref, samples):
    blocks, _, width = blocks_ref.shape
    image = blocks_ref[:, :samples, :].reshape(blocks * samples, width)
    text = blocks_ref[:, samples:, :].reshape(blocks * samples, width)
    return image, text


def product_kernel(image_most_ref, text_most_ref, *refs):
    *block_refs, out_ref, mark_ref = refs
    near_ref = block_refs[0]
    samples = near_ref.shape[1] // 2
    own_image = near_ref[0, :samples, :]
    own_text = near_ref[0, samples:, :]
    lane = lax.broadcasted_iota(jnp.int32, own_image.shape, 1)
    first = jnp.where(lane == 0, 1.0, 0.0).astype(BF16)
    start = 0
    for ref in block_refs:
        image, text = towers(ref, samples)
        stop = start + image.shape[0]
        found = row_products(jnp.concatenate([own_image, first], axis=0), text)
        out_ref[:samples, start:stop] = found[:samples]
        mark_ref[:, start:stop] = found[samples : samples + 8]
        out_ref[samples:, start:stop] = row_products(own_text, image)
        start = stop


def products(blocks, mosts):
    both = blocks[0].shape[1]
    columns = sum(b.shape[0] for b in blocks) * (both // 2)
    return pl.pallas_call(
        product_kernel,
        out_shape=(
            jax.ShapeDtypeStruct((both, columns), F32),
            jax.ShapeDtypeStruct((8, columns), F32),
        ),
        in_specs=[anyplace()] * 2 + [vmem()] * len(blocks),
        out_specs=(vmem(),) * 2,
        compiler_params=params(8),
    )(*mosts, *blocks)


def middle_kernel(
    tokens_of,
    scale_ref,
    bias_ref,
    gain_ref,
    count_ref,
    own_ref,
    other_ref,
    mark_ref,
    unit_ref,
    norm_ref,
    image_most_ref,
    text_most_ref,
    *refs,
):
    *block_refs, grad_ref, stat_ref = refs
    samples = unit_ref.shape[0] // 2
    scale, bias = scale_ref[0], bias_ref[0]
    dots = own_ref[...] + other_ref[...]
    logits = scale * dots + bias
    row = lax.broadcasted_iota(jnp.int32, dots.shape, 0) % samples
    column = lax.broadcasted_iota(jnp.int32, dots.shape, 1)
    sign = jnp.where(row == column, 1.0, -1.0).astype(F32)
    usable = jnp.where(mark_ref[:1, :] < 1.5, 1.0, 0.0)
    total = jnp.sum(usable, axis=1, keepdims=True)
    used = (usable > 0.5) & (row < count_ref[0])
    margin = -sign * logits
    small = jnp.exp(-jnp.abs(margin))
    soft = jnp.maximum(margin, 0.0) + jnp.log1p(small)
    sigmoid = jnp.where(margin >= 0, 1.0, small) / (1.0 + small)
    part = jnp.where(used, soft, 0.0)[:samples, :]
    loss = jnp.sum(jnp.sum(part, axis=1, keepdims=True), axis=0, keepdims=True) / total
    coeff = gain_ref[0] / total
    dlogit = (jnp.where(used, -sign * sigmoid, 0.0) * coeff).astype(BF16)
    radial = scale * jnp.sum(dlogit.astype(F32) * dots, axis=1, keepdims=True)
    raws = [jnp.zeros((samples, unit_ref.shape[1]), F32) for _ in range(2)]
    start = 0
    for ref in block_refs:
        image, text = towers(ref, samples)
        stop = start + image.shape[0]
        raws[0] += jnp.dot(dlogit[:samples, start:stop], text, preferred_element_type=F32)
        raws[1] += jnp.dot(dlogit[samples:, start:stop], image, preferred_element_type=F32)
        start = stop
    limits = []
    for n, most_ref in enumerate((image_most_ref, text_most_ref)):
        here = slice(n * samples, (n + 1) * samples)
        inward = unit_ref[here, :] * radial[here, :]
        grad = (scale * raws[n] - inward) / norm_ref[here, :1] / tokens_of[n]
        grad_ref[here, :] = grad
        steep = jnp.max(jnp.max(jnp.abs(grad), axis=1, keepdims=True), axis=0, keepdims=True)
        limits.append(1.2 * samples * tokens_of[n] * most_ref[:1, :1] * steep)
    line = lax.broadcasted_iota(jnp.int32, stat_ref.shape, 0)
    stat_ref[...] = jnp.where(line == 0, loss, jnp.where(line == 1, limits[0], limits[1]))


def middle(tokens_of, scale, bias, gain, count, own, other, mark, unit, norm, mosts, blocks):
    return pl.pallas_call(
        functools.partial(middle_kernel, tokens_of),
        out_shape=(
            jax.ShapeDtypeStruct(unit.shape, F32),
            jax.ShapeDtypeStruct((8, unit.shape[1]), F32),
        ),
        in_specs=[smem()] * 4 + [vmem()] * (7 + len(blocks)),
        out_specs=(vmem(), vmem()),
        compiler_params=params(12),
    )(scale, bias, gain, count, own, other, mark, unit, norm, *mosts, *blocks)


def weight_kernel(
    base, carries, grad_ref, slope_ref, turned_ref, stat_ref, _, soon_ref, late_ref, keep_ref, preact_grad
):
    rows, width = slope_ref.shape
    samples = grad_ref.shape[0] // 2
    tok = rows // samples
    for sample in range(samples):
        here = slice(sample * tok, (sample + 1) * tok)
        row = base * samples + sample
        for column in range(0, width, 128):
            columns = slice(column, column + 128)
            slope = slope_ref[here, columns]
            preact_grad[here, columns] = (grad_ref[row : row + 1, columns] * slope).astype(BF16)
    height = late_ref.shape[0]
    if carries:
        soon_ref[height:, :] = stat_ref[...]
    for n, (out, start) in enumerate(
        ((soon_ref, 0), (late_ref, 0), (keep_ref, 0), (keep_ref, height))
    ):
        out[start : start + height, :] = jnp.dot(
            turned_ref[n * height : (n + 1) * height, :],
            preact_grad[...],
            preferred_element_type=F32,
        )


def weight_terms(grad, slope, turned, stat, base, carries, after):
    depth, rows = turned.shape
    width = slope.shape[1]
    quarter = depth // 4
    soon = quarter + (stat.shape[0] if carries else 0)
    return pl.pallas_call(
        functools.partial(weight_kernel, base, carries),
        out_shape=tuple(jax.ShapeDtypeStruct((n, width), F32) for n in (soon, quarter, 2 * quarter)),
        in_specs=[vmem()] * 4 + [anyplace()],
        out_specs=(vmem(),) * 3,
        scratch_shapes=[pltpu.VMEM((rows, width), BF16)],
        compiler_params=params(8),
        cost_estimate=pl.CostEstimate(
            flops=2 * depth * rows * width,
            bytes_accessed=2 * depth * rows + 4 * rows * width + 4 * depth * width,
            transcendentals=0,
        ),
    )(grad, slope, turned, stat, after)


def sum_of(terms):
    total = None
    for term, unit in terms:
        value = term if unit is None else term.astype(F32) * unit
        total = value if total is None else total + value
    return total


def body(
    image_tokens,
    text_tokens,
    image_weight,
    text_weight,
    logit_scale,
    logit_bias,
    loss_scale,
    valid_count,
):
    samples, image_tok, depth = image_tokens.shape
    text_tok = text_tokens.shape[1]
    width = image_weight.shape[1]
    cycle = lax.axis_size("dp")
    bits = cycle.bit_length() - 1
    place = lax.axis_index("dp")

    def swap(array, mask):
        return lax.ppermute(array, "dp", [(i, i ^ mask) for i in range(cycle)])

    def swap_halves(array):
        return lax.ppermute(array, "mp", [(0, 1), (1, 0)])

    def bits_of(value, order):
        return sum(((value >> (len(order) - 1 - i)) & 1) << b for i, b in enumerate(order))

    image_flat = image_tokens.reshape(-1, depth)
    text_flat = text_tokens.reshape(-1, depth)
    text_orders = [list(range(2, bits)), list(range(3, bits)) + [2]]
    image_order = [2, 1] + list(range(3, bits))
    later = [(c, q) for c in range(2) for q in range(cycle // 4)]
    text_blocks = [
        2 * (high + bits_of(q, text_orders[c])) + c for high in (3, 1, 0, 2) for c, q in later
    ]
    image_blocks = [
        high + bits_of(q, image_order[1:])
        for high in (5, 1, 0, 4)
        for q in range(cycle // 4)
    ]
    text_blocks = jnp.asarray(text_blocks, jnp.int32) ^ (2 * place)
    image_blocks = jnp.asarray(image_blocks, jnp.int32) ^ place

    model_place = lax.axis_index("mp").astype(jnp.int32).reshape(1)
    pooled, square, image_slope, text_slope = forward(
        model_place, image_flat, text_flat, image_weight, text_weight, samples
    )
    unit, sent, norm = units(valid_count, pooled, square, swap_halves(square))

    low = max(bits - 2, 1)
    tops = [1 << b for b in reversed(range(low, bits))]
    masks = [tops[0] | tops[1], *tops] if len(tops) == 2 else tops
    arrived = [swap(sent, mask) for mask in masks]
    image_turned, image_most = turn(image_blocks, image_flat, sent)
    gathered = stack([sent] + arrived, image_most)
    text_turned, text_most = turn(text_blocks, text_flat, gathered)
    blocks = [gathered]
    for b in reversed(range(1, low)):
        blocks = blocks + [swap(block, 1 << b) for block in blocks]
    far = [swap(block, 1) for block in blocks[:1]]
    for block in blocks[1:]:
        far.append(swap(stack([block], text_most)[0], 1))
    blocks = blocks + far

    own_dots, mark = products(blocks, (image_most, text_most))
    grad, stat = middle(
        (image_tok, text_tok),
        logit_scale,
        logit_bias,
        loss_scale,
        valid_count,
        own_dots,
        swap_halves(own_dots),
        mark,
        unit,
        norm,
        (image_most, text_most),
        blocks,
    )

    lines = lax.broadcasted_iota(jnp.int32, (FOOT, width), 0)

    def footer(exponents, stat):
        rows = list(exponents)
        rest = stat[:1]
        for _ in range(3):
            part = lax.reduce_precision(rest, 5, 10)
            rows.append(part)
            rest = (rest - part) * 2048.0
        found = jnp.zeros((FOOT, width), F32)
        for n, row in enumerate(rows):
            found = jnp.where(lines == n, row, found)
        return found

    def exponents_of(stat):
        return [jnp.ceil(jnp.log2(jnp.maximum(stat[n : n + 1], 1e-30))) for n in (1, 2)]

    def merged(stat, message):
        foot = message[-FOOT:].astype(F32)
        loss = (foot[4:5] / 2048.0 + foot[3:4]) / 2048.0 + foot[2:3]
        there = [foot[:1], foot[1:2]]
        add = [loss, jnp.exp2(there[0]), jnp.exp2(there[1])]
        total = [stat[n : n + 1] + row for n, row in enumerate(add)]
        return jnp.concatenate(total), there

    def halves(terms):
        half = terms[0][0].shape[0] // 2
        return [[(term[rows], unit) for term, unit in terms] for rows in (slice(half), slice(half, None))]

    def leave(terms, stat, tower, bit, after):
        rows = terms[0][0].shape[0]
        exponents = exponents_of(stat)
        factor = HALF_MAX * jnp.exp2(-exponents[tower]) + 0.0 * after[:1].astype(F32)
        coded = sum_of(terms) * factor
        foot = footer(exponents, stat) + 0.0 * coded[:1]
        coded = jnp.pad(coded, ((0, FOOT), (0, 0))) + jnp.pad(foot, ((rows, 0), (0, 0)))
        coded = coded.astype(jnp.float16)
        return coded, swap(coded, 1 << bit)

    def take(terms, stat, tower, coming):
        stat, there = merged(stat, coming)
        return terms + [(coming[:-FOOT], jnp.exp2(there[tower]) / HALF_MAX)], stat

    def core_step(soon, late, keep):
        height = late.shape[0]
        there = swap(soon, 1)
        stays = [(keep[:height], None), (swap(late, 1), None)]
        return stays, [(keep[height:], None), (there[:height], None)], there[height:]

    image_terms = weight_terms(grad, image_slope, image_turned, stat, 0, True, stat)
    image, image_leaves, stat_there = core_step(*image_terms)
    start_stat = stat[:3] + stat_there[:3]
    text_terms = weight_terms(grad, text_slope, text_turned, stat, 1, False, image_terms[0])
    text, text_leaves, _ = core_step(*text_terms)

    coded, image_in = leave(image_leaves, start_stat, 0, image_order[0], start_stat)
    coded, text_in = leave(text_leaves, start_stat, 1, 1, coded)
    text, text_stat = take(text, start_stat, 1, text_in)
    parts = [(terms, text_stat) for terms in halves(text)]
    image, image_stat = take(image, start_stat, 0, image_in)
    for step in range(bits - 2):
        image, image_leaves = halves(image)
        arrivals, before = [], coded
        coded, image_in = leave(image_leaves, image_stat, 0, image_order[step + 1], before)
        for order, (terms, terms_stat) in zip(text_orders, parts):
            terms, leaves = halves(terms)
            last, arrival = leave(leaves, terms_stat, 1, order[step], coded if step == 0 else before)
            arrivals.append((terms, terms_stat, arrival))
        parts = [take(terms, old, 1, arrival) for terms, old, arrival in arrivals]
        image, image_stat = take(image, image_stat, 0, image_in)
    row = 0.0 * coded[:1].astype(F32)
    text = jnp.concatenate([sum_of(terms) + row for terms, _ in parts])
    loss = jnp.max(parts[0][1][:1] + row)
    return (loss, sum_of(image), text)


def solution(mesh):
    placed = (
        P("dp", None, None),
        P("dp", None, None),
        P(None, "mp"),
        P(None, "mp"),
        P(),
        P(),
        P(),
        P("dp"),
    )
    return jax.shard_map(
        body,
        mesh=mesh,
        in_specs=placed,
        out_specs=(P(), P("dp", "mp"), P("dp", "mp")),
        check_vma=False,
    )
```

```python
import functools

import jax
import jax.numpy as jnp
from jax import lax
from jax.experimental import pallas as pl
from jax.experimental.pallas import tpu as pltpu
from jax.sharding import PartitionSpec as P

F32 = jnp.float32
BF16 = jnp.bfloat16
ROWS = 256
JOB_ROWS = 256
JOB_COLUMNS = 256
STRIP = 64
ROOT = 0.7978845608028654
HALF_MAX = 16384.0
FOOT = 8
UNUSABLE = 2.0


def vmem():
    return pl.BlockSpec(memory_space=pltpu.VMEM)


def smem():
    return pl.BlockSpec(memory_space=pltpu.SMEM)


def anyplace():
    return pl.BlockSpec(memory_space=pl.ANY)


def hbm():
    return pl.BlockSpec(memory_space=pltpu.HBM)


def params(mib):
    return pltpu.CompilerParams(vmem_limit_bytes=mib * 2**20)


def gelu_and_slope(x):
    square = x * x
    cdf = 0.5 + 0.5 * jnp.tanh(x * (ROOT + (0.044715 * ROOT) * square))
    value = x * cdf
    rise = (value - value * cdf) * (2 * ROOT + (6 * 0.044715 * ROOT) * square)
    return value, cdf + rise


def forward_kernel(
    tokens_of,
    place_ref,
    image_hbm,
    text_hbm,
    image_w_hbm,
    text_w_hbm,
    pooled_ref,
    square_ref,
    image_slope_hbm,
    text_slope_hbm,
    image_v,
    text_v,
    image_w,
    text_w,
    image_slope,
    text_slope,
    in_sem,
    w_sem,
    out_sem,
):
    width = image_w.shape[1]
    samples = pooled_ref.shape[0] // 2
    towers_here = (
        (text_hbm, text_v, text_w_hbm, text_w, text_slope, text_slope_hbm, tokens_of[1], samples),
        (image_hbm, image_v, image_w_hbm, image_w, image_slope, image_slope_hbm, tokens_of[0], 0),
    )
    waits, tiles = [], []
    for t, (source, buf, w_source, w, _, _, _, _) in enumerate(towers_here):
        here = [
            pltpu.make_async_copy(w_source, w, w_sem.at[t]),
            pltpu.make_async_copy(source, buf, in_sem.at[t]),
        ]
        for copy in here:
            copy.start()
        waits.append(here)
        for start in range(0, buf.shape[0], JOB_ROWS):
            for column in range(0, width, JOB_COLUMNS):
                tiles.append((t, start, column))
    first = place_ref[0] * width

    def project(n):
        t, start, column = tiles[n]
        _, buf, _, w, slope, _, _, _ = towers_here[t]
        if start == 0 and column == 0:
            for copy in waits[t]:
                copy.wait()
        rows, columns = slice(start, start + JOB_ROWS), slice(column, column + JOB_COLUMNS)
        slope[rows, columns] = jnp.dot(buf[rows, :], w[:, columns], preferred_element_type=F32)

    out_copies = []
    project(0)
    for n, (t, start, tile_column) in enumerate(tiles):
        _, buf, _, _, slope, slope_out, tok, base = towers_here[t]
        if n + 1 < len(tiles):
            project(n + 1)
        for row in range(start, start + JOB_ROWS, STRIP):
            rows = slice(row, row + STRIP)
            here = (rows, slice(tile_column, tile_column + JOB_COLUMNS))
            token_columns = pl.ds(pl.multiple_of(first + tile_column, 128), JOB_COLUMNS)
            value, slant = gelu_and_slope(slope[here])
            slope[here] = slant
            hidden = buf[rows, token_columns].astype(F32) + value
            for part in range(0, STRIP, tok):
                sample = base + (row + part) // tok
                pooled_ref[sample : sample + 1, here[1]] = (
                    jnp.sum(hidden[part : part + tok], axis=0, keepdims=True) / tok
                )
        if tile_column + JOB_COLUMNS == width:
            part = pl.ds(start, JOB_ROWS)
            copy = pltpu.make_async_copy(
                slope.at[part, :], slope_out.at[part, :], out_sem.at[len(out_copies)]
            )
            copy.start()
            out_copies.append(copy)
    pooled = pooled_ref[...]
    total = jnp.sum(pooled * pooled, axis=1, keepdims=True)
    square_ref[...] = jnp.broadcast_to(total, square_ref.shape)
    for copy in out_copies:
        copy.wait()


def forward(place, image_flat, text_flat, image_w, text_w, samples):
    width = image_w.shape[1]
    depth = image_w.shape[0]
    rows_i, rows_t = image_flat.shape[0], text_flat.shape[0]
    jobs = (rows_i + rows_t) // JOB_ROWS
    return pl.pallas_call(
        functools.partial(forward_kernel, (rows_i // samples, rows_t // samples)),
        out_shape=(
            jax.ShapeDtypeStruct((2 * samples, width), F32),
            jax.ShapeDtypeStruct((2 * samples, 128), F32),
            jax.ShapeDtypeStruct((rows_i, width), F32),
            jax.ShapeDtypeStruct((rows_t, width), F32),
        ),
        in_specs=[smem()] + [hbm()] * 4,
        out_specs=(vmem(), vmem(), hbm(), hbm()),
        scratch_shapes=[
            pltpu.VMEM((rows_i, depth), BF16),
            pltpu.VMEM((rows_t, depth), BF16),
            pltpu.VMEM((depth, width), BF16),
            pltpu.VMEM((depth, width), BF16),
            pltpu.VMEM((rows_i, width), F32),
            pltpu.VMEM((rows_t, width), F32),
            pltpu.SemaphoreType.DMA((2,)),
            pltpu.SemaphoreType.DMA((2,)),
            pltpu.SemaphoreType.DMA((jobs,)),
        ],
        compiler_params=params(53),
        cost_estimate=pl.CostEstimate(
            flops=2 * (rows_i + rows_t) * depth * width,
            bytes_accessed=2 * (rows_i + rows_t) * (depth + 2 * width) + 4 * depth * width,
            transcendentals=(rows_i + rows_t) * width,
        ),
    )(place, image_flat, text_flat, image_w, text_w)


def unit_kernel(count_ref, pooled_ref, own_ref, other_ref, unit_ref, sent_ref, norm_ref):
    both = pooled_ref.shape[0]
    norm = jnp.sqrt(own_ref[...] + other_ref[...] + 1e-06)
    norm_ref[...] = norm
    unit = pooled_ref[...] / norm[:, :1]
    unit_ref[...] = unit
    row = lax.broadcasted_iota(jnp.int32, unit.shape, 0) % (both // 2)
    sent_ref[...] = jnp.where(row < count_ref[0], unit, UNUSABLE).astype(BF16)


def units(count, pooled, own, other):
    return pl.pallas_call(
        unit_kernel,
        out_shape=(
            jax.ShapeDtypeStruct(pooled.shape, F32),
            jax.ShapeDtypeStruct(pooled.shape, BF16),
            jax.ShapeDtypeStruct(own.shape, F32),
        ),
        in_specs=[smem()] + [pl.BlockSpec()] * 3,
        out_specs=(vmem(),) * 3,
        compiler_params=params(4),
    )(count, pooled, own, other)


def stack_kernel(afters, *refs):
    parts, out_ref = refs[afters:-1], refs[-1]
    for n, part in enumerate(parts):
        out_ref[n] = part[...]


def stack(parts, *afters):
    return pl.pallas_call(
        functools.partial(stack_kernel, len(afters)),
        out_shape=jax.ShapeDtypeStruct((len(parts), *parts[0].shape), parts[0].dtype),
        in_specs=[anyplace()] * len(afters) + [vmem()] * len(parts),
        out_specs=vmem(),
        compiler_params=params(4),
    )(*afters, *parts)


def turn_kernel(source_ref, tokens_ref, _, turned_ref, most_ref, turned):
    rows, _ = tokens_ref.shape
    blocks = source_ref.shape[0]
    height = turned_ref.shape[0] // blocks
    largest = None
    for start in range(0, rows, ROWS):
        tokens = tokens_ref[start : start + ROWS, :]
        turned[...] = tokens.T
        most = jnp.max(jnp.abs(tokens).astype(F32), axis=0, keepdims=True)
        largest = most if largest is None else jnp.maximum(largest, most)
        for q in range(blocks):
            source = pl.multiple_of(source_ref[q] * height, height)
            turned_ref[q * height : (q + 1) * height, start : start + ROWS] = turned[
                pl.ds(source, height), :
            ]
    most_ref[...] = jnp.broadcast_to(jnp.max(largest, axis=1, keepdims=True), most_ref.shape)


def turn(sources, flat, after):
    rows, depth = flat.shape
    blocks = sources.shape[0]
    odd = (depth // blocks) % 16
    picked = jnp.arange(16, dtype=jnp.int32) if odd else sources
    turned, most = pl.pallas_call(
        turn_kernel,
        out_shape=(
            jax.ShapeDtypeStruct((depth, rows), flat.dtype),
            jax.ShapeDtypeStruct((8, 128), F32),
        ),
        in_specs=[smem(), vmem(), anyplace()],
        out_specs=(vmem(), vmem()),
        scratch_shapes=[pltpu.VMEM((depth, ROWS), flat.dtype)],
        compiler_params=params(8),
        cost_estimate=pl.CostEstimate(
            flops=0, bytes_accessed=4 * rows * depth, transcendentals=0
        ),
    )(picked, flat, after)
    if odd:
        turned = turned.reshape(blocks, depth // blocks, rows)[sources].reshape(depth, rows)
    return turned, most


def row_products(left, right):
    return lax.dot_general(left, right, (((1,), (1,)), ((), ())), preferred_element_type=F32)


def towers(blocks_ref, samples):
    blocks, _, width = blocks_ref.shape
    image = blocks_ref[:, :samples, :].reshape(blocks * samples, width)
    text = blocks_ref[:, samples:, :].reshape(blocks * samples, width)
    return image, text


def product_kernel(image_most_ref, text_most_ref, *refs):
    *block_refs, out_ref, mark_ref = refs
    near_ref = block_refs[0]
    samples = near_ref.shape[1] // 2
    own_image = near_ref[0, :samples, :]
    own_text = near_ref[0, samples:, :]
    lane = lax.broadcasted_iota(jnp.int32, own_image.shape, 1)
    first = jnp.where(lane == 0, 1.0, 0.0).astype(BF16)
    start = 0
    for ref in block_refs:
        image, text = towers(ref, samples)
        stop = start + image.shape[0]
        found = row_products(jnp.concatenate([own_image, first], axis=0), text)
        out_ref[:samples, start:stop] = found[:samples]
        mark_ref[:, start:stop] = found[samples : samples + 8]
        out_ref[samples:, start:stop] = row_products(own_text, image)
        start = stop


def products(blocks, mosts):
    both = blocks[0].shape[1]
    columns = sum(b.shape[0] for b in blocks) * (both // 2)
    return pl.pallas_call(
        product_kernel,
        out_shape=(
            jax.ShapeDtypeStruct((both, columns), F32),
            jax.ShapeDtypeStruct((8, columns), F32),
        ),
        in_specs=[anyplace()] * 2 + [vmem()] * len(blocks),
        out_specs=(vmem(),) * 2,
        compiler_params=params(8),
    )(*mosts, *blocks)


def middle_kernel(
    tokens_of,
    scale_ref,
    bias_ref,
    gain_ref,
    count_ref,
    own_ref,
    other_ref,
    mark_ref,
    unit_ref,
    norm_ref,
    image_most_ref,
    text_most_ref,
    *refs,
):
    *block_refs, grad_ref, stat_ref = refs
    samples = unit_ref.shape[0] // 2
    scale, bias = scale_ref[0], bias_ref[0]
    dots = own_ref[...] + other_ref[...]
    logits = scale * dots + bias
    row = lax.broadcasted_iota(jnp.int32, dots.shape, 0) % samples
    column = lax.broadcasted_iota(jnp.int32, dots.shape, 1)
    sign = jnp.where(row == column, 1.0, -1.0).astype(F32)
    usable = jnp.where(mark_ref[:1, :] < 1.5, 1.0, 0.0)
    total = jnp.sum(usable, axis=1, keepdims=True)
    used = (usable > 0.5) & (row < count_ref[0])
    margin = -sign * logits
    small = jnp.exp(-jnp.abs(margin))
    soft = jnp.maximum(margin, 0.0) + jnp.log1p(small)
    sigmoid = jnp.where(margin >= 0, 1.0, small) / (1.0 + small)
    part = jnp.where(used, soft, 0.0)[:samples, :]
    loss = jnp.sum(jnp.sum(part, axis=1, keepdims=True), axis=0, keepdims=True) / total
    coeff = gain_ref[0] / total
    dlogit = (jnp.where(used, -sign * sigmoid, 0.0) * coeff).astype(BF16)
    radial = scale * jnp.sum(dlogit.astype(F32) * dots, axis=1, keepdims=True)
    raws = [jnp.zeros((samples, unit_ref.shape[1]), F32) for _ in range(2)]
    start = 0
    for ref in block_refs:
        image, text = towers(ref, samples)
        stop = start + image.shape[0]
        raws[0] += jnp.dot(dlogit[:samples, start:stop], text, preferred_element_type=F32)
        raws[1] += jnp.dot(dlogit[samples:, start:stop], image, preferred_element_type=F32)
        start = stop
    limits = []
    for n, most_ref in enumerate((image_most_ref, text_most_ref)):
        here = slice(n * samples, (n + 1) * samples)
        inward = unit_ref[here, :] * radial[here, :]
        grad = (scale * raws[n] - inward) / norm_ref[here, :1] / tokens_of[n]
        grad_ref[here, :] = grad
        steep = jnp.max(jnp.max(jnp.abs(grad), axis=1, keepdims=True), axis=0, keepdims=True)
        limits.append(1.2 * samples * tokens_of[n] * most_ref[:1, :1] * steep)
    line = lax.broadcasted_iota(jnp.int32, stat_ref.shape, 0)
    stat_ref[...] = jnp.where(line == 0, loss, jnp.where(line == 1, limits[0], limits[1]))


def middle(tokens_of, scale, bias, gain, count, own, other, mark, unit, norm, mosts, blocks):
    return pl.pallas_call(
        functools.partial(middle_kernel, tokens_of),
        out_shape=(
            jax.ShapeDtypeStruct(unit.shape, F32),
            jax.ShapeDtypeStruct((8, unit.shape[1]), F32),
        ),
        in_specs=[smem()] * 4 + [vmem()] * (7 + len(blocks)),
        out_specs=(vmem(), vmem()),
        compiler_params=params(12),
    )(scale, bias, gain, count, own, other, mark, unit, norm, *mosts, *blocks)


def weight_kernel(
    base, carries, grad_ref, slope_ref, turned_ref, stat_ref, _, soon_ref, late_ref, keep_ref, preact_grad
):
    rows, width = slope_ref.shape
    samples = grad_ref.shape[0] // 2
    tok = rows // samples
    for sample in range(samples):
        here = slice(sample * tok, (sample + 1) * tok)
        row = base * samples + sample
        for column in range(0, width, 128):
            columns = slice(column, column + 128)
            slope = slope_ref[here, columns]
            preact_grad[here, columns] = (grad_ref[row : row + 1, columns] * slope).astype(BF16)
    height = late_ref.shape[0]
    if carries:
        soon_ref[height:, :] = stat_ref[...]
    for n, (out, start) in enumerate(
        ((soon_ref, 0), (late_ref, 0), (keep_ref, 0), (keep_ref, height))
    ):
        out[start : start + height, :] = jnp.dot(
            turned_ref[n * height : (n + 1) * height, :],
            preact_grad[...],
            preferred_element_type=F32,
        )


def weight_terms(grad, slope, turned, stat, base, carries, after):
    depth, rows = turned.shape
    width = slope.shape[1]
    quarter = depth // 4
    soon = quarter + (stat.shape[0] if carries else 0)
    return pl.pallas_call(
        functools.partial(weight_kernel, base, carries),
        out_shape=tuple(jax.ShapeDtypeStruct((n, width), F32) for n in (soon, quarter, 2 * quarter)),
        in_specs=[vmem()] * 4 + [anyplace()],
        out_specs=(vmem(),) * 3,
        scratch_shapes=[pltpu.VMEM((rows, width), BF16)],
        compiler_params=params(8),
        cost_estimate=pl.CostEstimate(
            flops=2 * depth * rows * width,
            bytes_accessed=2 * depth * rows + 4 * rows * width + 4 * depth * width,
            transcendentals=0,
        ),
    )(grad, slope, turned, stat, after)


def sum_of(terms):
    total = None
    for term, unit in terms:
        value = term if unit is None else term.astype(F32) * unit
        total = value if total is None else total + value
    return total


def body(
    image_tokens,
    text_tokens,
    image_weight,
    text_weight,
    logit_scale,
    logit_bias,
    loss_scale,
    valid_count,
):
    samples, image_tok, depth = image_tokens.shape
    text_tok = text_tokens.shape[1]
    width = image_weight.shape[1]
    cycle = lax.axis_size("dp")
    bits = cycle.bit_length() - 1
    place = lax.axis_index("dp")

    def swap(array, mask):
        return lax.ppermute(array, "dp", [(i, i ^ mask) for i in range(cycle)])

    def swap_halves(array):
        return lax.ppermute(array, "mp", [(0, 1), (1, 0)])

    def bits_of(value, order):
        return sum(((value >> (len(order) - 1 - i)) & 1) << b for i, b in enumerate(order))

    image_flat = image_tokens.reshape(-1, depth)
    text_flat = text_tokens.reshape(-1, depth)
    text_orders = [list(range(2, bits)), list(range(3, bits)) + [2]]
    image_order = [2, 1] + list(range(3, bits))
    later = [(c, q) for c in range(2) for q in range(cycle // 4)]
    text_blocks = [
        2 * (high + bits_of(q, text_orders[c])) + c for high in (3, 1, 0, 2) for c, q in later
    ]
    image_blocks = [
        high + bits_of(q, image_order[1:])
        for high in (5, 1, 0, 4)
        for q in range(cycle // 4)
    ]
    text_blocks = jnp.asarray(text_blocks, jnp.int32) ^ (2 * place)
    image_blocks = jnp.asarray(image_blocks, jnp.int32) ^ place

    model_place = lax.axis_index("mp").astype(jnp.int32).reshape(1)
    pooled, square, image_slope, text_slope = forward(
        model_place, image_flat, text_flat, image_weight, text_weight, samples
    )
    unit, sent, norm = units(valid_count, pooled, square, swap_halves(square))

    low = max(bits - 2, 1)
    tops = [1 << b for b in reversed(range(low, bits))]
    masks = [tops[0] | tops[1], *tops] if len(tops) == 2 else tops
    arrived = [swap(sent, mask) for mask in masks]
    image_turned, image_most = turn(image_blocks, image_flat, sent)
    gathered = stack([sent] + arrived, image_most)
    text_turned, text_most = turn(text_blocks, text_flat, gathered)
    blocks = [gathered]
    for b in reversed(range(1, low)):
        blocks = blocks + [swap(block, 1 << b) for block in blocks]
    far = [swap(block, 1) for block in blocks[:1]]
    for block in blocks[1:]:
        far.append(swap(stack([block], text_most)[0], 1))
    blocks = blocks + far

    own_dots, mark = products(blocks, (image_most, text_most))
    grad, stat = middle(
        (image_tok, text_tok),
        logit_scale,
        logit_bias,
        loss_scale,
        valid_count,
        own_dots,
        swap_halves(own_dots),
        mark,
        unit,
        norm,
        (image_most, text_most),
        blocks,
    )

    lines = lax.broadcasted_iota(jnp.int32, (FOOT, width), 0)

    def footer(exponents, stat):
        rows = list(exponents)
        rest = stat[:1]
        for _ in range(3):
            part = lax.reduce_precision(rest, 5, 10)
            rows.append(part)
            rest = (rest - part) * 2048.0
        found = jnp.zeros((FOOT, width), F32)
        for n, row in enumerate(rows):
            found = jnp.where(lines == n, row, found)
        return found

    def exponents_of(stat):
        return [jnp.ceil(jnp.log2(jnp.maximum(stat[n : n + 1], 1e-30))) for n in (1, 2)]

    def merged(stat, message):
        foot = message[-FOOT:].astype(F32)
        loss = (foot[4:5] / 2048.0 + foot[3:4]) / 2048.0 + foot[2:3]
        there = [foot[:1], foot[1:2]]
        add = [loss, jnp.exp2(there[0]), jnp.exp2(there[1])]
        total = [stat[n : n + 1] + row for n, row in enumerate(add)]
        return jnp.concatenate(total), there

    def halves(terms):
        half = terms[0][0].shape[0] // 2
        return [[(term[rows], unit) for term, unit in terms] for rows in (slice(half), slice(half, None))]

    def coded_of(terms, stat, tower, after):
        factor = HALF_MAX * jnp.exp2(-exponents_of(stat)[tower]) + 0.0 * after[:1].astype(F32)
        return sum_of(terms) * factor

    def with_foot(coded, exponents, stat):
        rows = coded.shape[0]
        foot = footer(exponents, stat) + 0.0 * coded[:1]
        coded = jnp.pad(coded, ((0, FOOT), (0, 0))) + jnp.pad(foot, ((rows, 0), (0, 0)))
        return coded.astype(jnp.float16)

    def leave(terms, stat, tower, bit, after):
        coded = with_foot(coded_of(terms, stat, tower, after), exponents_of(stat), stat)
        return coded, swap(coded, 1 << bit)

    def take(terms, stat, tower, coming):
        stat, there = merged(stat, coming)
        return terms + [(coming[:-FOOT], jnp.exp2(there[tower]) / HALF_MAX)], stat

    def core_step(soon, late, keep):
        height = late.shape[0]
        there = swap(soon, 1)
        stays = [(keep[:height], None), (swap(late, 1), None)]
        return stays, [(keep[height:], None), (there[:height], None)], there[height:]

    image_terms = weight_terms(grad, image_slope, image_turned, stat, 0, True, stat)
    image, image_leaves, stat_there = core_step(*image_terms)
    start_stat = stat[:3] + stat_there[:3]
    text_terms = weight_terms(grad, text_slope, text_turned, stat, 1, False, image_terms[0])
    text, text_leaves, _ = core_step(*text_terms)

    coded, image_in = leave(image_leaves, start_stat, 0, image_order[0], start_stat)
    coded, text_in = leave(text_leaves, start_stat, 1, 1, coded)
    text, text_stat = take(text, start_stat, 1, text_in)
    parts = [(terms, text_stat) for terms in halves(text)]
    image_in = image_in.astype(F32) + 0.0 * coded[:1].astype(F32)
    image, image_stat = take(image, start_stat, 0, image_in)
    for step in range(bits - 3):
        image, image_leaves = halves(image)
        (first, first_stat), (second, second_stat) = parts
        first, first_leaves = halves(first)
        second, second_leaves = halves(second)
        coded, image_in = leave(image_leaves, image_stat, 0, image_order[step + 1], coded)
        coded, second_in = leave(second_leaves, second_stat, 1, text_orders[1][step], coded)
        coded, first_in = leave(first_leaves, first_stat, 1, text_orders[0][step], coded)
        parts = [(first, first_stat, first_in), (second, second_stat, second_in)]
        if step < bits - 4:
            parts = [take(terms, old, 1, arrival) for terms, old, arrival in parts]
        image, image_stat = take(image, image_stat, 0, image_in)

    (first, first_stat, first_in), (second, second_stat, second_in) = parts
    first, first_stat = take(first, first_stat, 1, first_in)
    first, first_leaves = halves(first)
    image, image_leaves = halves(image)
    image_coded = coded_of(image_leaves, image_stat, 0, coded)
    first_coded = coded_of(first_leaves, first_stat, 1, coded)
    exponents = [exponents_of(image_stat)[0], exponents_of(first_stat)[1]]
    rows = image_coded.shape[0]
    both = jnp.pad(image_coded, ((0, first_coded.shape[0]), (0, 0)))
    both = both + jnp.pad(first_coded, ((rows, 0), (0, 0)))
    both = with_foot(both, exponents, first_stat)
    both_in = swap(both, 1 << image_order[-1])
    second_in = second_in.astype(F32) + 0.0 * both[:1].astype(F32)
    second, second_stat = take(second, second_stat, 1, second_in)
    second, second_leaves = halves(second)
    coded, second_in = leave(second_leaves, second_stat, 1, text_orders[1][-1], coded)
    second, _ = take(second, second_stat, 1, second_in)
    first, first_stat = take(first, first_stat, 1, both_in[rows:])
    image, _ = take(image, image_stat, 0, jnp.concatenate([both_in[:rows], both_in[-FOOT:]]))
    row = 0.0 * coded[:1].astype(F32)
    text = jnp.concatenate([sum_of(first) + row, sum_of(second)])
    loss = jnp.max(first_stat[:1] + row)
    return (loss, sum_of(image), text)


def solution(mesh):
    placed = (
        P("dp", None, None),
        P("dp", None, None),
        P(None, "mp"),
        P(None, "mp"),
        P(),
        P(),
        P(),
        P("dp"),
    )
    return jax.shard_map(
        body,
        mesh=mesh,
        in_specs=placed,
        out_specs=(P(), P("dp", "mp"), P("dp", "mp")),
        check_vma=False,
    )
```

```python
import functools

import jax
import jax.numpy as jnp
from jax import lax
from jax.experimental import pallas as pl
from jax.experimental.pallas import tpu as pltpu
from jax.sharding import PartitionSpec as P

F32 = jnp.float32
BF16 = jnp.bfloat16
ROWS = 256
JOB_ROWS = 256
JOB_COLUMNS = 256
STRIP = 64
ROOT = 0.7978845608028654
HALF_MAX = 16384.0
FOOT = 8
UNUSABLE = 2.0


def vmem():
    return pl.BlockSpec(memory_space=pltpu.VMEM)


def smem():
    return pl.BlockSpec(memory_space=pltpu.SMEM)


def anyplace():
    return pl.BlockSpec(memory_space=pl.ANY)


def hbm():
    return pl.BlockSpec(memory_space=pltpu.HBM)


def params(mib):
    return pltpu.CompilerParams(vmem_limit_bytes=mib * 2**20)


def gelu(x):
    square = x * x
    return x * (0.5 + 0.5 * jnp.tanh(x * (ROOT + (0.044715 * ROOT) * square)))


def gelu_slope(x):
    square = x * x
    t = jnp.tanh(x * (ROOT + (0.044715 * ROOT) * square))
    rise = (1.0 - t) * (x * (ROOT + (3 * 0.044715 * ROOT) * square))
    return (0.5 + 0.5 * t) * (1.0 + rise)


def forward_kernel(
    tokens_of,
    place_ref,
    image_hbm,
    text_hbm,
    image_w_hbm,
    text_w_hbm,
    pooled_ref,
    square_ref,
    image_preact_hbm,
    text_preact_hbm,
    image_v,
    text_v,
    image_w,
    text_w,
    image_preact,
    text_preact,
    in_sem,
    w_sem,
    out_sem,
):
    width = image_w.shape[1]
    samples = pooled_ref.shape[0] // 2
    towers_here = (
        (text_hbm, text_v, text_w_hbm, text_w, text_preact, text_preact_hbm, tokens_of[1], samples),
        (image_hbm, image_v, image_w_hbm, image_w, image_preact, image_preact_hbm, tokens_of[0], 0),
    )
    waits, tiles = [], []
    for t, (source, buf, w_source, w, _, _, _, _) in enumerate(towers_here):
        here = [
            pltpu.make_async_copy(w_source, w, w_sem.at[t]),
            pltpu.make_async_copy(source, buf, in_sem.at[t]),
        ]
        for copy in here:
            copy.start()
        waits.append(here)
        for start in range(0, buf.shape[0], JOB_ROWS):
            for column in range(0, width, JOB_COLUMNS):
                tiles.append((t, start, column))
    first = place_ref[0] * width

    def project(n):
        t, start, column = tiles[n]
        _, buf, _, w, preact, _, _, _ = towers_here[t]
        if start == 0 and column == 0:
            for copy in waits[t]:
                copy.wait()
        rows, columns = slice(start, start + JOB_ROWS), slice(column, column + JOB_COLUMNS)
        preact[rows, columns] = jnp.dot(buf[rows, :], w[:, columns], preferred_element_type=F32)

    out_copies = []
    project(0)
    for n, (t, start, tile_column) in enumerate(tiles):
        _, buf, _, _, preact, preact_out, tok, base = towers_here[t]
        if n + 1 < len(tiles):
            project(n + 1)
        for row in range(start, start + JOB_ROWS, STRIP):
            rows = slice(row, row + STRIP)
            here = (rows, slice(tile_column, tile_column + JOB_COLUMNS))
            token_columns = pl.ds(pl.multiple_of(first + tile_column, 128), JOB_COLUMNS)
            hidden = buf[rows, token_columns].astype(F32) + gelu(preact[here])
            for part in range(0, STRIP, tok):
                sample = base + (row + part) // tok
                pooled_ref[sample : sample + 1, here[1]] = (
                    jnp.sum(hidden[part : part + tok], axis=0, keepdims=True) / tok
                )
        if tile_column + JOB_COLUMNS == width:
            part = pl.ds(start, JOB_ROWS)
            copy = pltpu.make_async_copy(
                preact.at[part, :], preact_out.at[part, :], out_sem.at[len(out_copies)]
            )
            copy.start()
            out_copies.append(copy)
    pooled = pooled_ref[...]
    total = jnp.sum(pooled * pooled, axis=1, keepdims=True)
    square_ref[...] = jnp.broadcast_to(total, square_ref.shape)
    for copy in out_copies:
        copy.wait()


def forward(place, image_flat, text_flat, image_w, text_w, samples):
    width = image_w.shape[1]
    depth = image_w.shape[0]
    rows_i, rows_t = image_flat.shape[0], text_flat.shape[0]
    jobs = (rows_i + rows_t) // JOB_ROWS
    return pl.pallas_call(
        functools.partial(forward_kernel, (rows_i // samples, rows_t // samples)),
        out_shape=(
            jax.ShapeDtypeStruct((2 * samples, width), F32),
            jax.ShapeDtypeStruct((2 * samples, 128), F32),
            jax.ShapeDtypeStruct((rows_i, width), F32),
            jax.ShapeDtypeStruct((rows_t, width), F32),
        ),
        in_specs=[smem()] + [hbm()] * 4,
        out_specs=(vmem(), vmem(), hbm(), hbm()),
        scratch_shapes=[
            pltpu.VMEM((rows_i, depth), BF16),
            pltpu.VMEM((rows_t, depth), BF16),
            pltpu.VMEM((depth, width), BF16),
            pltpu.VMEM((depth, width), BF16),
            pltpu.VMEM((rows_i, width), F32),
            pltpu.VMEM((rows_t, width), F32),
            pltpu.SemaphoreType.DMA((2,)),
            pltpu.SemaphoreType.DMA((2,)),
            pltpu.SemaphoreType.DMA((jobs,)),
        ],
        compiler_params=params(53),
        cost_estimate=pl.CostEstimate(
            flops=2 * (rows_i + rows_t) * depth * width,
            bytes_accessed=2 * (rows_i + rows_t) * (depth + 2 * width) + 4 * depth * width,
            transcendentals=(rows_i + rows_t) * width,
        ),
    )(place, image_flat, text_flat, image_w, text_w)


def unit_kernel(count_ref, pooled_ref, own_ref, other_ref, unit_ref, sent_ref, norm_ref):
    both = pooled_ref.shape[0]
    norm = jnp.sqrt(own_ref[...] + other_ref[...] + 1e-06)
    norm_ref[...] = norm
    unit = pooled_ref[...] / norm[:, :1]
    unit_ref[...] = unit
    row = lax.broadcasted_iota(jnp.int32, unit.shape, 0) % (both // 2)
    sent_ref[...] = jnp.where(row < count_ref[0], unit, UNUSABLE).astype(BF16)


def units(count, pooled, own, other):
    return pl.pallas_call(
        unit_kernel,
        out_shape=(
            jax.ShapeDtypeStruct(pooled.shape, F32),
            jax.ShapeDtypeStruct(pooled.shape, BF16),
            jax.ShapeDtypeStruct(own.shape, F32),
        ),
        in_specs=[smem()] + [pl.BlockSpec()] * 3,
        out_specs=(vmem(),) * 3,
        compiler_params=params(4),
    )(count, pooled, own, other)


def stack_kernel(afters, *refs):
    parts, out_ref = refs[afters:-1], refs[-1]
    for n, part in enumerate(parts):
        out_ref[n] = part[...]


def stack(parts, *afters):
    return pl.pallas_call(
        functools.partial(stack_kernel, len(afters)),
        out_shape=jax.ShapeDtypeStruct((len(parts), *parts[0].shape), parts[0].dtype),
        in_specs=[anyplace()] * len(afters) + [vmem()] * len(parts),
        out_specs=vmem(),
        compiler_params=params(4),
    )(*afters, *parts)


def slope_kernel(preact_ref, _, slope_ref):
    rows, width = preact_ref.shape
    for row in range(0, rows, STRIP):
        for column in range(0, width, JOB_COLUMNS):
            here = (slice(row, row + STRIP), slice(column, column + JOB_COLUMNS))
            slope_ref[here] = gelu_slope(preact_ref[here])


def slopes(preact, after):
    return pl.pallas_call(
        slope_kernel,
        out_shape=jax.ShapeDtypeStruct(preact.shape, F32),
        in_specs=[vmem(), anyplace()],
        out_specs=vmem(),
        compiler_params=params(4),
        cost_estimate=pl.CostEstimate(
            flops=0, bytes_accessed=8 * preact.size, transcendentals=preact.size
        ),
    )(preact, after)


def turn_kernel(source_ref, tokens_ref, _, turned_ref, most_ref, turned):
    rows, _ = tokens_ref.shape
    blocks = source_ref.shape[0]
    height = turned_ref.shape[0] // blocks
    largest = None
    for start in range(0, rows, ROWS):
        tokens = tokens_ref[start : start + ROWS, :]
        turned[...] = tokens.T
        most = jnp.max(jnp.abs(tokens).astype(F32), axis=0, keepdims=True)
        largest = most if largest is None else jnp.maximum(largest, most)
        for q in range(blocks):
            source = pl.multiple_of(source_ref[q] * height, height)
            turned_ref[q * height : (q + 1) * height, start : start + ROWS] = turned[
                pl.ds(source, height), :
            ]
    most_ref[...] = jnp.broadcast_to(jnp.max(largest, axis=1, keepdims=True), most_ref.shape)


def turn(sources, flat, after):
    rows, depth = flat.shape
    blocks = sources.shape[0]
    odd = (depth // blocks) % 16
    picked = jnp.arange(16, dtype=jnp.int32) if odd else sources
    turned, most = pl.pallas_call(
        turn_kernel,
        out_shape=(
            jax.ShapeDtypeStruct((depth, rows), flat.dtype),
            jax.ShapeDtypeStruct((8, 128), F32),
        ),
        in_specs=[smem(), vmem(), anyplace()],
        out_specs=(vmem(), vmem()),
        scratch_shapes=[pltpu.VMEM((depth, ROWS), flat.dtype)],
        compiler_params=params(8),
        cost_estimate=pl.CostEstimate(
            flops=0, bytes_accessed=4 * rows * depth, transcendentals=0
        ),
    )(picked, flat, after)
    if odd:
        turned = turned.reshape(blocks, depth // blocks, rows)[sources].reshape(depth, rows)
    return turned, most


def row_products(left, right):
    return lax.dot_general(left, right, (((1,), (1,)), ((), ())), preferred_element_type=F32)


def towers(blocks_ref, samples):
    blocks, _, width = blocks_ref.shape
    image = blocks_ref[:, :samples, :].reshape(blocks * samples, width)
    text = blocks_ref[:, samples:, :].reshape(blocks * samples, width)
    return image, text


def product_kernel(*refs):
    *block_refs, out_ref, mark_ref = refs
    near_ref = block_refs[0]
    samples = near_ref.shape[1] // 2
    own_image = near_ref[0, :samples, :]
    own_text = near_ref[0, samples:, :]
    lane = lax.broadcasted_iota(jnp.int32, own_image.shape, 1)
    first = jnp.where(lane == 0, 1.0, 0.0).astype(BF16)
    start = 0
    for ref in block_refs:
        image, text = towers(ref, samples)
        stop = start + image.shape[0]
        found = row_products(jnp.concatenate([own_image, first], axis=0), text)
        out_ref[:samples, start:stop] = found[:samples]
        mark_ref[:, start:stop] = found[samples : samples + 8]
        out_ref[samples:, start:stop] = row_products(own_text, image)
        start = stop


def products(blocks):
    both = blocks[0].shape[1]
    columns = sum(b.shape[0] for b in blocks) * (both // 2)
    return pl.pallas_call(
        product_kernel,
        out_shape=(
            jax.ShapeDtypeStruct((both, columns), F32),
            jax.ShapeDtypeStruct((8, columns), F32),
        ),
        in_specs=[vmem()] * len(blocks),
        out_specs=(vmem(),) * 2,
        compiler_params=params(8),
    )(*blocks)


def middle_kernel(
    tokens_of,
    scale_ref,
    bias_ref,
    gain_ref,
    count_ref,
    own_ref,
    other_ref,
    mark_ref,
    unit_ref,
    norm_ref,
    image_most_ref,
    text_most_ref,
    *refs,
):
    *block_refs, grad_ref, stat_ref = refs
    samples = unit_ref.shape[0] // 2
    scale, bias = scale_ref[0], bias_ref[0]
    dots = own_ref[...] + other_ref[...]
    logits = scale * dots + bias
    row = lax.broadcasted_iota(jnp.int32, dots.shape, 0) % samples
    column = lax.broadcasted_iota(jnp.int32, dots.shape, 1)
    sign = jnp.where(row == column, 1.0, -1.0).astype(F32)
    usable = jnp.where(mark_ref[:1, :] < 1.5, 1.0, 0.0)
    total = jnp.sum(usable, axis=1, keepdims=True)
    used = (usable > 0.5) & (row < count_ref[0])
    margin = -sign * logits
    small = jnp.exp(-jnp.abs(margin))
    soft = jnp.maximum(margin, 0.0) + jnp.log1p(small)
    sigmoid = jnp.where(margin >= 0, 1.0, small) / (1.0 + small)
    part = jnp.where(used, soft, 0.0)[:samples, :]
    loss = jnp.sum(jnp.sum(part, axis=1, keepdims=True), axis=0, keepdims=True) / total
    coeff = gain_ref[0] / total
    dlogit = (jnp.where(used, -sign * sigmoid, 0.0) * coeff).astype(BF16)
    radial = scale * jnp.sum(dlogit.astype(F32) * dots, axis=1, keepdims=True)
    raws = [jnp.zeros((samples, unit_ref.shape[1]), F32) for _ in range(2)]
    start = 0
    for ref in block_refs:
        image, text = towers(ref, samples)
        stop = start + image.shape[0]
        raws[0] += jnp.dot(dlogit[:samples, start:stop], text, preferred_element_type=F32)
        raws[1] += jnp.dot(dlogit[samples:, start:stop], image, preferred_element_type=F32)
        start = stop
    limits = []
    for n, most_ref in enumerate((image_most_ref, text_most_ref)):
        here = slice(n * samples, (n + 1) * samples)
        inward = unit_ref[here, :] * radial[here, :]
        grad = (scale * raws[n] - inward) / norm_ref[here, :1] / tokens_of[n]
        grad_ref[here, :] = grad
        steep = jnp.max(jnp.max(jnp.abs(grad), axis=1, keepdims=True), axis=0, keepdims=True)
        limits.append(1.2 * samples * tokens_of[n] * most_ref[:1, :1] * steep)
    line = lax.broadcasted_iota(jnp.int32, stat_ref.shape, 0)
    stat_ref[...] = jnp.where(line == 0, loss, jnp.where(line == 1, limits[0], limits[1]))


def middle(tokens_of, scale, bias, gain, count, own, other, mark, unit, norm, mosts, blocks):
    return pl.pallas_call(
        functools.partial(middle_kernel, tokens_of),
        out_shape=(
            jax.ShapeDtypeStruct(unit.shape, F32),
            jax.ShapeDtypeStruct((8, unit.shape[1]), F32),
        ),
        in_specs=[smem()] * 4 + [vmem()] * (7 + len(blocks)),
        out_specs=(vmem(), vmem()),
        compiler_params=params(12),
    )(scale, bias, gain, count, own, other, mark, unit, norm, *mosts, *blocks)


def weight_kernel(
    base, carries, grad_ref, slope_ref, turned_ref, stat_ref, _, soon_ref, late_ref, keep_ref, preact_grad
):
    rows, width = slope_ref.shape
    samples = grad_ref.shape[0] // 2
    tok = rows // samples
    for sample in range(samples):
        here = slice(sample * tok, (sample + 1) * tok)
        row = base * samples + sample
        for column in range(0, width, 128):
            columns = slice(column, column + 128)
            slope = slope_ref[here, columns]
            preact_grad[here, columns] = (grad_ref[row : row + 1, columns] * slope).astype(BF16)
    height = late_ref.shape[0]
    if carries:
        soon_ref[height:, :] = stat_ref[...]
    for n, (out, start) in enumerate(
        ((soon_ref, 0), (late_ref, 0), (keep_ref, 0), (keep_ref, height))
    ):
        out[start : start + height, :] = jnp.dot(
            turned_ref[n * height : (n + 1) * height, :],
            preact_grad[...],
            preferred_element_type=F32,
        )


def weight_terms(grad, slope, turned, stat, base, carries, after):
    depth, rows = turned.shape
    width = slope.shape[1]
    quarter = depth // 4
    soon = quarter + (stat.shape[0] if carries else 0)
    return pl.pallas_call(
        functools.partial(weight_kernel, base, carries),
        out_shape=tuple(jax.ShapeDtypeStruct((n, width), F32) for n in (soon, quarter, 2 * quarter)),
        in_specs=[vmem()] * 4 + [anyplace()],
        out_specs=(vmem(),) * 3,
        scratch_shapes=[pltpu.VMEM((rows, width), BF16)],
        compiler_params=params(8),
        cost_estimate=pl.CostEstimate(
            flops=2 * depth * rows * width,
            bytes_accessed=2 * depth * rows + 4 * rows * width + 4 * depth * width,
            transcendentals=0,
        ),
    )(grad, slope, turned, stat, after)


def sum_of(terms):
    total = None
    for term, unit in terms:
        value = term if unit is None else term.astype(F32) * unit
        total = value if total is None else total + value
    return total


def body(
    image_tokens,
    text_tokens,
    image_weight,
    text_weight,
    logit_scale,
    logit_bias,
    loss_scale,
    valid_count,
):
    samples, image_tok, depth = image_tokens.shape
    text_tok = text_tokens.shape[1]
    width = image_weight.shape[1]
    cycle = lax.axis_size("dp")
    bits = cycle.bit_length() - 1
    place = lax.axis_index("dp")

    def swap(array, mask):
        return lax.ppermute(array, "dp", [(i, i ^ mask) for i in range(cycle)])

    def swap_halves(array):
        return lax.ppermute(array, "mp", [(0, 1), (1, 0)])

    def bits_of(value, order):
        return sum(((value >> (len(order) - 1 - i)) & 1) << b for i, b in enumerate(order))

    image_flat = image_tokens.reshape(-1, depth)
    text_flat = text_tokens.reshape(-1, depth)
    text_orders = [list(range(2, bits)), list(range(3, bits)) + [2]]
    image_order = [2, 1] + list(range(3, bits))
    later = [(c, q) for c in range(2) for q in range(cycle // 4)]
    text_blocks = [
        2 * (high + bits_of(q, text_orders[c])) + c for high in (3, 1, 0, 2) for c, q in later
    ]
    image_blocks = [
        high + bits_of(q, image_order[1:])
        for high in (5, 1, 0, 4)
        for q in range(cycle // 4)
    ]
    text_blocks = jnp.asarray(text_blocks, jnp.int32) ^ (2 * place)
    image_blocks = jnp.asarray(image_blocks, jnp.int32) ^ place

    model_place = lax.axis_index("mp").astype(jnp.int32).reshape(1)
    pooled, square, image_preact, text_preact = forward(
        model_place, image_flat, text_flat, image_weight, text_weight, samples
    )
    unit, sent, norm = units(valid_count, pooled, square, swap_halves(square))

    low = max(bits - 2, 1)
    tops = [1 << b for b in reversed(range(low, bits))]
    masks = tops + [tops[0] | tops[1]] if len(tops) == 2 else tops
    arrived = [swap(sent, mask) for mask in masks]
    image_turned, image_most = turn(image_blocks, image_flat, sent)
    text_slope = slopes(text_preact, image_most)
    gathered = stack([sent] + arrived, text_slope)
    image_slope = slopes(image_preact, gathered)
    blocks = [gathered]
    for b in reversed(range(1, low)):
        blocks = blocks + [swap(block, 1 << b) for block in blocks]
    far = [swap(block, 1) for block in blocks[:1]]
    for block in blocks[1:]:
        far.append(swap(stack([block], image_slope)[0], 1))
    blocks = blocks + far

    own_dots, mark = products(blocks)
    text_turned, text_most = turn(text_blocks, text_flat, own_dots)
    grad, stat = middle(
        (image_tok, text_tok),
        logit_scale,
        logit_bias,
        loss_scale,
        valid_count,
        own_dots,
        swap_halves(own_dots),
        mark,
        unit,
        norm,
        (image_most, text_most),
        blocks,
    )

    lines = lax.broadcasted_iota(jnp.int32, (FOOT, width), 0)

    def footer(exponents, stat):
        rows = list(exponents)
        rest = stat[:1]
        for _ in range(3):
            part = lax.reduce_precision(rest, 5, 10)
            rows.append(part)
            rest = (rest - part) * 2048.0
        found = jnp.zeros((FOOT, width), F32)
        for n, row in enumerate(rows):
            found = jnp.where(lines == n, row, found)
        return found

    def exponents_of(stat):
        return [jnp.ceil(jnp.log2(jnp.maximum(stat[n : n + 1], 1e-30))) for n in (1, 2)]

    def merged(stat, message):
        foot = message[-FOOT:].astype(F32)
        loss = (foot[4:5] / 2048.0 + foot[3:4]) / 2048.0 + foot[2:3]
        there = [foot[:1], foot[1:2]]
        add = [loss, jnp.exp2(there[0]), jnp.exp2(there[1])]
        total = [stat[n : n + 1] + row for n, row in enumerate(add)]
        return jnp.concatenate(total), there

    def halves(terms):
        half = terms[0][0].shape[0] // 2
        return [[(term[rows], unit) for term, unit in terms] for rows in (slice(half), slice(half, None))]

    def coded_of(terms, stat, tower, after):
        factor = HALF_MAX * jnp.exp2(-exponents_of(stat)[tower]) + 0.0 * after[:1].astype(F32)
        return sum_of(terms) * factor

    def with_foot(coded, exponents, stat):
        rows = coded.shape[0]
        foot = footer(exponents, stat) + 0.0 * coded[:1]
        coded = jnp.pad(coded, ((0, FOOT), (0, 0))) + jnp.pad(foot, ((rows, 0), (0, 0)))
        return coded.astype(jnp.float16)

    def leave(terms, stat, tower, bit, after):
        coded = with_foot(coded_of(terms, stat, tower, after), exponents_of(stat), stat)
        return coded, swap(coded, 1 << bit)

    def take(terms, stat, tower, coming):
        stat, there = merged(stat, coming)
        return terms + [(coming[:-FOOT], jnp.exp2(there[tower]) / HALF_MAX)], stat

    def core_step(soon, late, keep):
        height = late.shape[0]
        there = swap(soon, 1)
        stays = [(keep[:height], None), (swap(late, 1), None)]
        return stays, [(keep[height:], None), (there[:height], None)], there[height:]

    text_terms = weight_terms(grad, text_slope, text_turned, stat, 1, True, stat)
    text, text_leaves, stat_there = core_step(*text_terms)
    start_stat = stat[:3] + stat_there[:3]
    image_terms = weight_terms(grad, image_slope, image_turned, stat, 0, False, text_terms[0])
    image, image_leaves, _ = core_step(*image_terms)

    coded, text_in = leave(text_leaves, start_stat, 1, 1, start_stat)
    coded, image_in = leave(image_leaves, start_stat, 0, image_order[0], coded)
    text, text_stat = take(text, start_stat, 1, text_in)
    parts = [(terms, text_stat) for terms in halves(text)]
    image, image_stat = take(image, start_stat, 0, image_in)
    for step in range(bits - 3):
        image, image_leaves = halves(image)
        (first, first_stat), (second, second_stat) = parts
        first, first_leaves = halves(first)
        second, second_leaves = halves(second)
        coded, second_in = leave(second_leaves, second_stat, 1, text_orders[1][step], coded)
        coded, first_in = leave(first_leaves, first_stat, 1, text_orders[0][step], coded)
        coded, image_in = leave(image_leaves, image_stat, 0, image_order[step + 1], coded)
        parts = [(first, first_stat, first_in), (second, second_stat, second_in)]
        if step < bits - 4:
            parts = [take(terms, old, 1, arrival) for terms, old, arrival in parts]
        image, image_stat = take(image, image_stat, 0, image_in)

    (first, first_stat, first_in), (second, second_stat, second_in) = parts
    first, first_stat = take(first, first_stat, 1, first_in)
    first, first_leaves = halves(first)
    image, image_leaves = halves(image)
    image_coded = coded_of(image_leaves, image_stat, 0, coded)
    first_coded = coded_of(first_leaves, first_stat, 1, coded)
    exponents = [exponents_of(image_stat)[0], exponents_of(first_stat)[1]]
    rows = image_coded.shape[0]
    both = jnp.pad(image_coded, ((0, first_coded.shape[0]), (0, 0)))
    both = both + jnp.pad(first_coded, ((rows, 0), (0, 0)))
    both = with_foot(both, exponents, first_stat)
    both_in = swap(both, 1 << image_order[-1])
    second_in = second_in.astype(F32) + 0.0 * both[:1].astype(F32)
    second, second_stat = take(second, second_stat, 1, second_in)
    second, second_leaves = halves(second)
    coded, second_in = leave(second_leaves, second_stat, 1, text_orders[1][-1], coded)
    second, _ = take(second, second_stat, 1, second_in)
    first, first_stat = take(first, first_stat, 1, both_in[rows:])
    image, _ = take(image, image_stat, 0, jnp.concatenate([both_in[:rows], both_in[-FOOT:]]))
    row = 0.0 * coded[:1].astype(F32)
    text = jnp.concatenate([sum_of(first) + row, sum_of(second)])
    loss = jnp.max(first_stat[:1] + row)
    return (loss, sum_of(image), text)


def solution(mesh):
    placed = (
        P("dp", None, None),
        P("dp", None, None),
        P(None, "mp"),
        P(None, "mp"),
        P(),
        P(),
        P(),
        P("dp"),
    )
    return jax.shard_map(
        body,
        mesh=mesh,
        in_specs=placed,
        out_specs=(P(), P("dp", "mp"), P("dp", "mp")),
        check_vma=False,
    )
```

```python
import functools

import jax
import jax.numpy as jnp
from jax import lax
from jax.experimental import pallas as pl
from jax.experimental.pallas import tpu as pltpu
from jax.sharding import PartitionSpec as P

F32 = jnp.float32
BF16 = jnp.bfloat16
ROWS = 256
JOB_ROWS = 256
JOB_COLUMNS = 256
STRIP = 64
ROOT = 0.7978845608028654
HALF_MAX = 16384.0
FOOT = 8
UNUSABLE = 2.0


def vmem():
    return pl.BlockSpec(memory_space=pltpu.VMEM)


def smem():
    return pl.BlockSpec(memory_space=pltpu.SMEM)


def anyplace():
    return pl.BlockSpec(memory_space=pl.ANY)


def hbm():
    return pl.BlockSpec(memory_space=pltpu.HBM)


def params(mib):
    return pltpu.CompilerParams(vmem_limit_bytes=mib * 2**20)


def gelu_and_slope(x):
    square = x * x
    cdf = 0.5 + 0.5 * jnp.tanh(x * (ROOT + (0.044715 * ROOT) * square))
    value = x * cdf
    rise = (value - value * cdf) * (2 * ROOT + (6 * 0.044715 * ROOT) * square)
    return value, cdf + rise


def forward_kernel(
    tokens_of,
    place_ref,
    image_hbm,
    text_hbm,
    image_w_hbm,
    text_w_hbm,
    pooled_ref,
    square_ref,
    image_slope_hbm,
    text_slope_hbm,
    image_v,
    text_v,
    image_w,
    text_w,
    image_slope,
    text_slope,
    even,
    odd,
    in_sem,
    w_sem,
    out_sem,
):
    width = image_w.shape[1]
    samples = pooled_ref.shape[0] // 2
    towers_here = (
        (text_hbm, text_v, text_w_hbm, text_w, text_slope, text_slope_hbm, tokens_of[1], samples),
        (image_hbm, image_v, image_w_hbm, image_w, image_slope, image_slope_hbm, tokens_of[0], 0),
    )
    waits, tiles = [], []
    for t, (source, buf, w_source, w, _, _, _, _) in enumerate(towers_here):
        here = [
            pltpu.make_async_copy(w_source, w, w_sem.at[t]),
            pltpu.make_async_copy(source, buf, in_sem.at[t]),
        ]
        for copy in here:
            copy.start()
        waits.append(here)
        for start in range(0, buf.shape[0], JOB_ROWS):
            for column in range(0, width, JOB_COLUMNS):
                tiles.append((t, start, column))
    first = place_ref[0] * width

    def project(n):
        t, start, column = tiles[n]
        _, buf, _, w, _, _, _, _ = towers_here[t]
        if start == 0 and column == 0:
            for copy in waits[t]:
                copy.wait()
        rows, columns = slice(start, start + JOB_ROWS), slice(column, column + JOB_COLUMNS)
        target = (even, odd)[n % 2]
        target[...] = jnp.dot(buf[rows, :], w[:, columns], preferred_element_type=F32)

    out_copies = []
    project(0)
    for n, (t, start, tile_column) in enumerate(tiles):
        _, buf, _, _, slope, slope_out, tok, base = towers_here[t]
        if n + 1 < len(tiles):
            project(n + 1)
        for row in range(start, start + JOB_ROWS, STRIP):
            rows = slice(row, row + STRIP)
            here = (rows, slice(tile_column, tile_column + JOB_COLUMNS))
            token_columns = pl.ds(pl.multiple_of(first + tile_column, 128), JOB_COLUMNS)
            preact = (even, odd)[n % 2][row - start : row - start + STRIP, :]
            value, slant = gelu_and_slope(preact)
            slope[here] = slant
            hidden = buf[rows, token_columns].astype(F32) + value
            for part in range(0, STRIP, tok):
                sample = base + (row + part) // tok
                pooled_ref[sample : sample + 1, here[1]] = (
                    jnp.sum(hidden[part : part + tok], axis=0, keepdims=True) / tok
                )
        if tile_column + JOB_COLUMNS == width:
            part = pl.ds(start, JOB_ROWS)
            copy = pltpu.make_async_copy(
                slope.at[part, :], slope_out.at[part, :], out_sem.at[len(out_copies)]
            )
            copy.start()
            out_copies.append(copy)
    pooled = pooled_ref[...]
    total = jnp.sum(pooled * pooled, axis=1, keepdims=True)
    square_ref[...] = jnp.broadcast_to(total, square_ref.shape)
    for copy in out_copies:
        copy.wait()


def forward(place, image_flat, text_flat, image_w, text_w, samples):
    width = image_w.shape[1]
    depth = image_w.shape[0]
    rows_i, rows_t = image_flat.shape[0], text_flat.shape[0]
    jobs = (rows_i + rows_t) // JOB_ROWS
    return pl.pallas_call(
        functools.partial(forward_kernel, (rows_i // samples, rows_t // samples)),
        out_shape=(
            jax.ShapeDtypeStruct((2 * samples, width), F32),
            jax.ShapeDtypeStruct((2 * samples, 128), F32),
            jax.ShapeDtypeStruct((rows_i, width), F32),
            jax.ShapeDtypeStruct((rows_t, width), F32),
        ),
        in_specs=[smem()] + [hbm()] * 4,
        out_specs=(vmem(), vmem(), hbm(), hbm()),
        scratch_shapes=[
            pltpu.VMEM((rows_i, depth), BF16),
            pltpu.VMEM((rows_t, depth), BF16),
            pltpu.VMEM((depth, width), BF16),
            pltpu.VMEM((depth, width), BF16),
            pltpu.VMEM((rows_i, width), F32),
            pltpu.VMEM((rows_t, width), F32),
            pltpu.VMEM((JOB_ROWS, JOB_COLUMNS), F32),
            pltpu.VMEM((JOB_ROWS, JOB_COLUMNS), F32),
            pltpu.SemaphoreType.DMA((2,)),
            pltpu.SemaphoreType.DMA((2,)),
            pltpu.SemaphoreType.DMA((jobs,)),
        ],
        compiler_params=params(53),
        cost_estimate=pl.CostEstimate(
            flops=2 * (rows_i + rows_t) * depth * width,
            bytes_accessed=2 * (rows_i + rows_t) * (depth + 2 * width) + 4 * depth * width,
            transcendentals=(rows_i + rows_t) * width,
        ),
    )(place, image_flat, text_flat, image_w, text_w)


def unit_kernel(count_ref, pooled_ref, own_ref, other_ref, unit_ref, sent_ref, norm_ref):
    both = pooled_ref.shape[0]
    norm = jnp.sqrt(own_ref[...] + other_ref[...] + 1e-06)
    norm_ref[...] = norm
    unit = pooled_ref[...] / norm[:, :1]
    unit_ref[...] = unit
    row = lax.broadcasted_iota(jnp.int32, unit.shape, 0) % (both // 2)
    sent_ref[...] = jnp.where(row < count_ref[0], unit, UNUSABLE).astype(BF16)


def units(count, pooled, own, other):
    return pl.pallas_call(
        unit_kernel,
        out_shape=(
            jax.ShapeDtypeStruct(pooled.shape, F32),
            jax.ShapeDtypeStruct(pooled.shape, BF16),
            jax.ShapeDtypeStruct(own.shape, F32),
        ),
        in_specs=[smem()] + [pl.BlockSpec()] * 3,
        out_specs=(vmem(),) * 3,
        compiler_params=params(4),
    )(count, pooled, own, other)


def stack_kernel(afters, *refs):
    parts, out_ref = refs[afters:-1], refs[-1]
    for n, part in enumerate(parts):
        out_ref[n] = part[...]


def stack(parts, *afters):
    return pl.pallas_call(
        functools.partial(stack_kernel, len(afters)),
        out_shape=jax.ShapeDtypeStruct((len(parts), *parts[0].shape), parts[0].dtype),
        in_specs=[anyplace()] * len(afters) + [vmem()] * len(parts),
        out_specs=vmem(),
        compiler_params=params(4),
    )(*afters, *parts)


def turn_kernel(source_ref, tokens_ref, _, turned_ref, most_ref, turned):
    rows, _ = tokens_ref.shape
    blocks = source_ref.shape[0]
    height = turned_ref.shape[0] // blocks
    largest = None
    for start in range(0, rows, ROWS):
        tokens = tokens_ref[start : start + ROWS, :]
        turned[...] = tokens.T
        most = jnp.max(jnp.abs(tokens).astype(F32), axis=0, keepdims=True)
        largest = most if largest is None else jnp.maximum(largest, most)
        for q in range(blocks):
            source = pl.multiple_of(source_ref[q] * height, height)
            turned_ref[q * height : (q + 1) * height, start : start + ROWS] = turned[
                pl.ds(source, height), :
            ]
    most_ref[...] = jnp.broadcast_to(jnp.max(largest, axis=1, keepdims=True), most_ref.shape)


def turn(sources, flat, after):
    rows, depth = flat.shape
    blocks = sources.shape[0]
    odd = (depth // blocks) % 16
    picked = jnp.arange(16, dtype=jnp.int32) if odd else sources
    turned, most = pl.pallas_call(
        turn_kernel,
        out_shape=(
            jax.ShapeDtypeStruct((depth, rows), flat.dtype),
            jax.ShapeDtypeStruct((8, 128), F32),
        ),
        in_specs=[smem(), vmem(), anyplace()],
        out_specs=(vmem(), vmem()),
        scratch_shapes=[pltpu.VMEM((depth, ROWS), flat.dtype)],
        compiler_params=params(8),
        cost_estimate=pl.CostEstimate(
            flops=0, bytes_accessed=4 * rows * depth, transcendentals=0
        ),
    )(picked, flat, after)
    if odd:
        turned = turned.reshape(blocks, depth // blocks, rows)[sources].reshape(depth, rows)
    return turned, most


def row_products(left, right):
    return lax.dot_general(left, right, (((1,), (1,)), ((), ())), preferred_element_type=F32)


def towers(blocks_ref, samples):
    blocks, _, width = blocks_ref.shape
    image = blocks_ref[:, :samples, :].reshape(blocks * samples, width)
    text = blocks_ref[:, samples:, :].reshape(blocks * samples, width)
    return image, text


def product_kernel(image_most_ref, text_most_ref, *refs):
    *block_refs, out_ref, mark_ref = refs
    near_ref = block_refs[0]
    samples = near_ref.shape[1] // 2
    own_image = near_ref[0, :samples, :]
    own_text = near_ref[0, samples:, :]
    lane = lax.broadcasted_iota(jnp.int32, own_image.shape, 1)
    first = jnp.where(lane == 0, 1.0, 0.0).astype(BF16)
    start = 0
    for ref in block_refs:
        image, text = towers(ref, samples)
        stop = start + image.shape[0]
        found = row_products(jnp.concatenate([own_image, first], axis=0), text)
        out_ref[:samples, start:stop] = found[:samples]
        mark_ref[:, start:stop] = found[samples : samples + 8]
        out_ref[samples:, start:stop] = row_products(own_text, image)
        start = stop


def products(blocks, mosts):
    both = blocks[0].shape[1]
    columns = sum(b.shape[0] for b in blocks) * (both // 2)
    return pl.pallas_call(
        product_kernel,
        out_shape=(
            jax.ShapeDtypeStruct((both, columns), F32),
            jax.ShapeDtypeStruct((8, columns), F32),
        ),
        in_specs=[anyplace()] * 2 + [vmem()] * len(blocks),
        out_specs=(vmem(),) * 2,
        compiler_params=params(8),
    )(*mosts, *blocks)


def middle_kernel(
    tokens_of,
    scale_ref,
    bias_ref,
    gain_ref,
    count_ref,
    own_ref,
    other_ref,
    mark_ref,
    unit_ref,
    norm_ref,
    image_most_ref,
    text_most_ref,
    *refs,
):
    *block_refs, grad_ref, stat_ref = refs
    samples = unit_ref.shape[0] // 2
    scale, bias = scale_ref[0], bias_ref[0]
    dots = own_ref[...] + other_ref[...]
    logits = scale * dots + bias
    row = lax.broadcasted_iota(jnp.int32, dots.shape, 0) % samples
    column = lax.broadcasted_iota(jnp.int32, dots.shape, 1)
    sign = jnp.where(row == column, 1.0, -1.0).astype(F32)
    usable = jnp.where(mark_ref[:1, :] < 1.5, 1.0, 0.0)
    total = jnp.sum(usable, axis=1, keepdims=True)
    used = (usable > 0.5) & (row < count_ref[0])
    margin = -sign * logits
    small = jnp.exp(-jnp.abs(margin))
    soft = jnp.maximum(margin, 0.0) + jnp.log1p(small)
    sigmoid = jnp.where(margin >= 0, 1.0, small) / (1.0 + small)
    part = jnp.where(used, soft, 0.0)[:samples, :]
    loss = jnp.sum(jnp.sum(part, axis=1, keepdims=True), axis=0, keepdims=True) / total
    coeff = gain_ref[0] / total
    dlogit = (jnp.where(used, -sign * sigmoid, 0.0) * coeff).astype(BF16)
    radial = scale * jnp.sum(dlogit.astype(F32) * dots, axis=1, keepdims=True)
    raws = [jnp.zeros((samples, unit_ref.shape[1]), F32) for _ in range(2)]
    start = 0
    for ref in block_refs:
        image, text = towers(ref, samples)
        stop = start + image.shape[0]
        raws[0] += jnp.dot(dlogit[:samples, start:stop], text, preferred_element_type=F32)
        raws[1] += jnp.dot(dlogit[samples:, start:stop], image, preferred_element_type=F32)
        start = stop
    limits = []
    for n, most_ref in enumerate((image_most_ref, text_most_ref)):
        here = slice(n * samples, (n + 1) * samples)
        inward = unit_ref[here, :] * radial[here, :]
        grad = (scale * raws[n] - inward) / norm_ref[here, :1] / tokens_of[n]
        grad_ref[here, :] = grad
        steep = jnp.max(jnp.max(jnp.abs(grad), axis=1, keepdims=True), axis=0, keepdims=True)
        limits.append(1.2 * samples * tokens_of[n] * most_ref[:1, :1] * steep)
    line = lax.broadcasted_iota(jnp.int32, stat_ref.shape, 0)
    stat_ref[...] = jnp.where(line == 0, loss, jnp.where(line == 1, limits[0], limits[1]))


def middle(tokens_of, scale, bias, gain, count, own, other, mark, unit, norm, mosts, blocks):
    return pl.pallas_call(
        functools.partial(middle_kernel, tokens_of),
        out_shape=(
            jax.ShapeDtypeStruct(unit.shape, F32),
            jax.ShapeDtypeStruct((8, unit.shape[1]), F32),
        ),
        in_specs=[smem()] * 4 + [vmem()] * (7 + len(blocks)),
        out_specs=(vmem(), vmem()),
        compiler_params=params(12),
    )(scale, bias, gain, count, own, other, mark, unit, norm, *mosts, *blocks)


def weight_kernel(
    base, carries, grad_ref, slope_ref, turned_ref, stat_ref, _, soon_ref, late_ref, keep_ref, preact_grad
):
    rows, width = slope_ref.shape
    samples = grad_ref.shape[0] // 2
    tok = rows // samples
    for sample in range(samples):
        here = slice(sample * tok, (sample + 1) * tok)
        row = base * samples + sample
        for column in range(0, width, 128):
            columns = slice(column, column + 128)
            slope = slope_ref[here, columns]
            preact_grad[here, columns] = (grad_ref[row : row + 1, columns] * slope).astype(BF16)
    height = late_ref.shape[0]
    if carries:
        soon_ref[height:, :] = stat_ref[...]
    for n, (out, start) in enumerate(
        ((soon_ref, 0), (late_ref, 0), (keep_ref, 0), (keep_ref, height))
    ):
        out[start : start + height, :] = jnp.dot(
            turned_ref[n * height : (n + 1) * height, :],
            preact_grad[...],
            preferred_element_type=F32,
        )


def weight_terms(grad, slope, turned, stat, base, carries, after):
    depth, rows = turned.shape
    width = slope.shape[1]
    quarter = depth // 4
    soon = quarter + (stat.shape[0] if carries else 0)
    return pl.pallas_call(
        functools.partial(weight_kernel, base, carries),
        out_shape=tuple(jax.ShapeDtypeStruct((n, width), F32) for n in (soon, quarter, 2 * quarter)),
        in_specs=[vmem()] * 4 + [anyplace()],
        out_specs=(vmem(),) * 3,
        scratch_shapes=[pltpu.VMEM((rows, width), BF16)],
        compiler_params=params(8),
        cost_estimate=pl.CostEstimate(
            flops=2 * depth * rows * width,
            bytes_accessed=2 * depth * rows + 4 * rows * width + 4 * depth * width,
            transcendentals=0,
        ),
    )(grad, slope, turned, stat, after)


def sum_of(terms):
    total = None
    for term, unit in terms:
        value = term if unit is None else term.astype(F32) * unit
        total = value if total is None else total + value
    return total


def body(
    image_tokens,
    text_tokens,
    image_weight,
    text_weight,
    logit_scale,
    logit_bias,
    loss_scale,
    valid_count,
):
    samples, image_tok, depth = image_tokens.shape
    text_tok = text_tokens.shape[1]
    width = image_weight.shape[1]
    cycle = lax.axis_size("dp")
    bits = cycle.bit_length() - 1
    place = lax.axis_index("dp")

    def swap(array, mask):
        return lax.ppermute(array, "dp", [(i, i ^ mask) for i in range(cycle)])

    def swap_halves(array):
        return lax.ppermute(array, "mp", [(0, 1), (1, 0)])

    def bits_of(value, order):
        return sum(((value >> (len(order) - 1 - i)) & 1) << b for i, b in enumerate(order))

    image_flat = image_tokens.reshape(-1, depth)
    text_flat = text_tokens.reshape(-1, depth)
    text_orders = [list(range(2, bits)), list(range(3, bits)) + [2]]
    image_order = [2, 1] + list(range(3, bits))
    later = [(c, q) for c in range(2) for q in range(cycle // 4)]
    text_blocks = [
        2 * (high + bits_of(q, text_orders[c])) + c for high in (3, 1, 0, 2) for c, q in later
    ]
    image_blocks = [
        high + bits_of(q, image_order[1:])
        for high in (5, 1, 0, 4)
        for q in range(cycle // 4)
    ]
    text_blocks = jnp.asarray(text_blocks, jnp.int32) ^ (2 * place)
    image_blocks = jnp.asarray(image_blocks, jnp.int32) ^ place

    model_place = lax.axis_index("mp").astype(jnp.int32).reshape(1)
    pooled, square, image_slope, text_slope = forward(
        model_place, image_flat, text_flat, image_weight, text_weight, samples
    )
    unit, sent, norm = units(valid_count, pooled, square, swap_halves(square))

    low = max(bits - 2, 1)
    tops = [1 << b for b in reversed(range(low, bits))]
    masks = [tops[0] | tops[1], *tops] if len(tops) == 2 else tops
    arrived = [swap(sent, mask) for mask in masks]
    image_turned, image_most = turn(image_blocks, image_flat, sent)
    gathered = stack([sent] + arrived, image_most)
    text_turned, text_most = turn(text_blocks, text_flat, gathered)
    blocks = [gathered]
    for b in reversed(range(1, low)):
        blocks = blocks + [swap(block, 1 << b) for block in blocks]
    far = [swap(block, 1) for block in blocks[:1]]
    for block in blocks[1:]:
        far.append(swap(stack([block], text_most)[0], 1))
    blocks = blocks + far

    own_dots, mark = products(blocks, (image_most, text_most))
    grad, stat = middle(
        (image_tok, text_tok),
        logit_scale,
        logit_bias,
        loss_scale,
        valid_count,
        own_dots,
        swap_halves(own_dots),
        mark,
        unit,
        norm,
        (image_most, text_most),
        blocks,
    )

    lines = lax.broadcasted_iota(jnp.int32, (FOOT, width), 0)

    def footer(exponents, stat):
        rows = list(exponents)
        rest = stat[:1]
        for _ in range(3):
            part = lax.reduce_precision(rest, 5, 10)
            rows.append(part)
            rest = (rest - part) * 2048.0
        found = jnp.zeros((FOOT, width), F32)
        for n, row in enumerate(rows):
            found = jnp.where(lines == n, row, found)
        return found

    def exponents_of(stat):
        return [jnp.ceil(jnp.log2(jnp.maximum(stat[n : n + 1], 1e-30))) for n in (1, 2)]

    def merged(stat, message):
        foot = message[-FOOT:].astype(F32)
        loss = (foot[4:5] / 2048.0 + foot[3:4]) / 2048.0 + foot[2:3]
        there = [foot[:1], foot[1:2]]
        add = [loss, jnp.exp2(there[0]), jnp.exp2(there[1])]
        total = [stat[n : n + 1] + row for n, row in enumerate(add)]
        return jnp.concatenate(total), there

    def halves(terms):
        half = terms[0][0].shape[0] // 2
        return [[(term[rows], unit) for term, unit in terms] for rows in (slice(half), slice(half, None))]

    def leave(terms, stat, tower, bit, after):
        rows = terms[0][0].shape[0]
        exponents = exponents_of(stat)
        factor = HALF_MAX * jnp.exp2(-exponents[tower]) + 0.0 * after[:1].astype(F32)
        coded = sum_of(terms) * factor
        foot = footer(exponents, stat) + 0.0 * coded[:1]
        coded = jnp.pad(coded, ((0, FOOT), (0, 0))) + jnp.pad(foot, ((rows, 0), (0, 0)))
        coded = coded.astype(jnp.float16)
        return coded, swap(coded, 1 << bit)

    def take(terms, stat, tower, coming):
        stat, there = merged(stat, coming)
        return terms + [(coming[:-FOOT], jnp.exp2(there[tower]) / HALF_MAX)], stat

    def core_step(soon, late, keep):
        height = late.shape[0]
        there = swap(soon, 1)
        stays = [(keep[:height], None), (swap(late, 1), None)]
        return stays, [(keep[height:], None), (there[:height], None)], there[height:]

    text_terms = weight_terms(grad, text_slope, text_turned, stat, 1, True, stat)
    text, text_leaves, stat_there = core_step(*text_terms)
    start_stat = stat[:3] + stat_there[:3]
    image_terms = weight_terms(grad, image_slope, image_turned, stat, 0, False, text_terms[0])
    image, image_leaves, _ = core_step(*image_terms)

    coded, text_in = leave(text_leaves, start_stat, 1, 1, start_stat)
    coded, image_in = leave(image_leaves, start_stat, 0, image_order[0], coded)
    text, text_stat = take(text, start_stat, 1, text_in)
    parts = [(terms, text_stat) for terms in halves(text)]
    image, image_stat = take(image, start_stat, 0, image_in)
    for step in range(bits - 2):
        image, image_leaves = halves(image)
        arrivals, before = [], coded
        for order, (terms, terms_stat) in zip(text_orders, parts):
            terms, leaves = halves(terms)
            last, arrival = leave(leaves, terms_stat, 1, order[step], before)
            before = last if step == 0 else before
            arrivals.append((terms, terms_stat, arrival))
        coded, image_in = leave(image_leaves, image_stat, 0, image_order[step + 1], before)
        parts = [take(terms, old, 1, arrival) for terms, old, arrival in arrivals]
        image, image_stat = take(image, image_stat, 0, image_in)
    row = 0.0 * coded[:1].astype(F32)
    text = jnp.concatenate([sum_of(terms) + row for terms, _ in parts])
    loss = jnp.max(parts[0][1][:1] + row)
    return (loss, sum_of(image), text)


def solution(mesh):
    placed = (
        P("dp", None, None),
        P("dp", None, None),
        P(None, "mp"),
        P(None, "mp"),
        P(),
        P(),
        P(),
        P("dp"),
    )
    return jax.shard_map(
        body,
        mesh=mesh,
        in_specs=placed,
        out_specs=(P(), P("dp", "mp"), P("dp", "mp")),
        check_vma=False,
    )
```

```python
import functools

import jax
import jax.numpy as jnp
from jax import lax
from jax.experimental import pallas as pl
from jax.experimental.pallas import tpu as pltpu
from jax.sharding import PartitionSpec as P

F32 = jnp.float32
BF16 = jnp.bfloat16
ROWS = 256
JOB_ROWS = 256
JOB_COLUMNS = 256
STRIP = 64
ROOT = 0.7978845608028654
HALF_MAX = 16384.0
FOOT = 8
UNUSABLE = 2.0


def vmem():
    return pl.BlockSpec(memory_space=pltpu.VMEM)


def smem():
    return pl.BlockSpec(memory_space=pltpu.SMEM)


def anyplace():
    return pl.BlockSpec(memory_space=pl.ANY)


def hbm():
    return pl.BlockSpec(memory_space=pltpu.HBM)


def params(mib):
    return pltpu.CompilerParams(vmem_limit_bytes=mib * 2**20)


def gelu_and_slope(x):
    square = x * x
    cdf = 0.5 + 0.5 * jnp.tanh(x * (ROOT + (0.044715 * ROOT) * square))
    value = x * cdf
    rise = (value - value * cdf) * (2 * ROOT + (6 * 0.044715 * ROOT) * square)
    return value, cdf + rise


def forward_kernel(
    tokens_of,
    place_ref,
    image_hbm,
    text_hbm,
    image_w_hbm,
    text_w_hbm,
    pooled_ref,
    square_ref,
    image_slope_hbm,
    text_slope_hbm,
    image_v,
    text_v,
    image_w,
    text_w,
    image_slope,
    text_slope,
    even,
    odd,
    in_sem,
    w_sem,
    out_sem,
):
    width = image_w.shape[1]
    samples = pooled_ref.shape[0] // 2
    towers_here = (
        (text_hbm, text_v, text_w_hbm, text_w, text_slope, text_slope_hbm, tokens_of[1], samples),
        (image_hbm, image_v, image_w_hbm, image_w, image_slope, image_slope_hbm, tokens_of[0], 0),
    )
    waits, tiles = [], []
    for t, (source, buf, w_source, w, _, _, _, _) in enumerate(towers_here):
        here = [
            pltpu.make_async_copy(w_source, w, w_sem.at[t]),
            pltpu.make_async_copy(source, buf, in_sem.at[t]),
        ]
        for copy in here:
            copy.start()
        waits.append(here)
        for start in range(0, buf.shape[0], JOB_ROWS):
            for column in range(0, width, JOB_COLUMNS):
                tiles.append((t, start, column))
    first = place_ref[0] * width

    def project(n):
        t, start, column = tiles[n]
        _, buf, _, w, _, _, _, _ = towers_here[t]
        if start == 0 and column == 0:
            for copy in waits[t]:
                copy.wait()
        rows, columns = slice(start, start + JOB_ROWS), slice(column, column + JOB_COLUMNS)
        target = (even, odd)[n % 2]
        target[...] = jnp.dot(buf[rows, :], w[:, columns], preferred_element_type=F32)

    out_copies = []
    project(0)
    for n, (t, start, tile_column) in enumerate(tiles):
        _, buf, _, _, slope, slope_out, tok, base = towers_here[t]
        if n + 1 < len(tiles):
            project(n + 1)
        for row in range(start, start + JOB_ROWS, STRIP):
            rows = slice(row, row + STRIP)
            here = (rows, slice(tile_column, tile_column + JOB_COLUMNS))
            token_columns = pl.ds(pl.multiple_of(first + tile_column, 128), JOB_COLUMNS)
            preact = (even, odd)[n % 2][row - start : row - start + STRIP, :]
            value, slant = gelu_and_slope(preact)
            slope[here] = slant
            hidden = buf[rows, token_columns].astype(F32) + value
            for part in range(0, STRIP, tok):
                sample = base + (row + part) // tok
                pooled_ref[sample : sample + 1, here[1]] = (
                    jnp.sum(hidden[part : part + tok], axis=0, keepdims=True) / tok
                )
        if tile_column + JOB_COLUMNS == width:
            part = pl.ds(start, JOB_ROWS)
            copy = pltpu.make_async_copy(
                slope.at[part, :], slope_out.at[part, :], out_sem.at[len(out_copies)]
            )
            copy.start()
            out_copies.append(copy)
    pooled = pooled_ref[...]
    total = jnp.sum(pooled * pooled, axis=1, keepdims=True)
    square_ref[...] = jnp.broadcast_to(total, square_ref.shape)
    for copy in out_copies:
        copy.wait()


def forward(place, image_flat, text_flat, image_w, text_w, samples):
    width = image_w.shape[1]
    depth = image_w.shape[0]
    rows_i, rows_t = image_flat.shape[0], text_flat.shape[0]
    jobs = (rows_i + rows_t) // JOB_ROWS
    return pl.pallas_call(
        functools.partial(forward_kernel, (rows_i // samples, rows_t // samples)),
        out_shape=(
            jax.ShapeDtypeStruct((2 * samples, width), F32),
            jax.ShapeDtypeStruct((2 * samples, 128), F32),
            jax.ShapeDtypeStruct((rows_i, width), F32),
            jax.ShapeDtypeStruct((rows_t, width), F32),
        ),
        in_specs=[smem()] + [hbm()] * 4,
        out_specs=(vmem(), vmem(), hbm(), hbm()),
        scratch_shapes=[
            pltpu.VMEM((rows_i, depth), BF16),
            pltpu.VMEM((rows_t, depth), BF16),
            pltpu.VMEM((depth, width), BF16),
            pltpu.VMEM((depth, width), BF16),
            pltpu.VMEM((rows_i, width), F32),
            pltpu.VMEM((rows_t, width), F32),
            pltpu.VMEM((JOB_ROWS, JOB_COLUMNS), F32),
            pltpu.VMEM((JOB_ROWS, JOB_COLUMNS), F32),
            pltpu.SemaphoreType.DMA((2,)),
            pltpu.SemaphoreType.DMA((2,)),
            pltpu.SemaphoreType.DMA((jobs,)),
        ],
        compiler_params=params(53),
        cost_estimate=pl.CostEstimate(
            flops=2 * (rows_i + rows_t) * depth * width,
            bytes_accessed=2 * (rows_i + rows_t) * (depth + 2 * width) + 4 * depth * width,
            transcendentals=(rows_i + rows_t) * width,
        ),
    )(place, image_flat, text_flat, image_w, text_w)


def unit_kernel(count_ref, pooled_ref, own_ref, other_ref, unit_ref, sent_ref, norm_ref):
    both = pooled_ref.shape[0]
    norm = jnp.sqrt(own_ref[...] + other_ref[...] + 1e-06)
    norm_ref[...] = norm
    unit = pooled_ref[...] / norm[:, :1]
    unit_ref[...] = unit
    row = lax.broadcasted_iota(jnp.int32, unit.shape, 0) % (both // 2)
    sent_ref[...] = jnp.where(row < count_ref[0], unit, UNUSABLE).astype(BF16)


def units(count, pooled, own, other):
    return pl.pallas_call(
        unit_kernel,
        out_shape=(
            jax.ShapeDtypeStruct(pooled.shape, F32),
            jax.ShapeDtypeStruct(pooled.shape, BF16),
            jax.ShapeDtypeStruct(own.shape, F32),
        ),
        in_specs=[smem()] + [pl.BlockSpec()] * 3,
        out_specs=(vmem(),) * 3,
        compiler_params=params(4),
    )(count, pooled, own, other)


def stack_kernel(afters, *refs):
    parts, out_ref = refs[afters:-1], refs[-1]
    for n, part in enumerate(parts):
        out_ref[n] = part[...]


def stack(parts, *afters):
    return pl.pallas_call(
        functools.partial(stack_kernel, len(afters)),
        out_shape=jax.ShapeDtypeStruct((len(parts), *parts[0].shape), parts[0].dtype),
        in_specs=[anyplace()] * len(afters) + [vmem()] * len(parts),
        out_specs=vmem(),
        compiler_params=params(4),
    )(*afters, *parts)


def turn_kernel(source_ref, tokens_ref, _, turned_ref, most_ref, turned):
    rows, _ = tokens_ref.shape
    blocks = source_ref.shape[0]
    height = turned_ref.shape[0] // blocks
    largest = None
    for start in range(0, rows, ROWS):
        tokens = tokens_ref[start : start + ROWS, :]
        turned[...] = tokens.T
        most = jnp.max(jnp.abs(tokens).astype(F32), axis=0, keepdims=True)
        largest = most if largest is None else jnp.maximum(largest, most)
        for q in range(blocks):
            source = pl.multiple_of(source_ref[q] * height, height)
            turned_ref[q * height : (q + 1) * height, start : start + ROWS] = turned[
                pl.ds(source, height), :
            ]
    most_ref[...] = jnp.broadcast_to(jnp.max(largest, axis=1, keepdims=True), most_ref.shape)


def turn(sources, flat, after):
    rows, depth = flat.shape
    blocks = sources.shape[0]
    odd = (depth // blocks) % 16
    picked = jnp.arange(16, dtype=jnp.int32) if odd else sources
    turned, most = pl.pallas_call(
        turn_kernel,
        out_shape=(
            jax.ShapeDtypeStruct((depth, rows), flat.dtype),
            jax.ShapeDtypeStruct((8, 128), F32),
        ),
        in_specs=[smem(), vmem(), anyplace()],
        out_specs=(vmem(), vmem()),
        scratch_shapes=[pltpu.VMEM((depth, ROWS), flat.dtype)],
        compiler_params=params(8),
        cost_estimate=pl.CostEstimate(
            flops=0, bytes_accessed=4 * rows * depth, transcendentals=0
        ),
    )(picked, flat, after)
    if odd:
        turned = turned.reshape(blocks, depth // blocks, rows)[sources].reshape(depth, rows)
    return turned, most


def row_products(left, right):
    return lax.dot_general(left, right, (((1,), (1,)), ((), ())), preferred_element_type=F32)


def towers(blocks_ref, samples):
    blocks, _, width = blocks_ref.shape
    image = blocks_ref[:, :samples, :].reshape(blocks * samples, width)
    text = blocks_ref[:, samples:, :].reshape(blocks * samples, width)
    return image, text


def product_kernel(image_most_ref, text_most_ref, *refs):
    *block_refs, out_ref, mark_ref = refs
    near_ref = block_refs[0]
    samples = near_ref.shape[1] // 2
    own_image = near_ref[0, :samples, :]
    own_text = near_ref[0, samples:, :]
    lane = lax.broadcasted_iota(jnp.int32, own_image.shape, 1)
    first = jnp.where(lane == 0, 1.0, 0.0).astype(BF16)
    start = 0
    for ref in block_refs:
        image, text = towers(ref, samples)
        stop = start + image.shape[0]
        found = row_products(jnp.concatenate([own_image, first], axis=0), text)
        out_ref[:samples, start:stop] = found[:samples]
        mark_ref[:, start:stop] = found[samples : samples + 8]
        out_ref[samples:, start:stop] = row_products(own_text, image)
        start = stop


def products(blocks, mosts):
    both = blocks[0].shape[1]
    columns = sum(b.shape[0] for b in blocks) * (both // 2)
    return pl.pallas_call(
        product_kernel,
        out_shape=(
            jax.ShapeDtypeStruct((both, columns), F32),
            jax.ShapeDtypeStruct((8, columns), F32),
        ),
        in_specs=[anyplace()] * 2 + [vmem()] * len(blocks),
        out_specs=(vmem(),) * 2,
        compiler_params=params(8),
    )(*mosts, *blocks)


def middle_kernel(
    tokens_of,
    scale_ref,
    bias_ref,
    gain_ref,
    count_ref,
    own_ref,
    other_ref,
    mark_ref,
    unit_ref,
    norm_ref,
    image_most_ref,
    text_most_ref,
    *refs,
):
    *block_refs, grad_ref, stat_ref = refs
    samples = unit_ref.shape[0] // 2
    scale, bias = scale_ref[0], bias_ref[0]
    dots = own_ref[...] + other_ref[...]
    logits = scale * dots + bias
    row = lax.broadcasted_iota(jnp.int32, dots.shape, 0) % samples
    column = lax.broadcasted_iota(jnp.int32, dots.shape, 1)
    sign = jnp.where(row == column, 1.0, -1.0).astype(F32)
    usable = jnp.where(mark_ref[:1, :] < 1.5, 1.0, 0.0)
    total = jnp.sum(usable, axis=1, keepdims=True)
    used = (usable > 0.5) & (row < count_ref[0])
    margin = -sign * logits
    small = jnp.exp(-jnp.abs(margin))
    soft = jnp.maximum(margin, 0.0) + jnp.log1p(small)
    sigmoid = jnp.where(margin >= 0, 1.0, small) / (1.0 + small)
    part = jnp.where(used, soft, 0.0)[:samples, :]
    loss = jnp.sum(jnp.sum(part, axis=1, keepdims=True), axis=0, keepdims=True) / total
    coeff = gain_ref[0] / total
    dlogit = (jnp.where(used, -sign * sigmoid, 0.0) * coeff).astype(BF16)
    radial = scale * jnp.sum(dlogit.astype(F32) * dots, axis=1, keepdims=True)
    raws = [jnp.zeros((samples, unit_ref.shape[1]), F32) for _ in range(2)]
    start = 0
    for ref in block_refs:
        image, text = towers(ref, samples)
        stop = start + image.shape[0]
        raws[0] += jnp.dot(dlogit[:samples, start:stop], text, preferred_element_type=F32)
        raws[1] += jnp.dot(dlogit[samples:, start:stop], image, preferred_element_type=F32)
        start = stop
    limits = []
    for n, most_ref in enumerate((image_most_ref, text_most_ref)):
        here = slice(n * samples, (n + 1) * samples)
        inward = unit_ref[here, :] * radial[here, :]
        grad = (scale * raws[n] - inward) / norm_ref[here, :1] / tokens_of[n]
        grad_ref[here, :] = grad
        steep = jnp.max(jnp.max(jnp.abs(grad), axis=1, keepdims=True), axis=0, keepdims=True)
        limits.append(1.2 * samples * tokens_of[n] * most_ref[:1, :1] * steep)
    line = lax.broadcasted_iota(jnp.int32, stat_ref.shape, 0)
    stat_ref[...] = jnp.where(line == 0, loss, jnp.where(line == 1, limits[0], limits[1]))


def middle(tokens_of, scale, bias, gain, count, own, other, mark, unit, norm, mosts, blocks):
    return pl.pallas_call(
        functools.partial(middle_kernel, tokens_of),
        out_shape=(
            jax.ShapeDtypeStruct(unit.shape, F32),
            jax.ShapeDtypeStruct((8, unit.shape[1]), F32),
        ),
        in_specs=[smem()] * 4 + [vmem()] * (7 + len(blocks)),
        out_specs=(vmem(), vmem()),
        compiler_params=params(12),
    )(scale, bias, gain, count, own, other, mark, unit, norm, *mosts, *blocks)


def weight_kernel(
    base, carries, grad_ref, slope_ref, turned_ref, stat_ref, _, soon_ref, late_ref, keep_ref, preact_grad
):
    rows, width = slope_ref.shape
    samples = grad_ref.shape[0] // 2
    tok = rows // samples
    for sample in range(samples):
        here = slice(sample * tok, (sample + 1) * tok)
        row = base * samples + sample
        for column in range(0, width, 128):
            columns = slice(column, column + 128)
            slope = slope_ref[here, columns]
            preact_grad[here, columns] = (grad_ref[row : row + 1, columns] * slope).astype(BF16)
    height = late_ref.shape[0]
    if carries:
        soon_ref[height:, :] = stat_ref[...]
    for n, (out, start) in enumerate(
        ((soon_ref, 0), (late_ref, 0), (keep_ref, 0), (keep_ref, height))
    ):
        out[start : start + height, :] = jnp.dot(
            turned_ref[n * height : (n + 1) * height, :],
            preact_grad[...],
            preferred_element_type=F32,
        )


def weight_terms(grad, slope, turned, stat, base, carries, after):
    depth, rows = turned.shape
    width = slope.shape[1]
    quarter = depth // 4
    soon = quarter + (stat.shape[0] if carries else 0)
    return pl.pallas_call(
        functools.partial(weight_kernel, base, carries),
        out_shape=tuple(jax.ShapeDtypeStruct((n, width), F32) for n in (soon, quarter, 2 * quarter)),
        in_specs=[vmem()] * 4 + [anyplace()],
        out_specs=(vmem(),) * 3,
        scratch_shapes=[pltpu.VMEM((rows, width), BF16)],
        compiler_params=params(8),
        cost_estimate=pl.CostEstimate(
            flops=2 * depth * rows * width,
            bytes_accessed=2 * depth * rows + 4 * rows * width + 4 * depth * width,
            transcendentals=0,
        ),
    )(grad, slope, turned, stat, after)


def sum_of(terms):
    total = None
    for term, unit in terms:
        value = term if unit is None else term.astype(F32) * unit
        total = value if total is None else total + value
    return total


def body(
    image_tokens,
    text_tokens,
    image_weight,
    text_weight,
    logit_scale,
    logit_bias,
    loss_scale,
    valid_count,
):
    samples, image_tok, depth = image_tokens.shape
    text_tok = text_tokens.shape[1]
    width = image_weight.shape[1]
    cycle = lax.axis_size("dp")
    bits = cycle.bit_length() - 1
    place = lax.axis_index("dp")

    def swap(array, mask):
        return lax.ppermute(array, "dp", [(i, i ^ mask) for i in range(cycle)])

    def swap_halves(array):
        return lax.ppermute(array, "mp", [(0, 1), (1, 0)])

    def bits_of(value, order):
        return sum(((value >> (len(order) - 1 - i)) & 1) << b for i, b in enumerate(order))

    image_flat = image_tokens.reshape(-1, depth)
    text_flat = text_tokens.reshape(-1, depth)
    text_orders = [list(range(2, bits)), list(range(3, bits)) + [2]]
    image_order = [2, 1] + list(range(3, bits))
    later = [(c, q) for c in range(2) for q in range(cycle // 4)]
    text_blocks = [
        2 * (high + bits_of(q, text_orders[c])) + c for high in (3, 1, 0, 2) for c, q in later
    ]
    image_blocks = [
        high + bits_of(q, image_order[1:])
        for high in (5, 1, 0, 4)
        for q in range(cycle // 4)
    ]
    text_blocks = jnp.asarray(text_blocks, jnp.int32) ^ (2 * place)
    image_blocks = jnp.asarray(image_blocks, jnp.int32) ^ place

    model_place = lax.axis_index("mp").astype(jnp.int32).reshape(1)
    pooled, square, image_slope, text_slope = forward(
        model_place, image_flat, text_flat, image_weight, text_weight, samples
    )
    unit, sent, norm = units(valid_count, pooled, square, swap_halves(square))

    low = max(bits - 2, 1)
    tops = [1 << b for b in reversed(range(low, bits))]
    masks = [tops[0] | tops[1], *tops] if len(tops) == 2 else tops
    arrived = [swap(sent, mask) for mask in masks]
    image_turned, image_most = turn(image_blocks, image_flat, sent)
    gathered = stack([sent] + arrived, image_most)
    text_turned, text_most = turn(text_blocks, text_flat, gathered)
    blocks = [gathered]
    for b in reversed(range(1, low)):
        blocks = blocks + [swap(block, 1 << b) for block in blocks]
    far = [swap(block, 1) for block in blocks[:1]]
    for block in blocks[1:]:
        far.append(swap(stack([block], text_most)[0], 1))
    blocks = blocks + far

    own_dots, mark = products(blocks, (image_most, text_most))
    grad, stat = middle(
        (image_tok, text_tok),
        logit_scale,
        logit_bias,
        loss_scale,
        valid_count,
        own_dots,
        swap_halves(own_dots),
        mark,
        unit,
        norm,
        (image_most, text_most),
        blocks,
    )

    lines = lax.broadcasted_iota(jnp.int32, (FOOT, width), 0)

    def footer(exponents, stat):
        rows = list(exponents)
        rest = stat[:1]
        for _ in range(3):
            part = lax.reduce_precision(rest, 5, 10)
            rows.append(part)
            rest = (rest - part) * 2048.0
        found = jnp.zeros((FOOT, width), F32)
        for n, row in enumerate(rows):
            found = jnp.where(lines == n, row, found)
        return found

    def exponents_of(stat):
        return [jnp.ceil(jnp.log2(jnp.maximum(stat[n : n + 1], 1e-30))) for n in (1, 2)]

    def merged(stat, message):
        foot = message[-FOOT:].astype(F32)
        loss = (foot[4:5] / 2048.0 + foot[3:4]) / 2048.0 + foot[2:3]
        there = [foot[:1], foot[1:2]]
        add = [loss, jnp.exp2(there[0]), jnp.exp2(there[1])]
        total = [stat[n : n + 1] + row for n, row in enumerate(add)]
        return jnp.concatenate(total), there

    def halves(terms):
        half = terms[0][0].shape[0] // 2
        return [[(term[rows], unit) for term, unit in terms] for rows in (slice(half), slice(half, None))]

    def leave(terms, stat, tower, bit, after):
        rows = terms[0][0].shape[0]
        exponents = exponents_of(stat)
        factor = HALF_MAX * jnp.exp2(-exponents[tower]) + 0.0 * after[:1].astype(F32)
        coded = sum_of(terms) * factor
        foot = footer(exponents, stat) + 0.0 * coded[:1]
        coded = jnp.pad(coded, ((0, FOOT), (0, 0))) + jnp.pad(foot, ((rows, 0), (0, 0)))
        coded = coded.astype(jnp.float16)
        return coded, swap(coded, 1 << bit)

    def take(terms, stat, tower, coming):
        stat, there = merged(stat, coming)
        return terms + [(coming[:-FOOT], jnp.exp2(there[tower]) / HALF_MAX)], stat

    def core_step(soon, late, keep):
        height = late.shape[0]
        there = swap(soon, 1)
        stays = [(keep[:height], None), (swap(late, 1), None)]
        return stays, [(keep[height:], None), (there[:height], None)], there[height:]

    text_terms = weight_terms(grad, text_slope, text_turned, stat, 1, True, stat)
    text, text_leaves, stat_there = core_step(*text_terms)
    start_stat = stat[:3] + stat_there[:3]
    image_terms = weight_terms(grad, image_slope, image_turned, stat, 0, False, text_terms[0])
    image, image_leaves, _ = core_step(*image_terms)

    text_coded, text_in = leave(text_leaves, start_stat, 1, 1, start_stat)
    coded, image_in = leave(image_leaves, start_stat, 0, image_order[0], text_coded)
    _, late, keep = image_terms
    late = late + 0.0 * text_coded[:1].astype(F32)
    image = [(keep[: late.shape[0]], None), (swap(late, 1), None)]
    _, late, keep = text_terms
    late = late + 0.0 * text_coded[:1].astype(F32)
    text = [(keep[: late.shape[0]], None), (swap(late, 1), None)]
    text, text_stat = take(text, start_stat, 1, text_in)
    parts = [(terms, text_stat) for terms in halves(text)]
    image, image_stat = take(image, start_stat, 0, image_in)
    for step in range(bits - 2):
        image, image_leaves = halves(image)
        arrivals, before = [], coded
        for order, (terms, terms_stat) in zip(text_orders, parts):
            terms, leaves = halves(terms)
            last, arrival = leave(leaves, terms_stat, 1, order[step], before)
            before = last if step == 0 else before
            arrivals.append((terms, terms_stat, arrival))
        coded, image_in = leave(image_leaves, image_stat, 0, image_order[step + 1], before)
        parts = [take(terms, old, 1, arrival) for terms, old, arrival in arrivals]
        image, image_stat = take(image, image_stat, 0, image_in)
    row = 0.0 * coded[:1].astype(F32)
    text = jnp.concatenate([sum_of(terms) + row for terms, _ in parts])
    loss = jnp.max(parts[0][1][:1] + row)
    return (loss, sum_of(image), text)


def solution(mesh):
    placed = (
        P("dp", None, None),
        P("dp", None, None),
        P(None, "mp"),
        P(None, "mp"),
        P(),
        P(),
        P(),
        P("dp"),
    )
    return jax.shard_map(
        body,
        mesh=mesh,
        in_specs=placed,
        out_specs=(P(), P("dp", "mp"), P("dp", "mp")),
        check_vma=False,
    )
```

```python
import functools

import jax
import jax.numpy as jnp
from jax import lax
from jax.experimental import pallas as pl
from jax.experimental.pallas import tpu as pltpu
from jax.sharding import PartitionSpec as P

F32 = jnp.float32
BF16 = jnp.bfloat16
ROWS = 256
JOB_ROWS = 256
JOB_COLUMNS = 256
STRIP = 64
ROOT = 0.7978845608028654
HALF_MAX = 16384.0
FOOT = 8
UNUSABLE = 2.0


def vmem():
    return pl.BlockSpec(memory_space=pltpu.VMEM)


def smem():
    return pl.BlockSpec(memory_space=pltpu.SMEM)


def anyplace():
    return pl.BlockSpec(memory_space=pl.ANY)


def hbm():
    return pl.BlockSpec(memory_space=pltpu.HBM)


def params(mib):
    return pltpu.CompilerParams(vmem_limit_bytes=mib * 2**20)


def gelu_and_slope(x):
    square = x * x
    cdf = 0.5 + 0.5 * jnp.tanh(x * (ROOT + (0.044715 * ROOT) * square))
    value = x * cdf
    rise = (value - value * cdf) * (2 * ROOT + (6 * 0.044715 * ROOT) * square)
    return value, cdf + rise


def forward_kernel(
    tokens_of,
    place_ref,
    image_hbm,
    text_hbm,
    image_w_hbm,
    text_w_hbm,
    pooled_ref,
    square_ref,
    image_slope_hbm,
    text_slope_hbm,
    image_v,
    text_v,
    image_w,
    text_w,
    image_slope,
    text_slope,
    even,
    odd,
    in_sem,
    w_sem,
    out_sem,
):
    width = image_w.shape[1]
    samples = pooled_ref.shape[0] // 2
    towers_here = (
        (text_hbm, text_v, text_w_hbm, text_w, text_slope, text_slope_hbm, tokens_of[1], samples),
        (image_hbm, image_v, image_w_hbm, image_w, image_slope, image_slope_hbm, tokens_of[0], 0),
    )
    waits, tiles = [], []
    for t, (source, buf, w_source, w, _, _, _, _) in enumerate(towers_here):
        here = [
            pltpu.make_async_copy(w_source, w, w_sem.at[t]),
            pltpu.make_async_copy(source, buf, in_sem.at[t]),
        ]
        for copy in here:
            copy.start()
        waits.append(here)
        for start in range(0, buf.shape[0], JOB_ROWS):
            for column in range(0, width, JOB_COLUMNS):
                tiles.append((t, start, column))
    first = place_ref[0] * width

    def project(n):
        t, start, column = tiles[n]
        _, buf, _, w, _, _, _, _ = towers_here[t]
        if start == 0 and column == 0:
            for copy in waits[t]:
                copy.wait()
        rows, columns = slice(start, start + JOB_ROWS), slice(column, column + JOB_COLUMNS)
        target = (even, odd)[n % 2]
        target[...] = jnp.dot(buf[rows, :], w[:, columns], preferred_element_type=F32)

    out_copies = []
    project(0)
    for n, (t, start, tile_column) in enumerate(tiles):
        _, buf, _, _, slope, slope_out, tok, base = towers_here[t]
        if n + 1 < len(tiles):
            project(n + 1)
        for row in range(start, start + JOB_ROWS, STRIP):
            rows = slice(row, row + STRIP)
            here = (rows, slice(tile_column, tile_column + JOB_COLUMNS))
            token_columns = pl.ds(pl.multiple_of(first + tile_column, 128), JOB_COLUMNS)
            preact = (even, odd)[n % 2][row - start : row - start + STRIP, :]
            value, slant = gelu_and_slope(preact)
            slope[here] = slant
            hidden = buf[rows, token_columns].astype(F32) + value
            for part in range(0, STRIP, tok):
                sample = base + (row + part) // tok
                pooled_ref[sample : sample + 1, here[1]] = (
                    jnp.sum(hidden[part : part + tok], axis=0, keepdims=True) / tok
                )
        if tile_column + JOB_COLUMNS == width:
            part = pl.ds(start, JOB_ROWS)
            copy = pltpu.make_async_copy(
                slope.at[part, :], slope_out.at[part, :], out_sem.at[len(out_copies)]
            )
            copy.start()
            out_copies.append(copy)
    pooled = pooled_ref[...]
    total = jnp.sum(pooled * pooled, axis=1, keepdims=True)
    square_ref[...] = jnp.broadcast_to(total, square_ref.shape)
    for copy in out_copies:
        copy.wait()


def forward(place, image_flat, text_flat, image_w, text_w, samples):
    width = image_w.shape[1]
    depth = image_w.shape[0]
    rows_i, rows_t = image_flat.shape[0], text_flat.shape[0]
    jobs = (rows_i + rows_t) // JOB_ROWS
    return pl.pallas_call(
        functools.partial(forward_kernel, (rows_i // samples, rows_t // samples)),
        out_shape=(
            jax.ShapeDtypeStruct((2 * samples, width), F32),
            jax.ShapeDtypeStruct((2 * samples, 128), F32),
            jax.ShapeDtypeStruct((rows_i, width), F32),
            jax.ShapeDtypeStruct((rows_t, width), F32),
        ),
        in_specs=[smem()] + [hbm()] * 4,
        out_specs=(vmem(), vmem(), hbm(), hbm()),
        scratch_shapes=[
            pltpu.VMEM((rows_i, depth), BF16),
            pltpu.VMEM((rows_t, depth), BF16),
            pltpu.VMEM((depth, width), BF16),
            pltpu.VMEM((depth, width), BF16),
            pltpu.VMEM((rows_i, width), F32),
            pltpu.VMEM((rows_t, width), F32),
            pltpu.VMEM((JOB_ROWS, JOB_COLUMNS), F32),
            pltpu.VMEM((JOB_ROWS, JOB_COLUMNS), F32),
            pltpu.SemaphoreType.DMA((2,)),
            pltpu.SemaphoreType.DMA((2,)),
            pltpu.SemaphoreType.DMA((jobs,)),
        ],
        compiler_params=params(53),
        cost_estimate=pl.CostEstimate(
            flops=2 * (rows_i + rows_t) * depth * width,
            bytes_accessed=2 * (rows_i + rows_t) * (depth + 2 * width) + 4 * depth * width,
            transcendentals=(rows_i + rows_t) * width,
        ),
    )(place, image_flat, text_flat, image_w, text_w)


def unit_kernel(count_ref, pooled_ref, own_ref, other_ref, unit_ref, sent_ref, norm_ref):
    both = pooled_ref.shape[0]
    norm = jnp.sqrt(own_ref[...] + other_ref[...] + 1e-06)
    norm_ref[...] = norm
    unit = pooled_ref[...] / norm[:, :1]
    unit_ref[...] = unit
    row = lax.broadcasted_iota(jnp.int32, unit.shape, 0) % (both // 2)
    sent_ref[...] = jnp.where(row < count_ref[0], unit, UNUSABLE).astype(BF16)


def units(count, pooled, own, other):
    return pl.pallas_call(
        unit_kernel,
        out_shape=(
            jax.ShapeDtypeStruct(pooled.shape, F32),
            jax.ShapeDtypeStruct(pooled.shape, BF16),
            jax.ShapeDtypeStruct(own.shape, F32),
        ),
        in_specs=[smem()] + [pl.BlockSpec()] * 3,
        out_specs=(vmem(),) * 3,
        compiler_params=params(4),
    )(count, pooled, own, other)


def stack_kernel(afters, *refs):
    parts, out_ref = refs[afters:-1], refs[-1]
    for n, part in enumerate(parts):
        out_ref[n] = part[...]


def stack(parts, *afters):
    return pl.pallas_call(
        functools.partial(stack_kernel, len(afters)),
        out_shape=jax.ShapeDtypeStruct((len(parts), *parts[0].shape), parts[0].dtype),
        in_specs=[anyplace()] * len(afters) + [vmem()] * len(parts),
        out_specs=vmem(),
        compiler_params=params(4),
    )(*afters, *parts)


def turn_kernel(source_ref, tokens_ref, _, turned_ref, most_ref, turned):
    rows, _ = tokens_ref.shape
    blocks = source_ref.shape[0]
    height = turned_ref.shape[0] // blocks
    largest = None
    for start in range(0, rows, ROWS):
        tokens = tokens_ref[start : start + ROWS, :]
        turned[...] = tokens.T
        most = jnp.max(jnp.abs(tokens).astype(F32), axis=0, keepdims=True)
        largest = most if largest is None else jnp.maximum(largest, most)
        for q in range(blocks):
            source = pl.multiple_of(source_ref[q] * height, height)
            turned_ref[q * height : (q + 1) * height, start : start + ROWS] = turned[
                pl.ds(source, height), :
            ]
    most_ref[...] = jnp.broadcast_to(jnp.max(largest, axis=1, keepdims=True), most_ref.shape)


def turn(sources, flat, after):
    rows, depth = flat.shape
    blocks = sources.shape[0]
    odd = (depth // blocks) % 16
    picked = jnp.arange(16, dtype=jnp.int32) if odd else sources
    turned, most = pl.pallas_call(
        turn_kernel,
        out_shape=(
            jax.ShapeDtypeStruct((depth, rows), flat.dtype),
            jax.ShapeDtypeStruct((8, 128), F32),
        ),
        in_specs=[smem(), vmem(), anyplace()],
        out_specs=(vmem(), vmem()),
        scratch_shapes=[pltpu.VMEM((depth, ROWS), flat.dtype)],
        compiler_params=params(8),
        cost_estimate=pl.CostEstimate(
            flops=0, bytes_accessed=4 * rows * depth, transcendentals=0
        ),
    )(picked, flat, after)
    if odd:
        turned = turned.reshape(blocks, depth // blocks, rows)[sources].reshape(depth, rows)
    return turned, most


def row_products(left, right):
    return lax.dot_general(left, right, (((1,), (1,)), ((), ())), preferred_element_type=F32)


def towers(blocks_ref, samples):
    blocks, _, width = blocks_ref.shape
    image = blocks_ref[:, :samples, :].reshape(blocks * samples, width)
    text = blocks_ref[:, samples:, :].reshape(blocks * samples, width)
    return image, text


def product_kernel(image_most_ref, text_most_ref, *refs):
    *block_refs, out_ref, mark_ref = refs
    near_ref = block_refs[0]
    samples = near_ref.shape[1] // 2
    own_image = near_ref[0, :samples, :]
    own_text = near_ref[0, samples:, :]
    lane = lax.broadcasted_iota(jnp.int32, own_image.shape, 1)
    first = jnp.where(lane == 0, 1.0, 0.0).astype(BF16)
    start = 0
    for ref in block_refs:
        image, text = towers(ref, samples)
        stop = start + image.shape[0]
        found = row_products(jnp.concatenate([own_image, first], axis=0), text)
        out_ref[:samples, start:stop] = found[:samples]
        mark_ref[:, start:stop] = found[samples : samples + 8]
        out_ref[samples:, start:stop] = row_products(own_text, image)
        start = stop


def products(blocks, mosts):
    both = blocks[0].shape[1]
    columns = sum(b.shape[0] for b in blocks) * (both // 2)
    return pl.pallas_call(
        product_kernel,
        out_shape=(
            jax.ShapeDtypeStruct((both, columns), F32),
            jax.ShapeDtypeStruct((8, columns), F32),
        ),
        in_specs=[anyplace()] * 2 + [vmem()] * len(blocks),
        out_specs=(vmem(),) * 2,
        compiler_params=params(8),
    )(*mosts, *blocks)


def middle_kernel(
    tokens_of,
    scale_ref,
    bias_ref,
    gain_ref,
    count_ref,
    own_ref,
    other_ref,
    mark_ref,
    unit_ref,
    norm_ref,
    image_most_ref,
    text_most_ref,
    *refs,
):
    *block_refs, grad_ref, stat_ref = refs
    samples = unit_ref.shape[0] // 2
    scale, bias = scale_ref[0], bias_ref[0]
    dots = own_ref[...] + other_ref[...]
    logits = scale * dots + bias
    row = lax.broadcasted_iota(jnp.int32, dots.shape, 0) % samples
    column = lax.broadcasted_iota(jnp.int32, dots.shape, 1)
    sign = jnp.where(row == column, 1.0, -1.0).astype(F32)
    usable = jnp.where(mark_ref[:1, :] < 1.5, 1.0, 0.0)
    total = jnp.sum(usable, axis=1, keepdims=True)
    used = (usable > 0.5) & (row < count_ref[0])
    margin = -sign * logits
    small = jnp.exp(-jnp.abs(margin))
    soft = jnp.maximum(margin, 0.0) + jnp.log1p(small)
    sigmoid = jnp.where(margin >= 0, 1.0, small) / (1.0 + small)
    part = jnp.where(used, soft, 0.0)[:samples, :]
    loss = jnp.sum(jnp.sum(part, axis=1, keepdims=True), axis=0, keepdims=True) / total
    coeff = gain_ref[0] / total
    dlogit = (jnp.where(used, -sign * sigmoid, 0.0) * coeff).astype(BF16)
    radial = scale * jnp.sum(dlogit.astype(F32) * dots, axis=1, keepdims=True)
    raws = [jnp.zeros((samples, unit_ref.shape[1]), F32) for _ in range(2)]
    start = 0
    for ref in block_refs:
        image, text = towers(ref, samples)
        stop = start + image.shape[0]
        raws[0] += jnp.dot(dlogit[:samples, start:stop], text, preferred_element_type=F32)
        raws[1] += jnp.dot(dlogit[samples:, start:stop], image, preferred_element_type=F32)
        start = stop
    limits = []
    for n, most_ref in enumerate((image_most_ref, text_most_ref)):
        here = slice(n * samples, (n + 1) * samples)
        inward = unit_ref[here, :] * radial[here, :]
        grad = (scale * raws[n] - inward) / norm_ref[here, :1] / tokens_of[n]
        grad_ref[here, :] = grad
        steep = jnp.max(jnp.max(jnp.abs(grad), axis=1, keepdims=True), axis=0, keepdims=True)
        limits.append(1.2 * samples * tokens_of[n] * most_ref[:1, :1] * steep)
    line = lax.broadcasted_iota(jnp.int32, stat_ref.shape, 0)
    stat_ref[...] = jnp.where(line == 0, loss, jnp.where(line == 1, limits[0], limits[1]))


def middle(tokens_of, scale, bias, gain, count, own, other, mark, unit, norm, mosts, blocks):
    return pl.pallas_call(
        functools.partial(middle_kernel, tokens_of),
        out_shape=(
            jax.ShapeDtypeStruct(unit.shape, F32),
            jax.ShapeDtypeStruct((8, unit.shape[1]), F32),
        ),
        in_specs=[smem()] * 4 + [vmem()] * (7 + len(blocks)),
        out_specs=(vmem(), vmem()),
        compiler_params=params(12),
    )(scale, bias, gain, count, own, other, mark, unit, norm, *mosts, *blocks)


def weight_kernel(
    base, carries, grad_ref, slope_ref, turned_ref, stat_ref, _, soon_ref, late_ref, keep_ref, preact_grad
):
    rows, width = slope_ref.shape
    samples = grad_ref.shape[0] // 2
    tok = rows // samples
    for sample in range(samples):
        here = slice(sample * tok, (sample + 1) * tok)
        row = base * samples + sample
        for column in range(0, width, 128):
            columns = slice(column, column + 128)
            slope = slope_ref[here, columns]
            preact_grad[here, columns] = (grad_ref[row : row + 1, columns] * slope).astype(BF16)
    height = late_ref.shape[0]
    if carries:
        soon_ref[height:, :] = stat_ref[...]
    for n, (out, start) in enumerate(
        ((soon_ref, 0), (late_ref, 0), (keep_ref, 0), (keep_ref, height))
    ):
        out[start : start + height, :] = jnp.dot(
            turned_ref[n * height : (n + 1) * height, :],
            preact_grad[...],
            preferred_element_type=F32,
        )


def weight_terms(grad, slope, turned, stat, base, carries, after):
    depth, rows = turned.shape
    width = slope.shape[1]
    quarter = depth // 4
    soon = quarter + (stat.shape[0] if carries else 0)
    return pl.pallas_call(
        functools.partial(weight_kernel, base, carries),
        out_shape=tuple(jax.ShapeDtypeStruct((n, width), F32) for n in (soon, quarter, 2 * quarter)),
        in_specs=[vmem()] * 4 + [anyplace()],
        out_specs=(vmem(),) * 3,
        scratch_shapes=[pltpu.VMEM((rows, width), BF16)],
        compiler_params=params(8),
        cost_estimate=pl.CostEstimate(
            flops=2 * depth * rows * width,
            bytes_accessed=2 * depth * rows + 4 * rows * width + 4 * depth * width,
            transcendentals=0,
        ),
    )(grad, slope, turned, stat, after)


def sum_of(terms):
    total = None
    for term, unit in terms:
        value = term if unit is None else term.astype(F32) * unit
        total = value if total is None else total + value
    return total


def body(
    image_tokens,
    text_tokens,
    image_weight,
    text_weight,
    logit_scale,
    logit_bias,
    loss_scale,
    valid_count,
):
    samples, image_tok, depth = image_tokens.shape
    text_tok = text_tokens.shape[1]
    width = image_weight.shape[1]
    cycle = lax.axis_size("dp")
    bits = cycle.bit_length() - 1
    place = lax.axis_index("dp")

    def swap(array, mask):
        return lax.ppermute(array, "dp", [(i, i ^ mask) for i in range(cycle)])

    def swap_halves(array):
        return lax.ppermute(array, "mp", [(0, 1), (1, 0)])

    def bits_of(value, order):
        return sum(((value >> (len(order) - 1 - i)) & 1) << b for i, b in enumerate(order))

    image_flat = image_tokens.reshape(-1, depth)
    text_flat = text_tokens.reshape(-1, depth)
    text_orders = [list(range(2, bits)), list(range(3, bits)) + [2]]
    image_order = [2, 1] + list(range(3, bits))
    later = [(c, q) for c in range(2) for q in range(cycle // 4)]
    text_blocks = [
        2 * (high + bits_of(q, text_orders[c])) + c for high in (3, 1, 0, 2) for c, q in later
    ]
    image_blocks = [
        high + bits_of(q, image_order[1:])
        for high in (5, 1, 0, 4)
        for q in range(cycle // 4)
    ]
    text_blocks = jnp.asarray(text_blocks, jnp.int32) ^ (2 * place)
    image_blocks = jnp.asarray(image_blocks, jnp.int32) ^ place

    model_place = lax.axis_index("mp").astype(jnp.int32).reshape(1)
    pooled, square, image_slope, text_slope = forward(
        model_place, image_flat, text_flat, image_weight, text_weight, samples
    )
    unit, sent, norm = units(valid_count, pooled, square, swap_halves(square))

    low = max(bits - 2, 1)
    tops = [1 << b for b in reversed(range(low, bits))]
    masks = [tops[0] | tops[1], *tops] if len(tops) == 2 else tops
    arrived = [swap(sent, mask) for mask in masks]
    image_turned, image_most = turn(image_blocks, image_flat, sent)
    gathered = stack([sent] + arrived, image_most)
    text_turned, text_most = turn(text_blocks, text_flat, gathered)
    blocks = [gathered]
    for b in reversed(range(1, low)):
        blocks = blocks + [swap(block, 1 << b) for block in blocks]
    far = [swap(block, 1) for block in blocks[:1]]
    for block in blocks[1:]:
        far.append(swap(stack([block], text_most)[0], 1))
    blocks = blocks + far

    own_dots, mark = products(blocks, (image_most, text_most))
    grad, stat = middle(
        (image_tok, text_tok),
        logit_scale,
        logit_bias,
        loss_scale,
        valid_count,
        own_dots,
        swap_halves(own_dots),
        mark,
        unit,
        norm,
        (image_most, text_most),
        blocks,
    )

    lines = lax.broadcasted_iota(jnp.int32, (FOOT, width), 0)

    def footer(exponents, stat):
        rows = list(exponents)
        rest = stat[:1]
        for _ in range(3):
            part = lax.reduce_precision(rest, 5, 10)
            rows.append(part)
            rest = (rest - part) * 2048.0
        found = jnp.zeros((FOOT, width), F32)
        for n, row in enumerate(rows):
            found = jnp.where(lines == n, row, found)
        return found

    def exponents_of(stat):
        return [jnp.ceil(jnp.log2(jnp.maximum(stat[n : n + 1], 1e-30))) for n in (1, 2)]

    def merged(stat, message):
        foot = message[-FOOT:].astype(F32)
        loss = (foot[4:5] / 2048.0 + foot[3:4]) / 2048.0 + foot[2:3]
        there = [foot[:1], foot[1:2]]
        add = [loss, jnp.exp2(there[0]), jnp.exp2(there[1])]
        total = [stat[n : n + 1] + row for n, row in enumerate(add)]
        return jnp.concatenate(total), there

    def halves(terms):
        half = terms[0][0].shape[0] // 2
        return [[(term[rows], unit) for term, unit in terms] for rows in (slice(half), slice(half, None))]

    def leave(terms, stat, tower, bit, after):
        rows = terms[0][0].shape[0]
        exponents = exponents_of(stat)
        factor = HALF_MAX * jnp.exp2(-exponents[tower]) + 0.0 * after[:1].astype(F32)
        coded = sum_of(terms) * factor
        foot = footer(exponents, stat) + 0.0 * coded[:1]
        coded = jnp.pad(coded, ((0, FOOT), (0, 0))) + jnp.pad(foot, ((rows, 0), (0, 0)))
        coded = coded.astype(jnp.float16)
        return coded, swap(coded, 1 << bit)

    def take(terms, stat, tower, coming):
        stat, there = merged(stat, coming)
        return terms + [(coming[:-FOOT], jnp.exp2(there[tower]) / HALF_MAX)], stat

    def core_step(soon, late, keep):
        height = late.shape[0]
        there = swap(soon, 1)
        stays = [(keep[:height], None), (swap(late, 1), None)]
        return stays, [(keep[height:], None), (there[:height], None)], there[height:]

    text_terms = weight_terms(grad, text_slope, text_turned, stat, 1, True, stat)
    text, text_leaves, stat_there = core_step(*text_terms)
    start_stat = stat[:3] + stat_there[:3]
    image_terms = weight_terms(grad, image_slope, image_turned, stat, 0, False, text_terms[0])
    image, image_leaves, _ = core_step(*image_terms)

    text_coded, text_in = leave(text_leaves, start_stat, 1, 1, start_stat)
    coded, image_in = leave(image_leaves, start_stat, 0, image_order[0], text_coded)
    _, late, keep = image_terms
    late = late + 0.0 * text_coded[:1].astype(F32)
    image = [(keep[: late.shape[0]], None), (swap(late, 1), None)]
    _, late, keep = text_terms
    late = late + 0.0 * text_coded[:1].astype(F32)
    text = [(keep[: late.shape[0]], None), (swap(late, 1), None)]
    text, text_stat = take(text, start_stat, 1, text_in)
    parts = [(terms, text_stat) for terms in halves(text)]
    image, image_stat = take(image, start_stat, 0, image_in)
    for step in range(bits - 2):
        image, image_leaves = halves(image)
        arrivals = [None, None]
        if step < bits - 3:
            terms, leaves = halves(parts[0][0])
            made, arrival = leave(leaves, parts[0][1], 1, text_orders[0][step], coded)
            arrivals[0] = (terms, parts[0][1], arrival)
            terms, leaves = halves(parts[1][0])
            made, arrival = leave(leaves, parts[1][1], 1, text_orders[1][step], made)
            arrivals[1] = (terms, parts[1][1], arrival)
            coded, image_in = leave(image_leaves, image_stat, 0, image_order[step + 1], made)
        else:
            coded, image_in = leave(image_leaves, image_stat, 0, image_order[step + 1], coded)
            terms, leaves = halves(parts[0][0])
            made, arrival = leave(leaves, parts[0][1], 1, text_orders[0][step], coded)
            arrivals[0] = (terms, parts[0][1], arrival)
            terms, leaves = halves(parts[1][0])
            made, arrival = leave(leaves, parts[1][1], 1, text_orders[1][step], made)
            arrivals[1] = (terms, parts[1][1], arrival)
        parts = [take(terms, old, 1, arrival) for terms, old, arrival in arrivals]
        image, image_stat = take(image, image_stat, 0, image_in)
    row = 0.0 * coded[:1].astype(F32)
    text = jnp.concatenate([sum_of(terms) + row for terms, _ in parts])
    loss = jnp.max(parts[0][1][:1] + row)
    return (loss, sum_of(image), text)


def solution(mesh):
    placed = (
        P("dp", None, None),
        P("dp", None, None),
        P(None, "mp"),
        P(None, "mp"),
        P(),
        P(),
        P(),
        P("dp"),
    )
    return jax.shard_map(
        body,
        mesh=mesh,
        in_specs=placed,
        out_specs=(P(), P("dp", "mp"), P("dp", "mp")),
        check_vma=False,
    )
```

```python
import functools

import jax
import jax.numpy as jnp
from jax import lax
from jax.experimental import pallas as pl
from jax.experimental.pallas import tpu as pltpu
from jax.sharding import PartitionSpec as P

F32 = jnp.float32
BF16 = jnp.bfloat16
ROWS = 256
JOB_ROWS = 256
JOB_COLUMNS = 256
STRIP = 64
ROOT = 0.7978845608028654
HALF_MAX = 16384.0
FOOT = 8
UNUSABLE = 2.0


def vmem():
    return pl.BlockSpec(memory_space=pltpu.VMEM)


def smem():
    return pl.BlockSpec(memory_space=pltpu.SMEM)


def anyplace():
    return pl.BlockSpec(memory_space=pl.ANY)


def hbm():
    return pl.BlockSpec(memory_space=pltpu.HBM)


def params(mib):
    return pltpu.CompilerParams(vmem_limit_bytes=mib * 2**20)


def gelu_and_slope(x):
    square = x * x
    cdf = 0.5 + 0.5 * jnp.tanh(x * (ROOT + (0.044715 * ROOT) * square))
    value = x * cdf
    rise = (value - value * cdf) * (2 * ROOT + (6 * 0.044715 * ROOT) * square)
    return value, cdf + rise


def forward_kernel(
    tokens_of,
    place_ref,
    image_hbm,
    text_hbm,
    image_w_hbm,
    text_w_hbm,
    pooled_ref,
    square_ref,
    image_slope_hbm,
    text_slope_hbm,
    image_v,
    text_v,
    image_w,
    text_w,
    image_slope,
    text_slope,
    even,
    odd,
    in_sem,
    w_sem,
    out_sem,
):
    width = image_w.shape[1]
    samples = pooled_ref.shape[0] // 2
    towers_here = (
        (text_hbm, text_v, text_w_hbm, text_w, text_slope, text_slope_hbm, tokens_of[1], samples),
        (image_hbm, image_v, image_w_hbm, image_w, image_slope, image_slope_hbm, tokens_of[0], 0),
    )
    waits, tiles = [], []
    for t, (source, buf, w_source, w, _, _, _, _) in enumerate(towers_here):
        here = [
            pltpu.make_async_copy(w_source, w, w_sem.at[t]),
            pltpu.make_async_copy(source, buf, in_sem.at[t]),
        ]
        for copy in here:
            copy.start()
        waits.append(here)
        for start in range(0, buf.shape[0], JOB_ROWS):
            for column in range(0, width, JOB_COLUMNS):
                tiles.append((t, start, column))
    first = place_ref[0] * width

    def project(n):
        t, start, column = tiles[n]
        _, buf, _, w, _, _, _, _ = towers_here[t]
        if start == 0 and column == 0:
            for copy in waits[t]:
                copy.wait()
        rows, columns = slice(start, start + JOB_ROWS), slice(column, column + JOB_COLUMNS)
        target = (even, odd)[n % 2]
        target[...] = jnp.dot(buf[rows, :], w[:, columns], preferred_element_type=F32)

    out_copies = []
    project(0)
    for n, (t, start, tile_column) in enumerate(tiles):
        _, buf, _, _, slope, slope_out, tok, base = towers_here[t]
        if n + 1 < len(tiles):
            project(n + 1)
        for row in range(start, start + JOB_ROWS, STRIP):
            rows = slice(row, row + STRIP)
            here = (rows, slice(tile_column, tile_column + JOB_COLUMNS))
            token_columns = pl.ds(pl.multiple_of(first + tile_column, 128), JOB_COLUMNS)
            preact = (even, odd)[n % 2][row - start : row - start + STRIP, :]
            value, slant = gelu_and_slope(preact)
            slope[here] = slant
            hidden = buf[rows, token_columns].astype(F32) + value
            for part in range(0, STRIP, tok):
                sample = base + (row + part) // tok
                pooled_ref[sample : sample + 1, here[1]] = (
                    jnp.sum(hidden[part : part + tok], axis=0, keepdims=True) / tok
                )
        if tile_column + JOB_COLUMNS == width:
            part = pl.ds(start, JOB_ROWS)
            copy = pltpu.make_async_copy(
                slope.at[part, :], slope_out.at[part, :], out_sem.at[len(out_copies)]
            )
            copy.start()
            out_copies.append(copy)
    pooled = pooled_ref[...]
    total = jnp.sum(pooled * pooled, axis=1, keepdims=True)
    square_ref[...] = jnp.broadcast_to(total, square_ref.shape)
    for copy in out_copies:
        copy.wait()


def forward(place, image_flat, text_flat, image_w, text_w, samples):
    width = image_w.shape[1]
    depth = image_w.shape[0]
    rows_i, rows_t = image_flat.shape[0], text_flat.shape[0]
    jobs = (rows_i + rows_t) // JOB_ROWS
    return pl.pallas_call(
        functools.partial(forward_kernel, (rows_i // samples, rows_t // samples)),
        out_shape=(
            jax.ShapeDtypeStruct((2 * samples, width), F32),
            jax.ShapeDtypeStruct((2 * samples, 128), F32),
            jax.ShapeDtypeStruct((rows_i, width), F32),
            jax.ShapeDtypeStruct((rows_t, width), F32),
        ),
        in_specs=[smem()] + [hbm()] * 4,
        out_specs=(vmem(), vmem(), hbm(), hbm()),
        scratch_shapes=[
            pltpu.VMEM((rows_i, depth), BF16),
            pltpu.VMEM((rows_t, depth), BF16),
            pltpu.VMEM((depth, width), BF16),
            pltpu.VMEM((depth, width), BF16),
            pltpu.VMEM((rows_i, width), F32),
            pltpu.VMEM((rows_t, width), F32),
            pltpu.VMEM((JOB_ROWS, JOB_COLUMNS), F32),
            pltpu.VMEM((JOB_ROWS, JOB_COLUMNS), F32),
            pltpu.SemaphoreType.DMA((2,)),
            pltpu.SemaphoreType.DMA((2,)),
            pltpu.SemaphoreType.DMA((jobs,)),
        ],
        compiler_params=params(53),
        cost_estimate=pl.CostEstimate(
            flops=2 * (rows_i + rows_t) * depth * width,
            bytes_accessed=2 * (rows_i + rows_t) * (depth + 2 * width) + 4 * depth * width,
            transcendentals=(rows_i + rows_t) * width,
        ),
    )(place, image_flat, text_flat, image_w, text_w)


def unit_kernel(count_ref, pooled_ref, own_ref, other_ref, unit_ref, sent_ref, norm_ref):
    both = pooled_ref.shape[0]
    norm = jnp.sqrt(own_ref[...] + other_ref[...] + 1e-06)
    norm_ref[...] = norm
    unit = pooled_ref[...] / norm[:, :1]
    unit_ref[...] = unit
    row = lax.broadcasted_iota(jnp.int32, unit.shape, 0) % (both // 2)
    sent_ref[...] = jnp.where(row < count_ref[0], unit, UNUSABLE).astype(BF16)


def units(count, pooled, own, other):
    return pl.pallas_call(
        unit_kernel,
        out_shape=(
            jax.ShapeDtypeStruct(pooled.shape, F32),
            jax.ShapeDtypeStruct(pooled.shape, BF16),
            jax.ShapeDtypeStruct(own.shape, F32),
        ),
        in_specs=[smem()] + [pl.BlockSpec()] * 3,
        out_specs=(vmem(),) * 3,
        compiler_params=params(4),
    )(count, pooled, own, other)


def stack_kernel(afters, *refs):
    parts, out_ref = refs[afters:-1], refs[-1]
    for n, part in enumerate(parts):
        out_ref[n] = part[...]


def stack(parts, *afters):
    return pl.pallas_call(
        functools.partial(stack_kernel, len(afters)),
        out_shape=jax.ShapeDtypeStruct((len(parts), *parts[0].shape), parts[0].dtype),
        in_specs=[anyplace()] * len(afters) + [vmem()] * len(parts),
        out_specs=vmem(),
        compiler_params=params(4),
    )(*afters, *parts)


def turn_kernel(source_ref, tokens_ref, _, turned_ref, most_ref, turned):
    rows, _ = tokens_ref.shape
    blocks = source_ref.shape[0]
    height = turned_ref.shape[0] // blocks
    largest = None
    for start in range(0, rows, ROWS):
        tokens = tokens_ref[start : start + ROWS, :]
        turned[...] = tokens.T
        most = jnp.max(jnp.abs(tokens).astype(F32), axis=0, keepdims=True)
        largest = most if largest is None else jnp.maximum(largest, most)
        for q in range(blocks):
            source = pl.multiple_of(source_ref[q] * height, height)
            turned_ref[q * height : (q + 1) * height, start : start + ROWS] = turned[
                pl.ds(source, height), :
            ]
    most_ref[...] = jnp.broadcast_to(jnp.max(largest, axis=1, keepdims=True), most_ref.shape)


def turn(sources, flat, after):
    rows, depth = flat.shape
    blocks = sources.shape[0]
    odd = (depth // blocks) % 16
    picked = jnp.arange(16, dtype=jnp.int32) if odd else sources
    turned, most = pl.pallas_call(
        turn_kernel,
        out_shape=(
            jax.ShapeDtypeStruct((depth, rows), flat.dtype),
            jax.ShapeDtypeStruct((8, 128), F32),
        ),
        in_specs=[smem(), vmem(), anyplace()],
        out_specs=(vmem(), vmem()),
        scratch_shapes=[pltpu.VMEM((depth, ROWS), flat.dtype)],
        compiler_params=params(8),
        cost_estimate=pl.CostEstimate(
            flops=0, bytes_accessed=4 * rows * depth, transcendentals=0
        ),
    )(picked, flat, after)
    if odd:
        turned = turned.reshape(blocks, depth // blocks, rows)[sources].reshape(depth, rows)
    return turned, most


def row_products(left, right):
    return lax.dot_general(left, right, (((1,), (1,)), ((), ())), preferred_element_type=F32)


def towers(blocks_ref, samples):
    blocks, _, width = blocks_ref.shape
    image = blocks_ref[:, :samples, :].reshape(blocks * samples, width)
    text = blocks_ref[:, samples:, :].reshape(blocks * samples, width)
    return image, text


def product_kernel(image_most_ref, text_most_ref, *refs):
    *block_refs, out_ref, mark_ref = refs
    near_ref = block_refs[0]
    samples = near_ref.shape[1] // 2
    own_image = near_ref[0, :samples, :]
    own_text = near_ref[0, samples:, :]
    lane = lax.broadcasted_iota(jnp.int32, own_image.shape, 1)
    first = jnp.where(lane == 0, 1.0, 0.0).astype(BF16)
    start = 0
    for ref in block_refs:
        image, text = towers(ref, samples)
        stop = start + image.shape[0]
        found = row_products(jnp.concatenate([own_image, first], axis=0), text)
        out_ref[:samples, start:stop] = found[:samples]
        mark_ref[:, start:stop] = found[samples : samples + 8]
        out_ref[samples:, start:stop] = row_products(own_text, image)
        start = stop


def products(blocks, mosts):
    both = blocks[0].shape[1]
    columns = sum(b.shape[0] for b in blocks) * (both // 2)
    return pl.pallas_call(
        product_kernel,
        out_shape=(
            jax.ShapeDtypeStruct((both, columns), F32),
            jax.ShapeDtypeStruct((8, columns), F32),
        ),
        in_specs=[anyplace()] * 2 + [vmem()] * len(blocks),
        out_specs=(vmem(),) * 2,
        compiler_params=params(8),
    )(*mosts, *blocks)


def middle_kernel(
    tokens_of,
    scale_ref,
    bias_ref,
    gain_ref,
    count_ref,
    own_ref,
    other_ref,
    mark_ref,
    unit_ref,
    norm_ref,
    image_most_ref,
    text_most_ref,
    *refs,
):
    *block_refs, grad_ref, stat_ref = refs
    samples = unit_ref.shape[0] // 2
    scale, bias = scale_ref[0], bias_ref[0]
    dots = own_ref[...] + other_ref[...]
    logits = scale * dots + bias
    row = lax.broadcasted_iota(jnp.int32, dots.shape, 0) % samples
    column = lax.broadcasted_iota(jnp.int32, dots.shape, 1)
    sign = jnp.where(row == column, 1.0, -1.0).astype(F32)
    usable = jnp.where(mark_ref[:1, :] < 1.5, 1.0, 0.0)
    total = jnp.sum(usable, axis=1, keepdims=True)
    used = (usable > 0.5) & (row < count_ref[0])
    margin = -sign * logits
    small = jnp.exp(-jnp.abs(margin))
    soft = jnp.maximum(margin, 0.0) + jnp.log1p(small)
    sigmoid = jnp.where(margin >= 0, 1.0, small) / (1.0 + small)
    part = jnp.where(used, soft, 0.0)[:samples, :]
    loss = jnp.sum(jnp.sum(part, axis=1, keepdims=True), axis=0, keepdims=True) / total
    coeff = gain_ref[0] / total
    dlogit = (jnp.where(used, -sign * sigmoid, 0.0) * coeff).astype(BF16)
    radial = scale * jnp.sum(dlogit.astype(F32) * dots, axis=1, keepdims=True)
    raws = [jnp.zeros((samples, unit_ref.shape[1]), F32) for _ in range(2)]
    start = 0
    for ref in block_refs:
        image, text = towers(ref, samples)
        stop = start + image.shape[0]
        raws[0] += jnp.dot(dlogit[:samples, start:stop], text, preferred_element_type=F32)
        raws[1] += jnp.dot(dlogit[samples:, start:stop], image, preferred_element_type=F32)
        start = stop
    limits = []
    for n, most_ref in enumerate((image_most_ref, text_most_ref)):
        here = slice(n * samples, (n + 1) * samples)
        inward = unit_ref[here, :] * radial[here, :]
        grad = (scale * raws[n] - inward) / norm_ref[here, :1] / tokens_of[n]
        grad_ref[here, :] = grad
        steep = jnp.max(jnp.max(jnp.abs(grad), axis=1, keepdims=True), axis=0, keepdims=True)
        limits.append(1.2 * samples * tokens_of[n] * most_ref[:1, :1] * steep)
    line = lax.broadcasted_iota(jnp.int32, stat_ref.shape, 0)
    stat_ref[...] = jnp.where(line == 0, loss, jnp.where(line == 1, limits[0], limits[1]))


def middle(tokens_of, scale, bias, gain, count, own, other, mark, unit, norm, mosts, blocks):
    return pl.pallas_call(
        functools.partial(middle_kernel, tokens_of),
        out_shape=(
            jax.ShapeDtypeStruct(unit.shape, F32),
            jax.ShapeDtypeStruct((8, unit.shape[1]), F32),
        ),
        in_specs=[smem()] * 4 + [vmem()] * (7 + len(blocks)),
        out_specs=(vmem(), vmem()),
        compiler_params=params(12),
    )(scale, bias, gain, count, own, other, mark, unit, norm, *mosts, *blocks)


def weight_kernel(
    base, carries, grad_ref, slope_ref, turned_ref, stat_ref, _, soon_ref, late_ref, keep_ref, preact_grad
):
    rows, width = slope_ref.shape
    samples = grad_ref.shape[0] // 2
    tok = rows // samples
    for sample in range(samples):
        here = slice(sample * tok, (sample + 1) * tok)
        row = base * samples + sample
        for column in range(0, width, 128):
            columns = slice(column, column + 128)
            slope = slope_ref[here, columns]
            preact_grad[here, columns] = (grad_ref[row : row + 1, columns] * slope).astype(BF16)
    height = late_ref.shape[0]
    if carries:
        soon_ref[height:, :] = stat_ref[...]
    for n, (out, start) in enumerate(
        ((soon_ref, 0), (late_ref, 0), (keep_ref, 0), (keep_ref, height))
    ):
        out[start : start + height, :] = jnp.dot(
            turned_ref[n * height : (n + 1) * height, :],
            preact_grad[...],
            preferred_element_type=F32,
        )


def weight_terms(grad, slope, turned, stat, base, carries, after):
    depth, rows = turned.shape
    width = slope.shape[1]
    quarter = depth // 4
    soon = quarter + (stat.shape[0] if carries else 0)
    return pl.pallas_call(
        functools.partial(weight_kernel, base, carries),
        out_shape=tuple(jax.ShapeDtypeStruct((n, width), F32) for n in (soon, quarter, 2 * quarter)),
        in_specs=[vmem()] * 4 + [anyplace()],
        out_specs=(vmem(),) * 3,
        scratch_shapes=[pltpu.VMEM((rows, width), BF16)],
        compiler_params=params(8),
        cost_estimate=pl.CostEstimate(
            flops=2 * depth * rows * width,
            bytes_accessed=2 * depth * rows + 4 * rows * width + 4 * depth * width,
            transcendentals=0,
        ),
    )(grad, slope, turned, stat, after)


def sum_of(terms):
    total = None
    for term, unit in terms:
        value = term if unit is None else term.astype(F32) * unit
        total = value if total is None else total + value
    return total


def body(
    image_tokens,
    text_tokens,
    image_weight,
    text_weight,
    logit_scale,
    logit_bias,
    loss_scale,
    valid_count,
):
    samples, image_tok, depth = image_tokens.shape
    text_tok = text_tokens.shape[1]
    width = image_weight.shape[1]
    cycle = lax.axis_size("dp")
    bits = cycle.bit_length() - 1
    place = lax.axis_index("dp")

    def swap(array, mask):
        return lax.ppermute(array, "dp", [(i, i ^ mask) for i in range(cycle)])

    def swap_halves(array):
        return lax.ppermute(array, "mp", [(0, 1), (1, 0)])

    def bits_of(value, order):
        return sum(((value >> (len(order) - 1 - i)) & 1) << b for i, b in enumerate(order))

    image_flat = image_tokens.reshape(-1, depth)
    text_flat = text_tokens.reshape(-1, depth)
    text_orders = [list(range(2, bits)), list(range(3, bits)) + [2]]
    image_order = [2, 1] + list(range(3, bits))
    later = [(c, q) for c in range(2) for q in range(cycle // 4)]
    text_blocks = [
        2 * (high + bits_of(q, text_orders[c])) + c for high in (3, 1, 0, 2) for c, q in later
    ]
    image_blocks = [
        high + bits_of(q, image_order[1:])
        for high in (5, 1, 0, 4)
        for q in range(cycle // 4)
    ]
    text_blocks = jnp.asarray(text_blocks, jnp.int32) ^ (2 * place)
    image_blocks = jnp.asarray(image_blocks, jnp.int32) ^ place

    model_place = lax.axis_index("mp").astype(jnp.int32).reshape(1)
    pooled, square, image_slope, text_slope = forward(
        model_place, image_flat, text_flat, image_weight, text_weight, samples
    )
    unit, sent, norm = units(valid_count, pooled, square, swap_halves(square))

    low = max(bits - 2, 1)
    tops = [1 << b for b in reversed(range(low, bits))]
    masks = [tops[0] | tops[1], *tops] if len(tops) == 2 else tops
    arrived = [swap(sent, mask) for mask in masks]
    image_turned, image_most = turn(image_blocks, image_flat, sent)
    gathered = stack([sent] + arrived, image_most)
    text_turned, text_most = turn(text_blocks, text_flat, gathered)
    blocks = [gathered]
    for b in reversed(range(1, low)):
        blocks = blocks + [swap(block, 1 << b) for block in blocks]
    far = [swap(block, 1) for block in blocks[:1]]
    for block in blocks[1:]:
        far.append(swap(stack([block], text_most)[0], 1))
    blocks = blocks + far

    own_dots, mark = products(blocks, (image_most, text_most))
    grad, stat = middle(
        (image_tok, text_tok),
        logit_scale,
        logit_bias,
        loss_scale,
        valid_count,
        own_dots,
        swap_halves(own_dots),
        mark,
        unit,
        norm,
        (image_most, text_most),
        blocks,
    )

    lines = lax.broadcasted_iota(jnp.int32, (FOOT, width), 0)

    def footer(exponents, stat):
        rows = list(exponents)
        rest = stat[:1]
        for _ in range(3):
            part = lax.reduce_precision(rest, 5, 10)
            rows.append(part)
            rest = (rest - part) * 2048.0
        found = jnp.zeros((FOOT, width), F32)
        for n, row in enumerate(rows):
            found = jnp.where(lines == n, row, found)
        return found

    def exponents_of(stat):
        return [jnp.ceil(jnp.log2(jnp.maximum(stat[n : n + 1], 1e-30))) for n in (1, 2)]

    def merged(stat, message):
        foot = message[-FOOT:].astype(F32)
        loss = (foot[4:5] / 2048.0 + foot[3:4]) / 2048.0 + foot[2:3]
        there = [foot[:1], foot[1:2]]
        add = [loss, jnp.exp2(there[0]), jnp.exp2(there[1])]
        total = [stat[n : n + 1] + row for n, row in enumerate(add)]
        return jnp.concatenate(total), there

    def halves(terms):
        half = terms[0][0].shape[0] // 2
        return [[(term[rows], unit) for term, unit in terms] for rows in (slice(half), slice(half, None))]

    def leave(terms, stat, tower, bit, after):
        rows = terms[0][0].shape[0]
        exponents = exponents_of(stat)
        factor = HALF_MAX * jnp.exp2(-exponents[tower]) + 0.0 * after[:1].astype(F32)
        coded = sum_of(terms) * factor
        foot = footer(exponents, stat) + 0.0 * coded[:1]
        coded = jnp.pad(coded, ((0, FOOT), (0, 0))) + jnp.pad(foot, ((rows, 0), (0, 0)))
        coded = coded.astype(jnp.float16)
        return coded, swap(coded, 1 << bit)

    def take(terms, stat, tower, coming):
        stat, there = merged(stat, coming)
        return terms + [(coming[:-FOOT], jnp.exp2(there[tower]) / HALF_MAX)], stat

    def core_step(soon, late, keep):
        height = late.shape[0]
        there = swap(soon, 1)
        stays = [(keep[:height], None), (swap(late, 1), None)]
        return stays, [(keep[height:], None), (there[:height], None)], there[height:]

    text_terms = weight_terms(grad, text_slope, text_turned, stat, 1, True, stat)
    text, text_leaves, stat_there = core_step(*text_terms)
    start_stat = stat[:3] + stat_there[:3]
    image_terms = weight_terms(grad, image_slope, image_turned, stat, 0, False, text_terms[0])
    image, image_leaves, _ = core_step(*image_terms)

    text_coded, text_in = leave(text_leaves, start_stat, 1, 1, start_stat)
    coded, image_in = leave(image_leaves, start_stat, 0, image_order[0], text_coded)
    _, late, keep = image_terms
    late = late + 0.0 * text_coded[:1].astype(F32)
    image = [(keep[: late.shape[0]], None), (swap(late, 1), None)]
    _, late, keep = text_terms
    late = late + 0.0 * text_coded[:1].astype(F32)
    text = [(keep[: late.shape[0]], None), (swap(late, 1), None)]
    text, text_stat = take(text, start_stat, 1, text_in)
    parts = [(terms, text_stat) for terms in halves(text)]
    for step in range(bits - 2):
        arrivals, before = [], coded
        for order, (terms, terms_stat) in zip(text_orders, parts):
            terms, leaves = halves(terms)
            last, arrival = leave(leaves, terms_stat, 1, order[step], before)
            before = last if step == 0 else before
            arrivals.append((terms, terms_stat, arrival))
        if step == 0:
            image_in = image_in.astype(F32) + 0.0 * before[:1].astype(F32)
            image, image_stat = take(image, start_stat, 0, image_in)
        image, image_leaves = halves(image)
        coded, image_in = leave(image_leaves, image_stat, 0, image_order[step + 1], before)
        parts = [take(terms, old, 1, arrival) for terms, old, arrival in arrivals]
        image, image_stat = take(image, image_stat, 0, image_in)
    row = 0.0 * coded[:1].astype(F32)
    text = jnp.concatenate([sum_of(terms) + row for terms, _ in parts])
    loss = jnp.max(parts[0][1][:1] + row)
    return (loss, sum_of(image), text)


def solution(mesh):
    placed = (
        P("dp", None, None),
        P("dp", None, None),
        P(None, "mp"),
        P(None, "mp"),
        P(),
        P(),
        P(),
        P("dp"),
    )
    return jax.shard_map(
        body,
        mesh=mesh,
        in_specs=placed,
        out_specs=(P(), P("dp", "mp"), P("dp", "mp")),
        check_vma=False,
    )
```

```python
import functools

import jax
import jax.numpy as jnp
from jax import lax
from jax.experimental import pallas as pl
from jax.experimental.pallas import tpu as pltpu
from jax.sharding import PartitionSpec as P

F32 = jnp.float32
BF16 = jnp.bfloat16
ROWS = 256
JOB_ROWS = 256
JOB_COLUMNS = 256
STRIP = 64
ROOT = 0.7978845608028654
HALF_MAX = 16384.0
FOOT = 8
UNUSABLE = 2.0


def vmem():
    return pl.BlockSpec(memory_space=pltpu.VMEM)


def smem():
    return pl.BlockSpec(memory_space=pltpu.SMEM)


def anyplace():
    return pl.BlockSpec(memory_space=pl.ANY)


def hbm():
    return pl.BlockSpec(memory_space=pltpu.HBM)


def params(mib):
    return pltpu.CompilerParams(vmem_limit_bytes=mib * 2**20)


def gelu_and_slope(x):
    square = x * x
    cdf = 0.5 + 0.5 * jnp.tanh(x * (ROOT + (0.044715 * ROOT) * square))
    value = x * cdf
    rise = (value - value * cdf) * (2 * ROOT + (6 * 0.044715 * ROOT) * square)
    return value, cdf + rise


def forward_kernel(
    tokens_of,
    place_ref,
    image_hbm,
    text_hbm,
    image_w_hbm,
    text_w_hbm,
    pooled_ref,
    square_ref,
    image_slope_hbm,
    text_slope_hbm,
    image_v,
    text_v,
    image_w,
    text_w,
    image_slope,
    text_slope,
    even,
    odd,
    in_sem,
    w_sem,
    out_sem,
):
    width = image_w.shape[1]
    samples = pooled_ref.shape[0] // 2
    towers_here = (
        (text_hbm, text_v, text_w_hbm, text_w, text_slope, text_slope_hbm, tokens_of[1], samples),
        (image_hbm, image_v, image_w_hbm, image_w, image_slope, image_slope_hbm, tokens_of[0], 0),
    )
    waits, tiles = [], []
    for t, (source, buf, w_source, w, _, _, _, _) in enumerate(towers_here):
        here = [
            pltpu.make_async_copy(w_source, w, w_sem.at[t]),
            pltpu.make_async_copy(source, buf, in_sem.at[t]),
        ]
        for copy in here:
            copy.start()
        waits.append(here)
        for start in range(0, buf.shape[0], JOB_ROWS):
            for column in range(0, width, JOB_COLUMNS):
                tiles.append((t, start, column))
    first = place_ref[0] * width

    def project(n):
        t, start, column = tiles[n]
        _, buf, _, w, _, _, _, _ = towers_here[t]
        if start == 0 and column == 0:
            for copy in waits[t]:
                copy.wait()
        rows, columns = slice(start, start + JOB_ROWS), slice(column, column + JOB_COLUMNS)
        target = (even, odd)[n % 2]
        target[...] = jnp.dot(buf[rows, :], w[:, columns], preferred_element_type=F32)

    out_copies = []
    project(0)
    for n, (t, start, tile_column) in enumerate(tiles):
        _, buf, _, _, slope, slope_out, tok, base = towers_here[t]
        if n + 1 < len(tiles):
            project(n + 1)
        for row in range(start, start + JOB_ROWS, STRIP):
            rows = slice(row, row + STRIP)
            here = (rows, slice(tile_column, tile_column + JOB_COLUMNS))
            token_columns = pl.ds(pl.multiple_of(first + tile_column, 128), JOB_COLUMNS)
            preact = (even, odd)[n % 2][row - start : row - start + STRIP, :]
            value, slant = gelu_and_slope(preact)
            slope[here] = slant
            hidden = buf[rows, token_columns].astype(F32) + value
            for part in range(0, STRIP, tok):
                sample = base + (row + part) // tok
                pooled_ref[sample : sample + 1, here[1]] = (
                    jnp.sum(hidden[part : part + tok], axis=0, keepdims=True) / tok
                )
        if tile_column + JOB_COLUMNS == width:
            part = pl.ds(start, JOB_ROWS)
            copy = pltpu.make_async_copy(
                slope.at[part, :], slope_out.at[part, :], out_sem.at[len(out_copies)]
            )
            copy.start()
            out_copies.append(copy)
    pooled = pooled_ref[...]
    total = jnp.sum(pooled * pooled, axis=1, keepdims=True)
    square_ref[...] = jnp.broadcast_to(total, square_ref.shape)
    for copy in out_copies:
        copy.wait()


def forward(place, image_flat, text_flat, image_w, text_w, samples):
    width = image_w.shape[1]
    depth = image_w.shape[0]
    rows_i, rows_t = image_flat.shape[0], text_flat.shape[0]
    jobs = (rows_i + rows_t) // JOB_ROWS
    return pl.pallas_call(
        functools.partial(forward_kernel, (rows_i // samples, rows_t // samples)),
        out_shape=(
            jax.ShapeDtypeStruct((2 * samples, width), F32),
            jax.ShapeDtypeStruct((2 * samples, 128), F32),
            jax.ShapeDtypeStruct((rows_i, width), F32),
            jax.ShapeDtypeStruct((rows_t, width), F32),
        ),
        in_specs=[smem()] + [hbm()] * 4,
        out_specs=(vmem(), vmem(), hbm(), hbm()),
        scratch_shapes=[
            pltpu.VMEM((rows_i, depth), BF16),
            pltpu.VMEM((rows_t, depth), BF16),
            pltpu.VMEM((depth, width), BF16),
            pltpu.VMEM((depth, width), BF16),
            pltpu.VMEM((rows_i, width), F32),
            pltpu.VMEM((rows_t, width), F32),
            pltpu.VMEM((JOB_ROWS, JOB_COLUMNS), F32),
            pltpu.VMEM((JOB_ROWS, JOB_COLUMNS), F32),
            pltpu.SemaphoreType.DMA((2,)),
            pltpu.SemaphoreType.DMA((2,)),
            pltpu.SemaphoreType.DMA((jobs,)),
        ],
        compiler_params=params(53),
        cost_estimate=pl.CostEstimate(
            flops=2 * (rows_i + rows_t) * depth * width,
            bytes_accessed=2 * (rows_i + rows_t) * (depth + 2 * width) + 4 * depth * width,
            transcendentals=(rows_i + rows_t) * width,
        ),
    )(place, image_flat, text_flat, image_w, text_w)


def unit_kernel(count_ref, pooled_ref, own_ref, other_ref, unit_ref, sent_ref, norm_ref):
    both = pooled_ref.shape[0]
    norm = jnp.sqrt(own_ref[...] + other_ref[...] + 1e-06)
    norm_ref[...] = norm
    unit = pooled_ref[...] / norm[:, :1]
    unit_ref[...] = unit
    row = lax.broadcasted_iota(jnp.int32, unit.shape, 0) % (both // 2)
    sent_ref[...] = jnp.where(row < count_ref[0], unit, UNUSABLE).astype(BF16)


def units(count, pooled, own, other):
    return pl.pallas_call(
        unit_kernel,
        out_shape=(
            jax.ShapeDtypeStruct(pooled.shape, F32),
            jax.ShapeDtypeStruct(pooled.shape, BF16),
            jax.ShapeDtypeStruct(own.shape, F32),
        ),
        in_specs=[smem()] + [pl.BlockSpec()] * 3,
        out_specs=(vmem(),) * 3,
        compiler_params=params(4),
    )(count, pooled, own, other)


def stack_kernel(afters, *refs):
    parts, out_ref = refs[afters:-1], refs[-1]
    for n, part in enumerate(parts):
        out_ref[n] = part[...]


def stack(parts, *afters):
    return pl.pallas_call(
        functools.partial(stack_kernel, len(afters)),
        out_shape=jax.ShapeDtypeStruct((len(parts), *parts[0].shape), parts[0].dtype),
        in_specs=[anyplace()] * len(afters) + [vmem()] * len(parts),
        out_specs=vmem(),
        compiler_params=params(4),
    )(*afters, *parts)


def turn_kernel(source_ref, tokens_ref, _, turned_ref, most_ref, turned):
    rows, _ = tokens_ref.shape
    blocks = source_ref.shape[0]
    height = turned_ref.shape[0] // blocks
    largest = None
    for start in range(0, rows, ROWS):
        tokens = tokens_ref[start : start + ROWS, :]
        turned[...] = tokens.T
        most = jnp.max(jnp.abs(tokens).astype(F32), axis=0, keepdims=True)
        largest = most if largest is None else jnp.maximum(largest, most)
        for q in range(blocks):
            source = pl.multiple_of(source_ref[q] * height, height)
            turned_ref[q * height : (q + 1) * height, start : start + ROWS] = turned[
                pl.ds(source, height), :
            ]
    most_ref[...] = jnp.broadcast_to(jnp.max(largest, axis=1, keepdims=True), most_ref.shape)


def turn(sources, flat, after):
    rows, depth = flat.shape
    blocks = sources.shape[0]
    odd = (depth // blocks) % 16
    picked = jnp.arange(16, dtype=jnp.int32) if odd else sources
    turned, most = pl.pallas_call(
        turn_kernel,
        out_shape=(
            jax.ShapeDtypeStruct((depth, rows), flat.dtype),
            jax.ShapeDtypeStruct((8, 128), F32),
        ),
        in_specs=[smem(), vmem(), anyplace()],
        out_specs=(vmem(), vmem()),
        scratch_shapes=[pltpu.VMEM((depth, ROWS), flat.dtype)],
        compiler_params=params(8),
        cost_estimate=pl.CostEstimate(
            flops=0, bytes_accessed=4 * rows * depth, transcendentals=0
        ),
    )(picked, flat, after)
    if odd:
        turned = turned.reshape(blocks, depth // blocks, rows)[sources].reshape(depth, rows)
    return turned, most


def row_products(left, right):
    return lax.dot_general(left, right, (((1,), (1,)), ((), ())), preferred_element_type=F32)


def towers(blocks_ref, samples):
    blocks, _, width = blocks_ref.shape
    image = blocks_ref[:, :samples, :].reshape(blocks * samples, width)
    text = blocks_ref[:, samples:, :].reshape(blocks * samples, width)
    return image, text


def product_kernel(image_most_ref, text_most_ref, *refs):
    *block_refs, out_ref, mark_ref = refs
    near_ref = block_refs[0]
    samples = near_ref.shape[1] // 2
    own_image = near_ref[0, :samples, :]
    own_text = near_ref[0, samples:, :]
    lane = lax.broadcasted_iota(jnp.int32, own_image.shape, 1)
    first = jnp.where(lane == 0, 1.0, 0.0).astype(BF16)
    start = 0
    for ref in block_refs:
        image, text = towers(ref, samples)
        stop = start + image.shape[0]
        found = row_products(jnp.concatenate([own_image, first], axis=0), text)
        out_ref[:samples, start:stop] = found[:samples]
        mark_ref[:, start:stop] = found[samples : samples + 8]
        out_ref[samples:, start:stop] = row_products(own_text, image)
        start = stop


def products(blocks, mosts):
    both = blocks[0].shape[1]
    columns = sum(b.shape[0] for b in blocks) * (both // 2)
    return pl.pallas_call(
        product_kernel,
        out_shape=(
            jax.ShapeDtypeStruct((both, columns), F32),
            jax.ShapeDtypeStruct((8, columns), F32),
        ),
        in_specs=[anyplace()] * 2 + [vmem()] * len(blocks),
        out_specs=(vmem(),) * 2,
        compiler_params=params(8),
    )(*mosts, *blocks)


def middle_kernel(
    tokens_of,
    scale_ref,
    bias_ref,
    gain_ref,
    count_ref,
    own_ref,
    other_ref,
    mark_ref,
    unit_ref,
    norm_ref,
    image_most_ref,
    text_most_ref,
    *refs,
):
    *block_refs, grad_ref, stat_ref = refs
    samples = unit_ref.shape[0] // 2
    scale, bias = scale_ref[0], bias_ref[0]
    dots = own_ref[...] + other_ref[...]
    logits = scale * dots + bias
    row = lax.broadcasted_iota(jnp.int32, dots.shape, 0) % samples
    column = lax.broadcasted_iota(jnp.int32, dots.shape, 1)
    sign = jnp.where(row == column, 1.0, -1.0).astype(F32)
    usable = jnp.where(mark_ref[:1, :] < 1.5, 1.0, 0.0)
    total = jnp.sum(usable, axis=1, keepdims=True)
    used = (usable > 0.5) & (row < count_ref[0])
    margin = -sign * logits
    small = jnp.exp(-jnp.abs(margin))
    soft = jnp.maximum(margin, 0.0) + jnp.log1p(small)
    sigmoid = jnp.where(margin >= 0, 1.0, small) / (1.0 + small)
    part = jnp.where(used, soft, 0.0)[:samples, :]
    loss = jnp.sum(jnp.sum(part, axis=1, keepdims=True), axis=0, keepdims=True) / total
    coeff = gain_ref[0] / total
    dlogit = (jnp.where(used, -sign * sigmoid, 0.0) * coeff).astype(BF16)
    radial = scale * jnp.sum(dlogit.astype(F32) * dots, axis=1, keepdims=True)
    raws = [jnp.zeros((samples, unit_ref.shape[1]), F32) for _ in range(2)]
    start = 0
    for ref in block_refs:
        image, text = towers(ref, samples)
        stop = start + image.shape[0]
        raws[0] += jnp.dot(dlogit[:samples, start:stop], text, preferred_element_type=F32)
        raws[1] += jnp.dot(dlogit[samples:, start:stop], image, preferred_element_type=F32)
        start = stop
    limits = []
    for n, most_ref in enumerate((image_most_ref, text_most_ref)):
        here = slice(n * samples, (n + 1) * samples)
        inward = unit_ref[here, :] * radial[here, :]
        grad = (scale * raws[n] - inward) / norm_ref[here, :1] / tokens_of[n]
        grad_ref[here, :] = grad
        steep = jnp.max(jnp.max(jnp.abs(grad), axis=1, keepdims=True), axis=0, keepdims=True)
        limits.append(1.2 * samples * tokens_of[n] * most_ref[:1, :1] * steep)
    line = lax.broadcasted_iota(jnp.int32, stat_ref.shape, 0)
    stat_ref[...] = jnp.where(line == 0, loss, jnp.where(line == 1, limits[0], limits[1]))


def middle(tokens_of, scale, bias, gain, count, own, other, mark, unit, norm, mosts, blocks):
    return pl.pallas_call(
        functools.partial(middle_kernel, tokens_of),
        out_shape=(
            jax.ShapeDtypeStruct(unit.shape, F32),
            jax.ShapeDtypeStruct((8, unit.shape[1]), F32),
        ),
        in_specs=[smem()] * 4 + [vmem()] * (7 + len(blocks)),
        out_specs=(vmem(), vmem()),
        compiler_params=params(12),
    )(scale, bias, gain, count, own, other, mark, unit, norm, *mosts, *blocks)


def weight_kernel(
    base, carries, grad_ref, slope_ref, turned_ref, stat_ref, _, soon_ref, late_ref, keep_ref, preact_grad
):
    rows, width = slope_ref.shape
    samples = grad_ref.shape[0] // 2
    tok = rows // samples
    for sample in range(samples):
        here = slice(sample * tok, (sample + 1) * tok)
        row = base * samples + sample
        for column in range(0, width, 128):
            columns = slice(column, column + 128)
            slope = slope_ref[here, columns]
            preact_grad[here, columns] = (grad_ref[row : row + 1, columns] * slope).astype(BF16)
    height = late_ref.shape[0]
    if carries:
        soon_ref[height:, :] = stat_ref[...]
    for n, (out, start) in enumerate(
        ((soon_ref, 0), (late_ref, 0), (keep_ref, 0), (keep_ref, height))
    ):
        out[start : start + height, :] = jnp.dot(
            turned_ref[n * height : (n + 1) * height, :],
            preact_grad[...],
            preferred_element_type=F32,
        )


def weight_terms(grad, slope, turned, stat, base, carries, after):
    depth, rows = turned.shape
    width = slope.shape[1]
    quarter = depth // 4
    soon = quarter + (stat.shape[0] if carries else 0)
    return pl.pallas_call(
        functools.partial(weight_kernel, base, carries),
        out_shape=tuple(jax.ShapeDtypeStruct((n, width), F32) for n in (soon, quarter, 2 * quarter)),
        in_specs=[vmem()] * 4 + [anyplace()],
        out_specs=(vmem(),) * 3,
        scratch_shapes=[pltpu.VMEM((rows, width), BF16)],
        compiler_params=params(8),
        cost_estimate=pl.CostEstimate(
            flops=2 * depth * rows * width,
            bytes_accessed=2 * depth * rows + 4 * rows * width + 4 * depth * width,
            transcendentals=0,
        ),
    )(grad, slope, turned, stat, after)


def sum_of(terms):
    total = None
    for term, unit in terms:
        value = term if unit is None else term.astype(F32) * unit
        total = value if total is None else total + value
    return total


def body(
    image_tokens,
    text_tokens,
    image_weight,
    text_weight,
    logit_scale,
    logit_bias,
    loss_scale,
    valid_count,
):
    samples, image_tok, depth = image_tokens.shape
    text_tok = text_tokens.shape[1]
    width = image_weight.shape[1]
    cycle = lax.axis_size("dp")
    bits = cycle.bit_length() - 1
    place = lax.axis_index("dp")

    def swap(array, mask):
        return lax.ppermute(array, "dp", [(i, i ^ mask) for i in range(cycle)])

    def swap_halves(array):
        return lax.ppermute(array, "mp", [(0, 1), (1, 0)])

    def bits_of(value, order):
        return sum(((value >> (len(order) - 1 - i)) & 1) << b for i, b in enumerate(order))

    image_flat = image_tokens.reshape(-1, depth)
    text_flat = text_tokens.reshape(-1, depth)
    text_orders = [list(range(2, bits)), list(range(3, bits)) + [2]]
    image_order = [2, 1] + list(range(3, bits))
    later = [(c, q) for c in range(2) for q in range(cycle // 4)]
    text_blocks = [
        2 * (high + bits_of(q, text_orders[c])) + c for high in (3, 1, 0, 2) for c, q in later
    ]
    image_blocks = [
        high + bits_of(q, image_order[1:])
        for high in (5, 1, 0, 4)
        for q in range(cycle // 4)
    ]
    text_blocks = jnp.asarray(text_blocks, jnp.int32) ^ (2 * place)
    image_blocks = jnp.asarray(image_blocks, jnp.int32) ^ place

    model_place = lax.axis_index("mp").astype(jnp.int32).reshape(1)
    pooled, square, image_slope, text_slope = forward(
        model_place, image_flat, text_flat, image_weight, text_weight, samples
    )
    unit, sent, norm = units(valid_count, pooled, square, swap_halves(square))

    low = max(bits - 2, 1)
    tops = [1 << b for b in reversed(range(low, bits))]
    masks = [tops[0] | tops[1], *tops] if len(tops) == 2 else tops
    arrived = [swap(sent, mask) for mask in masks]
    image_turned, image_most = turn(image_blocks, image_flat, sent)
    gathered = stack([sent] + arrived, image_most)
    text_turned, text_most = turn(text_blocks, text_flat, gathered)
    blocks = [gathered]
    for b in reversed(range(1, low)):
        blocks = blocks + [swap(block, 1 << b) for block in blocks]
    far = [swap(block, 1) for block in blocks[:1]]
    for block in blocks[1:]:
        far.append(swap(stack([block], text_most)[0], 1))
    blocks = blocks + far

    own_dots, mark = products(blocks, (image_most, text_most))
    grad, stat = middle(
        (image_tok, text_tok),
        logit_scale,
        logit_bias,
        loss_scale,
        valid_count,
        own_dots,
        swap_halves(own_dots),
        mark,
        unit,
        norm,
        (image_most, text_most),
        blocks,
    )

    lines = lax.broadcasted_iota(jnp.int32, (FOOT, width), 0)

    def footer(exponents, stat):
        rows = list(exponents)
        rest = stat[:1]
        for _ in range(3):
            part = lax.reduce_precision(rest, 5, 10)
            rows.append(part)
            rest = (rest - part) * 2048.0
        found = jnp.zeros((FOOT, width), F32)
        for n, row in enumerate(rows):
            found = jnp.where(lines == n, row, found)
        return found

    def exponents_of(stat):
        return [jnp.ceil(jnp.log2(jnp.maximum(stat[n : n + 1], 1e-30))) for n in (1, 2)]

    def merged(stat, message):
        foot = message[-FOOT:].astype(F32)
        loss = (foot[4:5] / 2048.0 + foot[3:4]) / 2048.0 + foot[2:3]
        there = [foot[:1], foot[1:2]]
        add = [loss, jnp.exp2(there[0]), jnp.exp2(there[1])]
        total = [stat[n : n + 1] + row for n, row in enumerate(add)]
        return jnp.concatenate(total), there

    def halves(terms):
        half = terms[0][0].shape[0] // 2
        return [[(term[rows], unit) for term, unit in terms] for rows in (slice(half), slice(half, None))]

    def leave(terms, stat, tower, bit, after):
        rows = terms[0][0].shape[0]
        exponents = exponents_of(stat)
        factor = HALF_MAX * jnp.exp2(-exponents[tower]) + 0.0 * after[:1].astype(F32)
        coded = sum_of(terms) * factor
        foot = footer(exponents, stat) + 0.0 * coded[:1]
        coded = jnp.pad(coded, ((0, FOOT), (0, 0))) + jnp.pad(foot, ((rows, 0), (0, 0)))
        coded = coded.astype(jnp.float16)
        return coded, swap(coded, 1 << bit)

    def take(terms, stat, tower, coming):
        stat, there = merged(stat, coming)
        return terms + [(coming[:-FOOT], jnp.exp2(there[tower]) / HALF_MAX)], stat

    def core_step(soon, late, keep):
        height = late.shape[0]
        there = swap(soon, 1)
        stays = [(keep[:height], None), (swap(late, 1), None)]
        return stays, [(keep[height:], None), (there[:height], None)], there[height:]

    text_terms = weight_terms(grad, text_slope, text_turned, stat, 1, True, stat)
    text, text_leaves, stat_there = core_step(*text_terms)
    start_stat = stat[:3] + stat_there[:3]
    image_terms = weight_terms(grad, image_slope, image_turned, stat, 0, False, text_terms[0])
    image, image_leaves, _ = core_step(*image_terms)

    text_coded, text_in = leave(text_leaves, start_stat, 1, 1, start_stat)
    coded, image_in = leave(image_leaves, start_stat, 0, image_order[0], text_coded)
    _, late, keep = image_terms
    late = late + 0.0 * text_coded[:1].astype(F32)
    image = [(keep[: late.shape[0]], None), (swap(late, 1), None)]
    _, late, keep = text_terms
    late = late + 0.0 * text_coded[:1].astype(F32)
    text = [(keep[: late.shape[0]], None), (swap(late, 1), None)]
    text, text_stat = take(text, start_stat, 1, text_in)
    parts = [(terms, text_stat) for terms in halves(text)]
    for step in range(bits - 2):
        arrivals = [None, None]
        if step > 0:
            image, image_leaves = halves(image)
        if step < bits - 3:
            terms, leaves = halves(parts[0][0])
            made, arrival = leave(leaves, parts[0][1], 1, text_orders[0][step], coded)
            arrivals[0] = (terms, parts[0][1], arrival)
            terms, leaves = halves(parts[1][0])
            made, arrival = leave(leaves, parts[1][1], 1, text_orders[1][step], made)
            arrivals[1] = (terms, parts[1][1], arrival)
            if step == 0:
                image_in = image_in.astype(F32) + 0.0 * made[:1].astype(F32)
                image, image_stat = take(image, start_stat, 0, image_in)
                image, image_leaves = halves(image)
            coded, image_in = leave(image_leaves, image_stat, 0, image_order[step + 1], made)
        else:
            coded, image_in = leave(image_leaves, image_stat, 0, image_order[step + 1], coded)
            terms, leaves = halves(parts[0][0])
            made, arrival = leave(leaves, parts[0][1], 1, text_orders[0][step], coded)
            arrivals[0] = (terms, parts[0][1], arrival)
            terms, leaves = halves(parts[1][0])
            made, arrival = leave(leaves, parts[1][1], 1, text_orders[1][step], made)
            arrivals[1] = (terms, parts[1][1], arrival)
        parts = [take(terms, old, 1, arrival) for terms, old, arrival in arrivals]
        image, image_stat = take(image, image_stat, 0, image_in)
    row = 0.0 * coded[:1].astype(F32)
    text = jnp.concatenate([sum_of(terms) + row for terms, _ in parts])
    loss = jnp.max(parts[0][1][:1] + row)
    return (loss, sum_of(image), text)


def solution(mesh):
    placed = (
        P("dp", None, None),
        P("dp", None, None),
        P(None, "mp"),
        P(None, "mp"),
        P(),
        P(),
        P(),
        P("dp"),
    )
    return jax.shard_map(
        body,
        mesh=mesh,
        in_specs=placed,
        out_specs=(P(), P("dp", "mp"), P("dp", "mp")),
        check_vma=False,
    )
```
